32 devices in a mesh: dp: 4 (over x, core), tensor: 8 (over z, y).
Axes of the slice: x: 2, y: 2, z: 4, core: 2. Of those that a mesh axis runs over, the one named last changes fastest.
Arguments:
- hidden_in: bfloat16 [4096, 4096], P(('dp', 'tensor')), parts along dimension 0, may hold values from -6 to 6
- norm_gain: bfloat16 [4096], replicated, may hold values from 0.099609375 to 1.8984375
- w_query: bfloat16 [4096, 4096], P(None, 'tensor'), may hold values from -0.09375 to 0.09375
- keyvalue_weight: bfloat16 [4096, 2048], P(None, 'tensor'), may hold values from -0.09375 to 0.09375
- w_out: bfloat16 [4096, 4096], P('tensor'), may hold values from -0.09375 to 0.09375
- prefix_keyvalue_cache: bfloat16 [4096, 2048], P(None, 'tensor'), may hold values from -600 to 600, as said below
- seg_ids: int32 [4096], P('dp'), parts along dimension 0, may hold values from 0 to 63, never falling along the last dimension, each value on 1 to 64 neighbouring positions
- seg_doc: int32 [256], P('dp'), parts along dimension 0, may hold values from 0 to 15
- doc_lens: int32 [16], replicated, may hold values from 1 to 1024, 4096 in all
Outputs:
- mixed: bfloat16 [4096, 4096], P(('dp', 'tensor')), parts along dimension 0
The draws below stay inside these ranges and needn't reach their ends.
There are 4 independent parts, one for each index of `dp`. The reference program is written for one: setup_inputs(seed, part) draws one part's arguments, and reference() takes and returns one part's arrays. A program takes and returns all parts, laid end to end along the dimension named above; an argument that names none is the same for every part. Nothing has to cross between parts.
Inputs may be any that keep to these rules, and one draw needn't show every extreme that they name: `seg_ids`: segment numbers never fall along the tokens; each of the 64 samples holds 1 to 64 tokens, one exactly 64. `doc_lens`: the documents fill the prefix end to end in order, lengths summing to 4096, the longest exactly 1024. `prefix_keyvalue_cache`: cached keys already carry the rotary map of their prefix positions.
All inputs are finite; a program needn't handle non-finite values.
Results may differ from the reference program's by a relative error of at most 0.028.
The reference program's roundings to bfloat16 on the way count: a program that leaves them out, or rounds other values in their place, can miss the bound.
Values may be sent and summed in bfloat16 or wider, within the bound.
No kernel may reach another device: no remote copies, remote signals or barrier semaphores. Data moves between devices by JAX's collectives and lax.ppermute only.
A program may use at most 192 MiB of HBM per device.

```python
import math
import jax
import jax.numpy as jnp
import numpy as np
from jax import lax

MODEL_WIDTH = 4096
QUERY_HEADS = 32
KEYVALUE_HEADS = 8
HEAD_SIZE = 128
PREFIX_SPAN = 4096
NDOCS = 16
SEG_MOST = 64
BATCH_TOKENS = 1024
SEGS = 64
DOC_MOST = 1024
N_TENSOR = 8


def draw_prefix_keyvalue_cache(key, part):
    column_span = KEYVALUE_HEADS * 2 * HEAD_SIZE
    base = jnp.clip(jax.random.normal(key, (PREFIX_SPAN, column_span), jnp.float32), -6.0, 6.0)
    return base.astype(jnp.bfloat16)


def with_ends(drawn, own_key, low, largest):
    place = [jax.random.randint(jax.random.fold_in(own_key, axis), (), 0, length) for axis, length in enumerate(drawn.shape)]
    widest = drawn.shape.index(max(drawn.shape))
    beside = place[:widest] + [(place[widest] + 1) % drawn.shape[widest]] + place[widest + 1:]
    return drawn.at[tuple(place)].set(low).at[tuple(beside)].set(largest)


def block_scale(stream_key, shape, pieces, smallest, top_value):
    factor_of, own = 1.0, jax.random.fold_in(stream_key, 6)
    for axis_at, blocks in pieces:
        draws = jnp.exp(jax.random.uniform(jax.random.fold_in(own, axis_at), (blocks,), jnp.float32, smallest / len(pieces), top_value / len(pieces)))
        factor_of = factor_of * jnp.repeat(draws, shape[axis_at] // blocks).reshape([-1 if axis == axis_at else 1 for axis in range(len(shape))])
    return factor_of


def split_up(number_of, total, reach, slope):
    portions = [(1 << 20) // math.isqrt(grade ** slope) + 1 for grade in range(2, number_of + 1)]
    surplus, given = total - reach - (number_of - 1), [1] * (number_of - 1)
    while surplus > 0:
        candidates = [i for i in range(number_of - 1) if given[i] < reach]
        pool, left = sum([portions[i] for i in candidates]), surplus
        for i in candidates:
            more = min(reach - given[i], max(1, left * portions[i] // pool), surplus)
            given[i] = given[i] + more
            surplus = surplus - more
    return np.array([reach] + given)


def uneven_parts(key, amount, total, limit, lean):
    if amount == 2:
        one = jax.random.randint(key, (), max(1, total - limit), min(limit, total - 1) + 1)
        return jnp.stack([one, total - one])
    sizes = jnp.asarray(split_up(amount, total, limit, lean), jnp.int32)
    twos = (amount - 1) // 2
    giver, sink = sizes[1:1 + 2 * twos:2], sizes[2:2 + 2 * twos:2]
    slack = jnp.minimum(giver - 1, limit - sink)
    passed = jax.random.randint(jax.random.fold_in(key, 1), (twos,), 0, 1 << 20) % (slack + 1)
    sizes = sizes.at[1:1 + 2 * twos:2].set(giver - passed).at[2:2 + 2 * twos:2].set(sink + passed)
    return sizes[jax.random.permutation(jax.random.fold_in(key, 2), amount)]


def normal_values(key, dims, spread, limit, shards=(), kind=jnp.bfloat16):
    level = block_scale(key, dims, shards, -0.22, 0.18) if shards else 1.0
    result = jax.random.normal(key, dims, jnp.float32) * spread * level
    return jnp.minimum(jnp.maximum(result, -limit), limit).astype(kind)


def setup_inputs(seed: int = 0, part: int = 0) -> dict:
    seeds = jax.random.split(jax.random.key(seed), 10)
    part_splits = jax.random.split(jax.random.fold_in(seeds[9], part), 10)
    hidden_in = normal_values(part_splits[0], (BATCH_TOKENS, MODEL_WIDTH), 1.0, 6.0, ((0, 8),))
    norm_gain = jnp.clip(1.0 + 0.18 * jax.random.normal(seeds[1], (MODEL_WIDTH,), jnp.float32), 0.099609375, 1.8984375).astype(jnp.bfloat16)
    w_query = normal_values(seeds[2], (MODEL_WIDTH, QUERY_HEADS * HEAD_SIZE), MODEL_WIDTH ** -0.5, 0.09375, ((1, 8),))
    keyvalue_weight = normal_values(seeds[3], (MODEL_WIDTH, KEYVALUE_HEADS * 2 * HEAD_SIZE), MODEL_WIDTH ** -0.5, 0.09375, ((1, 8),))
    w_out = normal_values(seeds[4], (QUERY_HEADS * HEAD_SIZE, MODEL_WIDTH), (QUERY_HEADS * HEAD_SIZE) ** -0.5, 0.09375, ((0, 8),))
    prefix_keyvalue_cache = draw_prefix_keyvalue_cache(jax.random.fold_in(seeds[9], 71), part)
    seg_ids = jnp.searchsorted(jnp.cumsum(uneven_parts(part_splits[6], SEGS, BATCH_TOKENS, SEG_MOST, 1)), jnp.arange(BATCH_TOKENS), side="right").astype(jnp.int32)
    seg_doc = with_ends(jax.random.randint(part_splits[7], (SEGS,), 0, NDOCS), jax.random.fold_in(part_splits[7], 1), 0, NDOCS - 1).astype(jnp.int32)
    doc_lens = uneven_parts(seeds[8], NDOCS, PREFIX_SPAN, DOC_MOST, 1).astype(jnp.int32)
    return {"hidden_in": hidden_in, "norm_gain": norm_gain, "w_query": w_query, "keyvalue_weight": keyvalue_weight, "w_out": w_out, "prefix_keyvalue_cache": prefix_keyvalue_cache, "seg_ids": seg_ids, "seg_doc": seg_doc, "doc_lens": doc_lens}


eps = 1e-05
rope_theta = 500000.0

def normalize(rows_in, gain):
    values = rows_in.astype(jnp.float32)
    mean_square = lax.optimization_barrier(jnp.mean(values * values, axis=-1, keepdims=True))
    return (values * lax.rsqrt(mean_square + eps) * gain.astype(jnp.float32)).astype(jnp.bfloat16)

def rotary_tables(positions, head_dim):
    half_dim = head_dim // 2
    inverse = rope_theta ** (-(jnp.arange(half_dim, dtype=jnp.float32) * 2.0 / head_dim))
    angles = positions.astype(jnp.float32)[:, None] * inverse[None, :]
    return (jnp.cos(angles), jnp.sin(angles))

def apply_rotation(vectors, cosine_table, sine_table):
    half_dim = vectors.shape[-1] // 2
    lower_half = vectors[..., :half_dim]
    upper_half = vectors[..., half_dim:]
    cos_part = cosine_table[:, None, :]
    sin_part = sine_table[:, None, :]
    return jnp.concatenate([lower_half * cos_part - upper_half * sin_part, upper_half * cos_part + lower_half * sin_part], axis=-1)

def token_tables(seg_ids, seg_doc, doc_lens, prefix_len):
    token_count = seg_ids.shape[0]
    token_order = jnp.arange(token_count, dtype=jnp.int32)
    seg_start = lax.optimization_barrier(jnp.sum((seg_ids[None, :] < seg_ids[:, None]).astype(jnp.int32), axis=1, dtype=jnp.int32))
    positions = prefix_len + token_order - seg_start
    segments = jnp.arange(seg_doc.shape[0], dtype=jnp.int32)
    tok_doc = lax.optimization_barrier(jnp.sum(jnp.where(seg_ids[:, None] == segments[None, :], seg_doc[None, :], 0), axis=1, dtype=jnp.int32))
    doc_ends = jnp.cumsum(doc_lens, dtype=jnp.int32)
    prefix_order = jnp.arange(prefix_len, dtype=jnp.int32)
    key_doc = lax.optimization_barrier(jnp.sum((doc_ends[None, :] <= prefix_order[:, None]).astype(jnp.int32), axis=1, dtype=jnp.int32))
    return (positions, tok_doc, key_doc)

def attend_block(query_matrix, all_keys, all_values, allowed, score_scale):
    scores = jnp.einsum('bmgd,kmd->bmgk', query_matrix.astype(jnp.float32), all_keys.astype(jnp.float32)) * score_scale
    scores = jnp.where(allowed[:, None, None, :], scores, -1e+30)
    row_max = lax.optimization_barrier(jnp.max(scores, axis=-1, keepdims=True))
    weights = jnp.exp(scores - row_max)
    row_total = lax.optimization_barrier(jnp.sum(weights, axis=-1, keepdims=True))
    weights_bf = (weights / row_total).astype(jnp.bfloat16)
    return jnp.einsum('bmgk,kmd->bmgd', weights_bf.astype(jnp.float32), all_values.astype(jnp.float32)).astype(jnp.bfloat16)

def reference(hidden_in, norm_gain, w_query, keyvalue_weight, w_out, prefix_keyvalue_cache, seg_ids, seg_doc, doc_lens):
    normalized_input = normalize(hidden_in, norm_gain)
    positions, tok_doc, key_doc = token_tables(seg_ids, seg_doc, doc_lens, PREFIX_SPAN)
    cosine_table, sine_table = rotary_tables(positions, HEAD_SIZE)
    group_width = QUERY_HEADS // KEYVALUE_HEADS
    query_projected = jnp.dot(normalized_input, w_query, preferred_element_type=jnp.float32).reshape(BATCH_TOKENS, QUERY_HEADS, HEAD_SIZE)
    query_matrix = apply_rotation(query_projected, cosine_table, sine_table).astype(jnp.bfloat16).reshape(BATCH_TOKENS, KEYVALUE_HEADS, group_width, HEAD_SIZE)
    keyvalue_projected = jnp.dot(normalized_input, keyvalue_weight, preferred_element_type=jnp.float32).reshape(BATCH_TOKENS, KEYVALUE_HEADS, 2, HEAD_SIZE)
    keys_new = apply_rotation(keyvalue_projected[:, :, 0], cosine_table, sine_table).astype(jnp.bfloat16)
    values_new = keyvalue_projected[:, :, 1].astype(jnp.bfloat16)
    cache_divided = prefix_keyvalue_cache.reshape(PREFIX_SPAN, KEYVALUE_HEADS, 2, HEAD_SIZE)
    all_keys = jnp.concatenate([cache_divided[:, :, 0], keys_new], axis=0)
    all_values = jnp.concatenate([cache_divided[:, :, 1], values_new], axis=0)
    block_rows = min(64, BATCH_TOKENS)
    score_scale = 1.0 / math.sqrt(HEAD_SIZE)
    token_order = jnp.arange(BATCH_TOKENS, dtype=jnp.int32)

    def one_block(block_index):
        first_row = block_index * block_rows
        query_rows = lax.dynamic_slice_in_dim(query_matrix, first_row, block_rows, 0)
        row_docs = lax.dynamic_slice_in_dim(tok_doc, first_row, block_rows, 0)
        row_segs = lax.dynamic_slice_in_dim(seg_ids, first_row, block_rows, 0)
        places = first_row + jnp.arange(block_rows, dtype=jnp.int32)
        prefix_ok = key_doc[None, :] == row_docs[:, None]
        own_ok = (seg_ids[None, :] == row_segs[:, None]) & (token_order[None, :] <= places[:, None])
        allowed = jnp.concatenate([prefix_ok, own_ok], axis=1)
        return attend_block(query_rows, all_keys, all_values, allowed, score_scale)
    attended = lax.map(one_block, jnp.arange(BATCH_TOKENS // block_rows, dtype=jnp.int32)).reshape(BATCH_TOKENS, QUERY_HEADS * HEAD_SIZE)
    per_group = QUERY_HEADS * HEAD_SIZE // N_TENSOR

    def add_group(running, group_index):
        first_col = group_index * per_group
        term = jnp.dot(lax.dynamic_slice_in_dim(attended, first_col, per_group, 1), lax.dynamic_slice_in_dim(w_out, first_col, per_group, 0), preferred_element_type=jnp.float32)
        rounded = lax.optimization_barrier(term.astype(jnp.bfloat16))
        return (running + rounded.astype(jnp.float32), None)
    summed, unused = lax.scan(add_group, jnp.zeros((BATCH_TOKENS, MODEL_WIDTH), jnp.float32), jnp.arange(N_TENSOR, dtype=jnp.int32))
    return (hidden_in.astype(jnp.float32) + summed).astype(jnp.bfloat16)
```

```python
import functools
import math

import jax
import jax.numpy as jnp
import numpy as np
from jax import lax
from jax.experimental import pallas as pl
from jax.experimental.pallas import tpu as pltpu
from jax.sharding import PartitionSpec as P

HEAD = 128
TILE = 64
KEY_BLOCK = 256
MASKED = -1e30
EPS = 1e-05
ROPE_THETA = 500000.0
VMEM_LIMIT = 48 * 1024 * 1024


def ring_order(size):
    zs = 4 if size % 8 == 0 else 1
    ys = size // zs
    if zs == 1:
        return list(range(size))
    cycle = [(0, 0)]
    for y in range(ys):
        column = range(1, zs) if y % 2 == 0 else range(zs - 1, 0, -1)
        cycle += [(z, y) for z in column]
    cycle += [(0, y) for y in range(ys - 1, 0, -1)]
    return [z * ys + y for z, y in cycle]


def ready_tiles(order):
    size = len(order)
    place = {rank: i for i, rank in enumerate(order)}

    def distance(a, b):
        apart = (place[a] - place[b]) % size
        return min(apart, size - apart)

    steps = size // 2 + 1
    found = [[[] for _ in range(steps + 1)] for _ in range(size)]
    for rank in range(size):
        last = order[(place[rank] + size // 2) % size]
        for chunk in range(size):
            own = distance(rank, chunk)
            before = distance(rank, chunk - 1) if chunk else 0
            late = steps if max(own, before) == size // 2 and chunk != last else None
            first = max(own, before)
            found[rank][first if late is None else late].append(2 * chunk)
            found[rank][own].append(2 * chunk + 1)
    return found


def step_kernel(pieces, rows, heads, *refs):
    total = pieces * rows
    width = heads * HEAD
    it = iter(refs)
    ids, lists = next(it), next(it)
    xs = [next(it) for _ in range(pieces)]
    gain, wq, wkv, cos_tab, sin_tab, key_wide, cache, doc_bias, own_bias = [next(it) for _ in range(9)]
    first = pieces == 1 and rows == 128
    if not first:
        next(it), next(it), next(it)
    qb, kvb, att = next(it), next(it), next(it)
    (x_s, xn_s, wq_s, wkv_s, cos_s, sin_s, qo_s, kvo_s, key_s, val_s, qt_s, kvt_s, db_s, ob_s, sc_s, at_s,
     wide_s, own_s, m_s, l_s, o_s, sem_in, sem_tab, sem_w, sem_k, sem_out, sem_tile, sem_att) = list(it)
    prefix = key_wide.shape[0]
    blocks = prefix // KEY_BLOCK

    key_copy = pltpu.make_async_copy(key_wide, key_s, sem_k.at[0])
    val_copy = pltpu.make_async_copy(cache.at[:, pl.ds(HEAD, HEAD)], val_s, sem_k.at[1])
    if pieces:
        x_copies, tab_copies = [], []
        for i in range(pieces):
            span = pl.ds(i * rows, rows)
            place = pl.ds(pl.multiple_of(ids[i] * TILE, TILE), rows)
            x_copies.append(pltpu.make_async_copy(xs[i], x_s.at[span], sem_in.at[i]))
            tab_copies.append(pltpu.make_async_copy(cos_tab.at[place], cos_s.at[span], sem_tab.at[2 * i]))
            tab_copies.append(pltpu.make_async_copy(sin_tab.at[place], sin_s.at[span], sem_tab.at[2 * i + 1]))
        for copy in x_copies:
            copy.start()
        w_copies = [
            pltpu.make_async_copy(wq.at[:, pl.ds(c, 256)], wq_s.at[:, pl.ds(c, 256)], sem_w.at[j])
            for j, c in enumerate(range(0, width, 256))
        ]
        w_copies.append(pltpu.make_async_copy(wkv, wkv_s, sem_w.at[len(w_copies)]))
        for copy in w_copies:
            copy.start()
        for copy in tab_copies:
            copy.start()
    key_copy.start()
    val_copy.start()

    if pieces:
        gains = gain[...]
        for i in range(pieces):
            x_copies[i].wait()

        def norm_rows(r, carry):
            span = pl.ds(pl.multiple_of(r * 16, 16), 16)
            values = x_s[span, :].astype(jnp.float32)
            mean_square = jnp.mean(values * values, axis=-1, keepdims=True)
            xn_s[span, :] = (values * lax.rsqrt(mean_square + EPS) * gains).astype(jnp.bfloat16)
            return carry

        lax.fori_loop(0, total // 16, norm_rows, 0)
        for copy in tab_copies:
            copy.wait()
        cosine, sine = cos_s[...], sin_s[...]

        def rotate(v):
            return (v * cosine + pltpu.roll(v, HEAD // 2, 1) * sine).astype(jnp.bfloat16)

        for j, c in enumerate(range(0, width, 256)):
            w_copies[j].wait()
            made = jnp.dot(xn_s[...], wq_s[:, c:c + 256], preferred_element_type=jnp.float32)
            for h in range(2):
                qo_s[c // HEAD + h] = rotate(made[:, h * HEAD:(h + 1) * HEAD])
        w_copies[-1].wait()
        made = jnp.dot(xn_s[...], wkv_s[...], preferred_element_type=jnp.float32)
        kvo_s[:, :HEAD] = rotate(made[:, :HEAD])
        kvo_s[:, HEAD:] = made[:, HEAD:].astype(jnp.bfloat16)
        outs = []
        for i in range(pieces):
            span = pl.ds(i * rows, rows)
            place = pl.ds(pl.multiple_of(ids[i] * TILE, TILE), rows)
            outs.append(pltpu.make_async_copy(qo_s.at[:, span], qb.at[:, place], sem_out.at[2 * i]))
            outs.append(pltpu.make_async_copy(kvo_s.at[span], kvb.at[place], sem_out.at[2 * i + 1]))
        for copy in outs:
            copy.start()
        for copy in outs:
            copy.wait()

    count = ids[2]
    factor = math.log2(math.e) / math.sqrt(HEAD)

    def fetches(i, slot):
        tile = ids[3 + i]
        at = pl.multiple_of(tile * TILE, TILE)
        before = pl.multiple_of(jnp.maximum(tile - 1, 0) * TILE, TILE)
        return [
            pltpu.make_async_copy(qb.at[:, pl.ds(at, TILE)], qt_s.at[slot], sem_tile.at[slot, 0]),
            pltpu.make_async_copy(kvb.at[pl.ds(before, 2 * TILE)], kvt_s.at[slot], sem_tile.at[slot, 1]),
            pltpu.make_async_copy(doc_bias.at[pl.ds(at, TILE)], db_s.at[slot], sem_tile.at[slot, 2]),
            pltpu.make_async_copy(own_bias.at[pl.ds(at, TILE)], ob_s.at[slot], sem_tile.at[slot, 3]),
        ]

    def att_copy(i):
        at = pl.multiple_of(ids[3 + i] * TILE, TILE)
        return pltpu.make_async_copy(at_s, att.at[pl.ds(at, TILE)], sem_att)

    @pl.when(count > 0)
    def _():
        for copy in fetches(0, 0):
            copy.start()

    key_copy.wait()
    val_copy.wait()
    contract_last = (((1,), (1,)), ((), ()))

    def one_tile(i, carry):
        slot = lax.rem(i, 2)

        @pl.when(i + 1 < count)
        def _():
            for copy in fetches(i + 1, 1 - slot):
                copy.start()

        for copy in fetches(i, slot):
            copy.wait()
        tile = ids[3 + i]
        needed = lists[tile * (blocks + 1)]
        for h in range(heads):
            wide_s[h * TILE:(h + 1) * TILE, :HEAD] = qt_s[slot, h]
            wide_s[h * TILE:(h + 1) * TILE, HEAD:] = db_s[slot]
        own = lax.dot_general(
            wide_s[:, :HEAD], kvt_s[slot, :, :HEAD], contract_last, preferred_element_type=jnp.float32
        )
        own = (own.reshape(heads, TILE, HEAD) + ob_s[slot][None]).reshape(heads * TILE, HEAD)
        own_s[...] = own
        m_s[...] = own

        def score_block(j, c):
            block = lists[tile * (blocks + 1) + 1 + j]
            keys = key_s[pl.ds(pl.multiple_of(block * KEY_BLOCK, KEY_BLOCK), KEY_BLOCK), :]
            scores = lax.dot_general(wide_s[...], keys, contract_last, preferred_element_type=jnp.float32)
            sc_s[j] = scores
            m_s[...] = jnp.maximum(m_s[...], jnp.maximum(scores[:, :HEAD], scores[:, HEAD:]))
            return c

        lax.fori_loop(0, needed, score_block, 0)
        top = jnp.max(m_s[...], axis=1, keepdims=True)
        weights = jnp.exp2((own_s[...] - top) * factor)
        l_s[...] = weights
        o_s[...] = jnp.dot(weights.astype(jnp.bfloat16), kvt_s[slot, :, HEAD:], preferred_element_type=jnp.float32)

        def value_block(j, c):
            block = lists[tile * (blocks + 1) + 1 + j]
            values = val_s[pl.ds(pl.multiple_of(block * KEY_BLOCK, KEY_BLOCK), KEY_BLOCK), :]
            weights = jnp.exp2((sc_s[j] - top) * factor)
            l_s[...] += weights[:, :HEAD] + weights[:, HEAD:]
            o_s[...] += jnp.dot(weights.astype(jnp.bfloat16), values, preferred_element_type=jnp.float32)
            return c

        lax.fori_loop(0, needed, value_block, 0)
        result = (o_s[...] / jnp.sum(l_s[...], axis=1, keepdims=True)).astype(jnp.bfloat16)

        @pl.when(i > 0)
        def _():
            att_copy(i - 1).wait()

        for h in range(heads):
            at_s[:, h * HEAD:(h + 1) * HEAD] = result[h * TILE:(h + 1) * TILE]
        att_copy(i).start()
        return carry

    lax.fori_loop(0, count, one_tile, 0)

    @pl.when(count > 0)
    def _():
        att_copy(count - 1).wait()


def run_step(ids, lists, xs, fixed, state, dims):
    tokens, heads, prefix, depth = dims
    pieces = len(xs)
    rows = xs[0].shape[0] if pieces else TILE
    total = max(pieces * rows, 16)
    width = heads * HEAD
    any_spec = pl.BlockSpec(memory_space=pl.ANY)
    vmem_spec = pl.BlockSpec(memory_space=pltpu.VMEM)
    operands = list(xs) + list(fixed)
    specs = [any_spec] * pieces + [vmem_spec] + [any_spec] * (len(fixed) - 1)
    aliases = {}
    if state is not None:
        aliases = {2 + len(operands) + i: i for i in range(3)}
        operands += list(state)
        specs += [any_spec] * 3
    out_shape = [
        jax.ShapeDtypeStruct((heads, tokens, HEAD), jnp.bfloat16),
        jax.ShapeDtypeStruct((tokens, 2 * HEAD), jnp.bfloat16),
        jax.ShapeDtypeStruct((tokens, width), jnp.bfloat16),
    ]
    small = 16
    w_rows = depth if pieces else small
    scratch = [
        pltpu.VMEM((total, depth), jnp.bfloat16),
        pltpu.VMEM((total, depth), jnp.bfloat16),
        pltpu.VMEM((w_rows, width), jnp.bfloat16),
        pltpu.VMEM((w_rows, 2 * HEAD), jnp.bfloat16),
        pltpu.VMEM((total, HEAD), jnp.float32),
        pltpu.VMEM((total, HEAD), jnp.float32),
        pltpu.VMEM((heads, total, HEAD), jnp.bfloat16),
        pltpu.VMEM((total, 2 * HEAD), jnp.bfloat16),
        pltpu.VMEM((prefix, 2 * HEAD), jnp.bfloat16),
        pltpu.VMEM((prefix, HEAD), jnp.bfloat16),
        pltpu.VMEM((2, heads, TILE, HEAD), jnp.bfloat16),
        pltpu.VMEM((2, 2 * TILE, 2 * HEAD), jnp.bfloat16),
        pltpu.VMEM((2, TILE, HEAD), jnp.bfloat16),
        pltpu.VMEM((2, TILE, HEAD), jnp.float32),
        pltpu.VMEM((prefix // KEY_BLOCK, heads * TILE, KEY_BLOCK), jnp.float32),
        pltpu.VMEM((TILE, width), jnp.bfloat16),
        pltpu.VMEM((heads * TILE, 2 * HEAD), jnp.bfloat16),
        pltpu.VMEM((heads * TILE, HEAD), jnp.float32),
        pltpu.VMEM((heads * TILE, HEAD), jnp.float32),
        pltpu.VMEM((heads * TILE, HEAD), jnp.float32),
        pltpu.VMEM((heads * TILE, HEAD), jnp.float32),
        pltpu.SemaphoreType.DMA((max(pieces, 1),)),
        pltpu.SemaphoreType.DMA((2 * max(pieces, 1),)),
        pltpu.SemaphoreType.DMA((width // 256 + 1,)),
        pltpu.SemaphoreType.DMA((2,)),
        pltpu.SemaphoreType.DMA((2 * max(pieces, 1),)),
        pltpu.SemaphoreType.DMA((2, 4)),
        pltpu.SemaphoreType.DMA,
    ]
    flops = 2 * pieces * rows * depth * (width + 256) + 2 * 2 * 2 * TILE * width * prefix
    return pl.pallas_call(
        functools.partial(step_kernel, pieces, rows, heads),
        grid_spec=pltpu.PrefetchScalarGridSpec(
            num_scalar_prefetch=2,
            grid=(),
            in_specs=specs,
            out_specs=[any_spec] * 3,
            scratch_shapes=scratch,
        ),
        out_shape=out_shape,
        input_output_aliases=aliases,
        compiler_params=pltpu.CompilerParams(vmem_limit_bytes=VMEM_LIMIT),
        cost_estimate=pl.CostEstimate(flops=flops, bytes_accessed=12 << 20, transcendentals=0),
    )(ids, lists, *operands)


def send_kernel(has, count, *refs):
    refs = refs[1:]
    atts, weights = refs[:count], refs[count:2 * count]
    rest = iter(refs[2 * count:])
    arrived = [[next(rest) for _ in range(has[i])] for i in range(count)]
    outs = refs[-count:]
    for i in range(count):
        made = jnp.dot(atts[i][...], weights[i][...], preferred_element_type=jnp.float32)
        made = made.astype(jnp.bfloat16).astype(jnp.float32)
        for other in arrived[i]:
            made = made + other[...].astype(jnp.float32)
        outs[i][...] = made.astype(jnp.bfloat16)


def run_send(ids, att, w_out, arrived, pieces, chunk_rows, columns, out_width=None, into=None):
    count = len(arrived)
    block = 512
    per_piece = columns // block
    width = att.shape[1]
    in_specs = [pl.BlockSpec((chunk_rows, width), lambda b, ids, i=i: (ids[i], 0)) for i in range(count)]
    in_specs += [pl.BlockSpec((width, block), lambda b, ids, p=p: (0, p * per_piece + b)) for p in pieces]
    operands = [att] * count + [w_out] * count
    has = []
    for i, group in enumerate(arrived):
        has.append(len(group))
        for other in group:
            offset = pieces[i] * per_piece if other.shape[1] != columns else 0
            in_specs.append(pl.BlockSpec((chunk_rows, block), lambda b, ids, o=offset: (0, o + b)))
            operands.append(other)
    aliases = {}
    if into is not None:
        aliases = {1 + len(operands): 0}
        operands.append(into)
        in_specs.append(pl.BlockSpec(memory_space=pl.ANY))
    out_width = out_width or columns
    out_specs = [
        pl.BlockSpec((chunk_rows, block), lambda b, ids, o=(p * per_piece if out_width != columns else 0): (0, o + b))
        for p in pieces
    ]
    return pl.pallas_call(
        functools.partial(send_kernel, has, count),
        grid_spec=pltpu.PrefetchScalarGridSpec(
            num_scalar_prefetch=1, grid=(per_piece,), in_specs=in_specs, out_specs=out_specs
        ),
        out_shape=[jax.ShapeDtypeStruct((chunk_rows, out_width), jnp.bfloat16)] * count,
        input_output_aliases=aliases,
        compiler_params=pltpu.CompilerParams(vmem_limit_bytes=VMEM_LIMIT),
        cost_estimate=pl.CostEstimate(
            flops=2 * count * chunk_rows * width * columns, bytes_accessed=4 << 20, transcendentals=0
        ),
    )(ids, *operands)


def tables(seg_ids, seg_doc, doc_lens, prefix, cache):
    tokens = seg_ids.shape[0]
    tiles = tokens // TILE
    blocks = prefix // KEY_BLOCK
    docs = doc_lens.shape[0]
    order = jnp.arange(tokens, dtype=jnp.int32)
    start = jnp.sum((seg_ids[None, :] < seg_ids[:, None]).astype(jnp.int32), axis=1, dtype=jnp.int32)
    positions = prefix + order - start
    segments = jnp.arange(seg_doc.shape[0], dtype=jnp.int32)
    tok_doc = jnp.sum(
        jnp.where(seg_ids[:, None] == segments[None, :], seg_doc[None, :], 0), axis=1, dtype=jnp.int32
    )
    doc_list = jnp.arange(docs, dtype=jnp.int32)
    doc_ends = jnp.sum(jnp.where(doc_list[None, :] <= doc_list[:, None], doc_lens[None, :], 0), axis=1)
    doc_starts = doc_ends - doc_lens
    lanes = jnp.arange(HEAD, dtype=jnp.int32)
    half = HEAD // 2
    inverse = ROPE_THETA ** (-(jnp.arange(half, dtype=jnp.float32) * 2.0 / HEAD))
    inverse = jnp.concatenate([inverse, inverse])
    angles = positions.astype(jnp.float32)[:, None] * inverse[None, :]
    cosine = jnp.cos(angles)
    sine = jnp.sin(angles) * jnp.where(lanes < half, -1.0, 1.0)[None, :]
    doc_bias = jnp.where(lanes[None, :] == tok_doc[:, None], 0.0, MASKED).astype(jnp.bfloat16)
    spot = jnp.arange(prefix, dtype=jnp.int32)
    low = jnp.pad(doc_starts, (0, HEAD - docs))
    high = jnp.pad(doc_ends, (0, HEAD - docs))
    one_hot = ((spot[:, None] >= low[None, :]) & (spot[:, None] < high[None, :])).astype(jnp.bfloat16)
    key_wide = jnp.concatenate([cache[:, :HEAD], one_hot], axis=1)
    first_key = jnp.maximum(jnp.arange(tiles, dtype=jnp.int32) - 1, 0) * TILE
    spots = first_key[:, None] + lanes[None, :]
    by_tile = seg_ids.reshape(tiles, TILE)
    earlier = jnp.concatenate([by_tile[:1], by_tile[:-1]], axis=0)
    later = jnp.concatenate([by_tile[1:2], by_tile[1:]], axis=0)
    window_seg = jnp.concatenate([earlier, later], axis=1)
    ok = (window_seg[:, None, :] == by_tile[:, :, None]) & (
        spots[:, None, :] <= order.reshape(tiles, TILE)[:, :, None]
    )
    own_bias = jnp.where(ok, 0.0, MASKED).astype(jnp.float32).reshape(tokens, HEAD)
    present = jnp.any(tok_doc.reshape(tiles, TILE)[:, :, None] == doc_list[None, None, :], axis=1)
    edge = jnp.arange(blocks, dtype=jnp.int32) * KEY_BLOCK
    overlap = (doc_starts[:, None] < edge[None, :] + KEY_BLOCK) & (doc_ends[:, None] > edge[None, :])
    flags = jnp.any(present[:, :, None] & overlap[None, :, :], axis=1).astype(jnp.int32)
    block_ids = jnp.arange(blocks, dtype=jnp.int32)
    rank = jnp.sum(jnp.where(block_ids[None, :, None] > block_ids[None, None, :], flags[:, None, :], 0), axis=2)
    listed = jnp.sum(
        jnp.where((rank[:, :, None] == block_ids[None, None, :]) & (flags[:, :, None] > 0), block_ids[None, :, None], 0),
        axis=1,
    )
    lists = jnp.concatenate([jnp.sum(flags, axis=1, keepdims=True), listed], axis=1).astype(jnp.int32).reshape(-1)
    return cosine, sine, key_wide, doc_bias, own_bias, lists


def local(
    hidden_in, norm_gain, w_query, keyvalue_weight, w_out, prefix_keyvalue_cache, seg_ids, seg_doc, doc_lens
):
    size = lax.axis_size("tensor")
    tokens = seg_ids.shape[0]
    prefix = prefix_keyvalue_cache.shape[0]
    chunk_rows, depth = hidden_in.shape
    heads = w_query.shape[1] // HEAD
    order = ring_order(size)
    half = size // 2
    rank = lax.axis_index("tensor")

    forward_pairs = [(order[i], order[(i + 1) % size]) for i in range(size)]
    backward_pairs = [(b, a) for a, b in forward_pairs]

    def forward(x):
        return lax.ppermute(x, "tensor", forward_pairs)

    def backward(x):
        return lax.ppermute(x, "tensor", backward_pairs)

    if keyvalue_weight.shape[1] == HEAD:
        swap = [(i, i ^ 1) for i in range(size)]
        even = rank % 2 == 0
        other_weight, other_cache = lax.ppermute((keyvalue_weight, prefix_keyvalue_cache), "tensor", swap)
        keyvalue_weight = jnp.concatenate(
            [jnp.where(even, keyvalue_weight, other_weight), jnp.where(even, other_weight, keyvalue_weight)], axis=1
        )
        prefix_keyvalue_cache = jnp.concatenate(
            [
                jnp.where(even, prefix_keyvalue_cache, other_cache),
                jnp.where(even, other_cache, prefix_keyvalue_cache),
            ],
            axis=1,
        )

    place = {r: i for i, r in enumerate(order)}
    around = np.array([[order[(place[r] + d) % size] for d in range(size)] for r in range(size)], np.int32)
    ready = ready_tiles(order)
    most = max(len(ready[r][s]) for r in range(size) for s in range(half + 2))
    plan = np.zeros((size, half + 2, 3 + most), np.int32)
    for r in range(size):
        for s in range(half + 2):
            ids = [0, 0]
            if s < half:
                ids = [2 * around[r][(-s) % size], 2 * around[r][s]]
            elif s == half:
                ids = [2 * around[r][half], 2 * around[r][half] + 1]
            row = ids + [len(ready[r][s])] + ready[r][s]
            plan[r, s, :len(row)] = row
    my_plan = jnp.asarray(plan)[rank]
    my_around = jnp.asarray(around)[rank]

    cosine, sine, key_wide, doc_bias, own_bias, lists = tables(
        seg_ids, seg_doc, doc_lens, prefix, prefix_keyvalue_cache
    )
    gain = norm_gain.astype(jnp.float32).reshape(1, depth)
    fixed = (gain, w_query, keyvalue_weight, cosine, sine, key_wide, prefix_keyvalue_cache, doc_bias, own_bias)
    dims = (tokens, heads, prefix, depth)

    from_left, from_right = hidden_in, hidden_in
    state = None
    held = [hidden_in]
    for s in range(half):
        if s + 1 < half:
            next_left, next_right = forward(from_left), backward(from_right)
        else:
            next_left, next_right = forward(from_left[:TILE]), backward(from_right[TILE:])
        state = run_step(my_plan[s], lists, held, fixed, state, dims)
        from_left, from_right = next_left, next_right
        held = [from_left, from_right]
    state = run_step(my_plan[half], lists, held, fixed, state, dims)
    state = run_step(my_plan[half + 1], lists, [], fixed, state, dims)
    att = state[2]

    columns = depth // 2

    def ids_of(*distances):
        return jnp.stack([my_around[d % size] for d in distances])

    sent = run_send(ids_of(half, half), att, w_out, [[], []], [0, 1], chunk_rows, columns)
    arrived = [[[forward(sent[0])], []], [[], [backward(sent[1])]]]
    for d in range(half - 1, 0, -1):
        following = []
        for piece in range(2):
            made = run_send(ids_of(d, -d), att, w_out, arrived[piece], [piece, piece], chunk_rows, columns)
            following.append([[forward(made[0])], [backward(made[1])]])
        arrived = following
    out = None
    for piece in range(2):
        group = [arrived[piece][0][0], arrived[piece][1][0], hidden_in]
        out = run_send(
            ids_of(0), att, w_out, [group], [piece], chunk_rows, columns, out_width=depth, into=out
        )[0]
    return out


def solution(mesh):
    return jax.shard_map(
        local,
        mesh=mesh,
        in_specs=(
            P(("dp", "tensor"), None),
            P(),
            P(None, "tensor"),
            P(None, "tensor"),
            P("tensor", None),
            P(None, "tensor"),
            P("dp"),
            P("dp"),
            P(),
        ),
        out_specs=P(("dp", "tensor"), None),
        check_vma=False,
    )
```

```python
import functools
import math

import jax
import jax.numpy as jnp
import numpy as np
from jax import lax
from jax.experimental import pallas as pl
from jax.experimental.pallas import tpu as pltpu
from jax.sharding import PartitionSpec as P

HEAD = 128
TILE = 64
KEY_BLOCK = 256
GROUP = 4
MASKED = -1e30
EPS = 1e-05
ROPE_THETA = 500000.0
VMEM_LIMIT = 48 * 1024 * 1024


def ring_order(size):
    zs = 4 if size % 8 == 0 else 1
    ys = size // zs
    if zs == 1:
        return list(range(size))
    cycle = [(0, 0)]
    for y in range(ys):
        column = range(1, zs) if y % 2 == 0 else range(zs - 1, 0, -1)
        cycle += [(z, y) for z in column]
    cycle += [(0, y) for y in range(ys - 1, 0, -1)]
    return [z * ys + y for z, y in cycle]


def ready_tiles(order):
    size = len(order)
    place = {rank: i for i, rank in enumerate(order)}

    def distance(a, b):
        apart = (place[a] - place[b]) % size
        return min(apart, size - apart)

    steps = size // 2 + 1
    found = [[[] for _ in range(steps + 1)] for _ in range(size)]
    for rank in range(size):
        last = order[(place[rank] + size // 2) % size]
        for chunk in range(size):
            own = distance(rank, chunk)
            before = distance(rank, chunk - 1) if chunk else 0
            late = steps if max(own, before) == size // 2 and chunk != last else None
            first = max(own, before)
            found[rank][first if late is None else late].append(2 * chunk)
            found[rank][own].append(2 * chunk + 1)
    return found


def step_kernel(pieces, rows, heads, *refs):
    total = pieces * rows
    width = heads * HEAD
    it = iter(refs)
    ids, lists = next(it), next(it)
    xs = [next(it) for _ in range(pieces)]
    gain, wq, wkv, cos_tab, sin_tab, key_wide, cache, doc_bias, own_bias = [next(it) for _ in range(9)]
    first = pieces == 1 and rows == 128
    if not first:
        next(it), next(it), next(it)
    qb, kvb, att = next(it), next(it), next(it)
    (x_s, xn_s, wq_s, wkv_s, cos_s, sin_s, qo_s, kvo_s, key_s, val_s, qt_s, kvt_s, db_s, ob_s, sc_s, at_s,
     wide_s, own_s, m_s, l_s, o_s, sem_in, sem_tab, sem_w, sem_k, sem_out, sem_tile, sem_att) = list(it)
    blocks = key_wide.shape[0] - 1
    stride = blocks + GROUP

    key_copy = pltpu.make_async_copy(key_wide, key_s, sem_k.at[0])
    val_copy = pltpu.make_async_copy(cache.at[:, pl.ds(HEAD, HEAD)], val_s, sem_k.at[1])
    if pieces:
        x_copies, tab_copies = [], []
        for i in range(pieces):
            span = pl.ds(i * rows, rows)
            place = pl.ds(pl.multiple_of(ids[i] * TILE, TILE), rows)
            x_copies.append(pltpu.make_async_copy(xs[i], x_s.at[span], sem_in.at[i]))
            tab_copies.append(pltpu.make_async_copy(cos_tab.at[place], cos_s.at[span], sem_tab.at[2 * i]))
            tab_copies.append(pltpu.make_async_copy(sin_tab.at[place], sin_s.at[span], sem_tab.at[2 * i + 1]))
        for copy in x_copies:
            copy.start()
        w_copies = [
            pltpu.make_async_copy(wq.at[:, pl.ds(c, 256)], wq_s.at[:, pl.ds(c, 256)], sem_w.at[j])
            for j, c in enumerate(range(0, width, 256))
        ]
        w_copies.append(pltpu.make_async_copy(wkv, wkv_s, sem_w.at[len(w_copies)]))
        for copy in w_copies:
            copy.start()
        for copy in tab_copies:
            copy.start()
    key_copy.start()
    val_copy.start()

    if pieces:
        gains = gain[...]
        for i in range(pieces):
            x_copies[i].wait()

        def norm_rows(r, carry):
            span = pl.ds(pl.multiple_of(r * 16, 16), 16)
            values = x_s[span, :].astype(jnp.float32)
            mean_square = jnp.mean(values * values, axis=-1, keepdims=True)
            xn_s[span, :] = (values * lax.rsqrt(mean_square + EPS) * gains).astype(jnp.bfloat16)
            return carry

        lax.fori_loop(0, total // 16, norm_rows, 0, unroll=4)
        for copy in tab_copies:
            copy.wait()
        cosine, sine = cos_s[...], sin_s[...]

        def rotate(v):
            return (v * cosine + pltpu.roll(v, HEAD // 2, 1) * sine).astype(jnp.bfloat16)

        for j, c in enumerate(range(0, width, 256)):
            w_copies[j].wait()
            made = jnp.dot(xn_s[...], wq_s[:, c:c + 256], preferred_element_type=jnp.float32)
            for h in range(2):
                qo_s[c // HEAD + h] = rotate(made[:, h * HEAD:(h + 1) * HEAD])
        w_copies[-1].wait()
        made = jnp.dot(xn_s[...], wkv_s[...], preferred_element_type=jnp.float32)
        kvo_s[:, :HEAD] = rotate(made[:, :HEAD])
        kvo_s[:, HEAD:] = made[:, HEAD:].astype(jnp.bfloat16)
        outs = []
        for i in range(pieces):
            span = pl.ds(i * rows, rows)
            place = pl.ds(pl.multiple_of(ids[i] * TILE, TILE), rows)
            outs.append(pltpu.make_async_copy(qo_s.at[:, span], qb.at[:, place], sem_out.at[2 * i]))
            outs.append(pltpu.make_async_copy(kvo_s.at[span], kvb.at[place], sem_out.at[2 * i + 1]))
        for copy in outs:
            copy.start()
        for copy in outs:
            copy.wait()

    count = ids[2]
    factor = math.log2(math.e) / math.sqrt(HEAD)

    def fetches(i, slot):
        tile = ids[3 + i]
        at = pl.multiple_of(tile * TILE, TILE)
        before = pl.multiple_of(jnp.maximum(tile - 1, 0) * TILE, TILE)
        return [
            pltpu.make_async_copy(qb.at[:, pl.ds(at, TILE)], qt_s.at[slot], sem_tile.at[slot, 0]),
            pltpu.make_async_copy(kvb.at[pl.ds(before, 2 * TILE)], kvt_s.at[slot], sem_tile.at[slot, 1]),
            pltpu.make_async_copy(doc_bias.at[pl.ds(at, TILE)], db_s.at[slot], sem_tile.at[slot, 2]),
            pltpu.make_async_copy(own_bias.at[pl.ds(at, TILE)], ob_s.at[slot], sem_tile.at[slot, 3]),
        ]

    def att_copy(i):
        at = pl.multiple_of(ids[3 + i] * TILE, TILE)
        return pltpu.make_async_copy(at_s, att.at[pl.ds(at, TILE)], sem_att)

    @pl.when(count > 0)
    def _():
        for copy in fetches(0, 0):
            copy.start()

    key_copy.wait()
    val_copy.wait()
    contract_last = (((1,), (1,)), ((), ()))

    def one_tile(i, carry):
        slot = lax.rem(i, 2)

        @pl.when(i + 1 < count)
        def _():
            for copy in fetches(i + 1, 1 - slot):
                copy.start()

        for copy in fetches(i, slot):
            copy.wait()
        tile = ids[3 + i]
        needed = lists[tile * stride]
        for h in range(heads):
            wide_s[h * TILE:(h + 1) * TILE, :HEAD] = qt_s[slot, h]
            wide_s[h * TILE:(h + 1) * TILE, HEAD:] = db_s[slot]
        own = lax.dot_general(
            wide_s[:, :HEAD], kvt_s[slot, :, :HEAD], contract_last, preferred_element_type=jnp.float32
        )
        own = (own.reshape(heads, TILE, HEAD) + ob_s[slot][None]).reshape(heads * TILE, HEAD)
        own_s[...] = own
        m_s[...] = own

        def score_group(g, c):
            top_here = m_s[...]
            for u in range(GROUP):
                block = lists[tile * stride + 1 + g * GROUP + u]
                scores = jnp.dot(wide_s[...], key_s[block], preferred_element_type=jnp.float32)
                sc_s[g * GROUP + u] = scores
                top_here = jnp.maximum(top_here, jnp.maximum(scores[:, :HEAD], scores[:, HEAD:]))
            m_s[...] = top_here
            return c

        lax.fori_loop(0, needed, score_group, 0)
        top = jnp.max(m_s[...], axis=1, keepdims=True)
        weights = jnp.exp2((own_s[...] - top) * factor)
        l_s[...] = weights
        o_s[...] = jnp.dot(weights.astype(jnp.bfloat16), kvt_s[slot, :, HEAD:], preferred_element_type=jnp.float32)

        def value_group(g, c):
            total_here, sum_here = o_s[...], l_s[...]
            for u in range(GROUP):
                block = lists[tile * stride + 1 + g * GROUP + u]
                at = pl.multiple_of(jnp.minimum(block, blocks - 1) * KEY_BLOCK, KEY_BLOCK)
                weights = jnp.exp2((sc_s[g * GROUP + u] - top) * factor)
                sum_here = sum_here + (weights[:, :HEAD] + weights[:, HEAD:])
                total_here = total_here + jnp.dot(
                    weights.astype(jnp.bfloat16), val_s[pl.ds(at, KEY_BLOCK), :], preferred_element_type=jnp.float32
                )
            o_s[...] = total_here
            l_s[...] = sum_here
            return c

        lax.fori_loop(0, needed, value_group, 0)
        result = (o_s[...] / jnp.sum(l_s[...], axis=1, keepdims=True)).astype(jnp.bfloat16)

        @pl.when(i > 0)
        def _():
            att_copy(i - 1).wait()

        for h in range(heads):
            at_s[:, h * HEAD:(h + 1) * HEAD] = result[h * TILE:(h + 1) * TILE]
        att_copy(i).start()
        return carry

    lax.fori_loop(0, count, one_tile, 0)

    @pl.when(count > 0)
    def _():
        att_copy(count - 1).wait()


def run_step(ids, lists, xs, fixed, state, dims):
    tokens, heads, prefix, depth = dims
    pieces = len(xs)
    rows = xs[0].shape[0] if pieces else TILE
    total = max(pieces * rows, 16)
    width = heads * HEAD
    any_spec = pl.BlockSpec(memory_space=pl.ANY)
    vmem_spec = pl.BlockSpec(memory_space=pltpu.VMEM)
    operands = list(xs) + list(fixed)
    specs = [any_spec] * pieces + [vmem_spec] + [any_spec] * (len(fixed) - 1)
    aliases = {}
    if state is not None:
        aliases = {2 + len(operands) + i: i for i in range(3)}
        operands += list(state)
        specs += [any_spec] * 3
    out_shape = [
        jax.ShapeDtypeStruct((heads, tokens, HEAD), jnp.bfloat16),
        jax.ShapeDtypeStruct((tokens, 2 * HEAD), jnp.bfloat16),
        jax.ShapeDtypeStruct((tokens, width), jnp.bfloat16),
    ]
    small = 16
    w_rows = depth if pieces else small
    scratch = [
        pltpu.VMEM((total, depth), jnp.bfloat16),
        pltpu.VMEM((total, depth), jnp.bfloat16),
        pltpu.VMEM((w_rows, width), jnp.bfloat16),
        pltpu.VMEM((w_rows, 2 * HEAD), jnp.bfloat16),
        pltpu.VMEM((total, HEAD), jnp.float32),
        pltpu.VMEM((total, HEAD), jnp.float32),
        pltpu.VMEM((heads, total, HEAD), jnp.bfloat16),
        pltpu.VMEM((total, 2 * HEAD), jnp.bfloat16),
        pltpu.VMEM((prefix // KEY_BLOCK + 1, 2 * HEAD, KEY_BLOCK), jnp.bfloat16),
        pltpu.VMEM((prefix, HEAD), jnp.bfloat16),
        pltpu.VMEM((2, heads, TILE, HEAD), jnp.bfloat16),
        pltpu.VMEM((2, 2 * TILE, 2 * HEAD), jnp.bfloat16),
        pltpu.VMEM((2, TILE, HEAD), jnp.bfloat16),
        pltpu.VMEM((2, TILE, HEAD), jnp.float32),
        pltpu.VMEM((prefix // KEY_BLOCK, heads * TILE, KEY_BLOCK), jnp.float32),
        pltpu.VMEM((TILE, width), jnp.bfloat16),
        pltpu.VMEM((heads * TILE, 2 * HEAD), jnp.bfloat16),
        pltpu.VMEM((heads * TILE, HEAD), jnp.float32),
        pltpu.VMEM((heads * TILE, HEAD), jnp.float32),
        pltpu.VMEM((heads * TILE, HEAD), jnp.float32),
        pltpu.VMEM((heads * TILE, HEAD), jnp.float32),
        pltpu.SemaphoreType.DMA((max(pieces, 1),)),
        pltpu.SemaphoreType.DMA((2 * max(pieces, 1),)),
        pltpu.SemaphoreType.DMA((width // 256 + 1,)),
        pltpu.SemaphoreType.DMA((2,)),
        pltpu.SemaphoreType.DMA((2 * max(pieces, 1),)),
        pltpu.SemaphoreType.DMA((2, 4)),
        pltpu.SemaphoreType.DMA,
    ]
    flops = 2 * pieces * rows * depth * (width + 256) + 2 * 2 * 2 * TILE * width * prefix
    return pl.pallas_call(
        functools.partial(step_kernel, pieces, rows, heads),
        grid_spec=pltpu.PrefetchScalarGridSpec(
            num_scalar_prefetch=2,
            grid=(),
            in_specs=specs,
            out_specs=[any_spec] * 3,
            scratch_shapes=scratch,
        ),
        out_shape=out_shape,
        input_output_aliases=aliases,
        compiler_params=pltpu.CompilerParams(vmem_limit_bytes=VMEM_LIMIT),
        cost_estimate=pl.CostEstimate(flops=flops, bytes_accessed=12 << 20, transcendentals=0),
    )(ids, lists, *operands)


def send_kernel(has, shared, *refs):
    count = len(has)
    rest = iter(refs[1:])
    atts = [next(rest) for _ in range(count)]
    weights = [next(rest)] * count if shared else [next(rest) for _ in range(count)]
    arrived = [[next(rest) for _ in range(many)] for many in has]
    outs = refs[-count:]
    for i in range(count):
        made = jnp.dot(atts[i][...], weights[i][...], preferred_element_type=jnp.float32)
        made = made.astype(jnp.bfloat16).astype(jnp.float32)
        for other in arrived[i]:
            made = made + other[...].astype(jnp.float32)
        outs[i][...] = made.astype(jnp.bfloat16)


def run_send(ids, att, w_out, arrived, pieces, chunk_rows, columns):
    count = len(arrived)
    block = 512
    per_piece = columns // block
    width = att.shape[1]
    shared = len(set(pieces)) == 1
    used = pieces[:1] if shared else pieces
    row_block = pl.BlockSpec((chunk_rows, block), lambda b, ids: (0, b))
    in_specs = [pl.BlockSpec((chunk_rows, width), lambda b, ids, i=i: (ids[i], 0)) for i in range(count)]
    in_specs += [pl.BlockSpec((width, block), lambda b, ids, p=p: (0, p * per_piece + b)) for p in used]
    operands = [att] * count + [w_out] * len(used)
    for group in arrived:
        operands += group
        in_specs += [row_block] * len(group)
    return pl.pallas_call(
        functools.partial(send_kernel, [len(group) for group in arrived], shared),
        grid_spec=pltpu.PrefetchScalarGridSpec(
            num_scalar_prefetch=1, grid=(per_piece,), in_specs=in_specs, out_specs=[row_block] * count
        ),
        out_shape=[jax.ShapeDtypeStruct((chunk_rows, columns), jnp.bfloat16)] * count,
        compiler_params=pltpu.CompilerParams(vmem_limit_bytes=VMEM_LIMIT),
        cost_estimate=pl.CostEstimate(
            flops=2 * count * chunk_rows * width * columns, bytes_accessed=4 << 20, transcendentals=0
        ),
    )(ids, *operands)


def tables(seg_ids, seg_doc, doc_lens, prefix, cache):
    tokens = seg_ids.shape[0]
    tiles = tokens // TILE
    blocks = prefix // KEY_BLOCK
    docs = doc_lens.shape[0]
    order = jnp.arange(tokens, dtype=jnp.int32)
    start = jnp.sum((seg_ids[None, :] < seg_ids[:, None]).astype(jnp.int32), axis=1, dtype=jnp.int32)
    positions = prefix + order - start
    segments = jnp.arange(seg_doc.shape[0], dtype=jnp.int32)
    tok_doc = jnp.sum(
        jnp.where(seg_ids[:, None] == segments[None, :], seg_doc[None, :], 0), axis=1, dtype=jnp.int32
    )
    doc_list = jnp.arange(docs, dtype=jnp.int32)
    doc_ends = jnp.sum(jnp.where(doc_list[None, :] <= doc_list[:, None], doc_lens[None, :], 0), axis=1)
    doc_starts = doc_ends - doc_lens
    lanes = jnp.arange(HEAD, dtype=jnp.int32)
    half = HEAD // 2
    inverse = ROPE_THETA ** (-(jnp.arange(half, dtype=jnp.float32) * 2.0 / HEAD))
    inverse = jnp.concatenate([inverse, inverse])
    angles = positions.astype(jnp.float32)[:, None] * inverse[None, :]
    cosine = jnp.cos(angles)
    sine = jnp.sin(angles) * jnp.where(lanes < half, -1.0, 1.0)[None, :]
    doc_bias = jnp.where(lanes[None, :] == tok_doc[:, None], 0.0, MASKED).astype(jnp.bfloat16)
    spot = jnp.arange(prefix + KEY_BLOCK, dtype=jnp.int32).reshape(blocks + 1, 1, KEY_BLOCK)
    low = jnp.pad(doc_starts, (0, HEAD - docs), constant_values=prefix).reshape(1, HEAD, 1)
    high = jnp.pad(doc_ends, (0, HEAD - docs), constant_values=prefix + KEY_BLOCK).reshape(1, HEAD, 1)
    one_hot = ((spot >= low) & (spot < high)).astype(jnp.bfloat16)
    by_block = cache[:, :HEAD].reshape(blocks, KEY_BLOCK, HEAD).transpose(0, 2, 1)
    key_wide = jnp.concatenate([jnp.pad(by_block, ((0, 1), (0, 0), (0, 0))), one_hot], axis=1)
    first_key = jnp.maximum(jnp.arange(tiles, dtype=jnp.int32) - 1, 0) * TILE
    spots = first_key[:, None] + lanes[None, :]
    by_tile = seg_ids.reshape(tiles, TILE)
    earlier = jnp.concatenate([by_tile[:1], by_tile[:-1]], axis=0)
    later = jnp.concatenate([by_tile[1:2], by_tile[1:]], axis=0)
    window_seg = jnp.concatenate([earlier, later], axis=1)
    ok = (window_seg[:, None, :] == by_tile[:, :, None]) & (
        spots[:, None, :] <= order.reshape(tiles, TILE)[:, :, None]
    )
    own_bias = jnp.where(ok, 0.0, MASKED).astype(jnp.float32).reshape(tokens, HEAD)
    present = jnp.any(tok_doc.reshape(tiles, TILE)[:, :, None] == doc_list[None, None, :], axis=1)
    edge = jnp.arange(blocks, dtype=jnp.int32) * KEY_BLOCK
    overlap = (doc_starts[:, None] < edge[None, :] + KEY_BLOCK) & (doc_ends[:, None] > edge[None, :])
    flags = jnp.any(present[:, :, None] & overlap[None, :, :], axis=1).astype(jnp.int32)
    block_ids = jnp.arange(blocks, dtype=jnp.int32)
    rank = jnp.sum(jnp.where(block_ids[None, :, None] > block_ids[None, None, :], flags[:, None, :], 0), axis=2)
    listed = jnp.sum(
        jnp.where((rank[:, :, None] == block_ids[None, None, :]) & (flags[:, :, None] > 0), block_ids[None, :, None], 0),
        axis=1,
    )
    count = jnp.sum(flags, axis=1, keepdims=True)
    listed = jnp.where(block_ids[None, :] < count, listed, blocks)
    groups = (count + GROUP - 1) // GROUP
    lists = jnp.pad(jnp.concatenate([groups, listed], axis=1), ((0, 0), (0, GROUP - 1)))
    lists = lists.astype(jnp.int32).reshape(-1)
    return cosine, sine, key_wide, doc_bias, own_bias, lists


def local(
    hidden_in, norm_gain, w_query, keyvalue_weight, w_out, prefix_keyvalue_cache, seg_ids, seg_doc, doc_lens
):
    size = lax.axis_size("tensor")
    tokens = seg_ids.shape[0]
    prefix = prefix_keyvalue_cache.shape[0]
    chunk_rows, depth = hidden_in.shape
    heads = w_query.shape[1] // HEAD
    order = ring_order(size)
    half = size // 2
    rank = lax.axis_index("tensor")

    forward_pairs = [(order[i], order[(i + 1) % size]) for i in range(size)]
    backward_pairs = [(b, a) for a, b in forward_pairs]

    def forward(x):
        return lax.ppermute(x, "tensor", forward_pairs)

    def backward(x):
        return lax.ppermute(x, "tensor", backward_pairs)

    if keyvalue_weight.shape[1] == HEAD:
        swap = [(i, i ^ 1) for i in range(size)]
        even = rank % 2 == 0
        other_weight, other_cache = lax.ppermute((keyvalue_weight, prefix_keyvalue_cache), "tensor", swap)
        keyvalue_weight = jnp.concatenate(
            [jnp.where(even, keyvalue_weight, other_weight), jnp.where(even, other_weight, keyvalue_weight)], axis=1
        )
        prefix_keyvalue_cache = jnp.concatenate(
            [
                jnp.where(even, prefix_keyvalue_cache, other_cache),
                jnp.where(even, other_cache, prefix_keyvalue_cache),
            ],
            axis=1,
        )

    place = {r: i for i, r in enumerate(order)}
    around = np.array([[order[(place[r] + d) % size] for d in range(size)] for r in range(size)], np.int32)
    ready = ready_tiles(order)
    most = max(len(ready[r][s]) for r in range(size) for s in range(half + 2))
    plan = np.zeros((size, half + 2, 3 + most), np.int32)
    for r in range(size):
        for s in range(half + 2):
            ids = [0, 0]
            if s < half:
                ids = [2 * around[r][(-s) % size], 2 * around[r][s]]
            elif s == half:
                ids = [2 * around[r][half], 2 * around[r][half] + 1]
            row = ids + [len(ready[r][s])] + ready[r][s]
            plan[r, s, :len(row)] = row
    my_plan = jnp.asarray(plan)[rank]
    my_around = jnp.asarray(around)[rank]

    cosine, sine, key_wide, doc_bias, own_bias, lists = tables(
        seg_ids, seg_doc, doc_lens, prefix, prefix_keyvalue_cache
    )
    gain = norm_gain.astype(jnp.float32).reshape(1, depth)
    fixed = (gain, w_query, keyvalue_weight, cosine, sine, key_wide, prefix_keyvalue_cache, doc_bias, own_bias)
    dims = (tokens, heads, prefix, depth)

    from_left, from_right = hidden_in, hidden_in
    state = None
    held = [hidden_in]
    for s in range(half):
        if s + 1 < half:
            next_left, next_right = forward(from_left), backward(from_right)
        else:
            next_left, next_right = forward(from_left[:TILE]), backward(from_right[TILE:])
        state = run_step(my_plan[s], lists, held, fixed, state, dims)
        (next_left, next_right), state = lax.optimization_barrier(((next_left, next_right), tuple(state)))
        from_left, from_right = next_left, next_right
        held = [from_left, from_right]
    state = run_step(my_plan[half], lists, held, fixed, state, dims)
    columns = depth // 2

    def ids_of(*distances):
        return jnp.stack([my_around[d % size] for d in distances])

    sent = run_send(ids_of(half, half), state[2], w_out, [[], []], [0, 1], chunk_rows, columns)
    sent, state = lax.optimization_barrier((tuple(sent), tuple(state)))
    arrived = [[[forward(sent[0])], []], [[], [backward(sent[1])]]]
    att = run_step(my_plan[half + 1], lists, [], fixed, state, dims)[2]
    for d in range(half - 1, 0, -1):
        following = []
        for piece in range(2):
            made = run_send(ids_of(d, -d), att, w_out, arrived[piece], [piece, piece], chunk_rows, columns)
            following.append([[forward(made[0])], [backward(made[1])]])
        arrived = following
    own = run_send(ids_of(0), att, w_out, [[]], [0], chunk_rows, depth)[0]
    result = hidden_in.astype(jnp.float32) + own.astype(jnp.float32)
    (left_0,), (right_0,) = arrived[0]
    (left_1,), (right_1,) = arrived[1]
    summed = jnp.concatenate(
        [left.astype(jnp.float32) + right.astype(jnp.float32) for left, right in ((left_0, right_0), (left_1, right_1))],
        axis=1,
    )
    return (result + summed).astype(jnp.bfloat16)


def solution(mesh):
    return jax.shard_map(
        local,
        mesh=mesh,
        in_specs=(
            P(("dp", "tensor"), None),
            P(),
            P(None, "tensor"),
            P(None, "tensor"),
            P("tensor", None),
            P(None, "tensor"),
            P("dp"),
            P("dp"),
            P(),
        ),
        out_specs=P(("dp", "tensor"), None),
        check_vma=False,
    )
```

```python
import functools
import math

import jax
import jax.numpy as jnp
import numpy as np
from jax import lax
from jax.experimental import pallas as pl
from jax.experimental.pallas import tpu as pltpu
from jax.sharding import PartitionSpec as P

HEAD = 128
TILE = 64
KEY_BLOCK = 256
GROUP = 4
MASKED = -1e30
EPS = 1e-05
ROPE_THETA = 500000.0
VMEM_LIMIT = 48 * 1024 * 1024


def ring_order(size):
    zs = 4 if size % 8 == 0 else 1
    ys = size // zs
    if zs == 1:
        return list(range(size))
    cycle = [(0, 0)]
    for y in range(ys):
        column = range(1, zs) if y % 2 == 0 else range(zs - 1, 0, -1)
        cycle += [(z, y) for z in column]
    cycle += [(0, y) for y in range(ys - 1, 0, -1)]
    return [z * ys + y for z, y in cycle]


def arrival_slots(order, rank):
    size = len(order)
    half = size // 2
    place = {r: i for i, r in enumerate(order)}
    slots = {}
    for chunk in range(size):
        behind = (place[rank] - place[chunk]) % size
        if behind == 0:
            slots[chunk, 0] = slots[chunk, 1] = 0
        elif behind < half:
            slots[chunk, 0], slots[chunk, 1] = 2 * behind - 1, 2 * behind
        elif behind == half:
            slots[chunk, 0] = slots[chunk, 1] = size - 1
        else:
            slots[chunk, 1], slots[chunk, 0] = 2 * (size - behind) - 1, 2 * (size - behind)
    return slots


def ready_tiles(order):
    size = len(order)
    found = [[[] for _ in range(size)] for _ in range(size)]
    for rank in range(size):
        slots = arrival_slots(order, rank)
        for chunk in range(size):
            before = slots[chunk - 1, 1] if chunk else slots[chunk, 1]
            lower = max(slots[chunk, 0], before)
            found[rank][lower].append(2 * chunk)
            found[rank][max(slots[chunk, 0], slots[chunk, 1])].append(2 * chunk + 1)
    return found


def step_kernel(pieces, rows, heads, *refs):
    total = pieces * rows
    width = heads * HEAD
    it = iter(refs)
    ids, lists = next(it), next(it)
    xs = [next(it) for _ in range(pieces)]
    gain, wq, wkv, cos_tab, sin_tab, key_wide, cache, doc_bias, own_bias = [next(it) for _ in range(9)]
    first = pieces == 1 and rows == 128
    if not first:
        next(it), next(it), next(it)
    qb, kvb, att = next(it), next(it), next(it)
    (x_s, xn_s, wq_s, wkv_s, cos_s, sin_s, qo_s, kvo_s, key_s, val_s, qt_s, kvt_s, db_s, ob_s, sc_s, at_s,
     wide_s, own_s, m_s, l_s, o_s, sem_in, sem_tab, sem_w, sem_k, sem_out, sem_tile, sem_att) = list(it)
    blocks = key_wide.shape[0] - 1
    stride = blocks + GROUP

    key_copy = pltpu.make_async_copy(key_wide, key_s, sem_k.at[0])
    val_copy = pltpu.make_async_copy(cache.at[:, pl.ds(HEAD, HEAD)], val_s, sem_k.at[1])
    if pieces:
        x_copies, tab_copies = [], []
        for i in range(pieces):
            span = pl.ds(i * rows, rows)
            place = pl.ds(pl.multiple_of(ids[i] * TILE, TILE), rows)
            x_copies.append(pltpu.make_async_copy(xs[i], x_s.at[span], sem_in.at[i]))
            tab_copies.append(pltpu.make_async_copy(cos_tab.at[place], cos_s.at[span], sem_tab.at[2 * i]))
            tab_copies.append(pltpu.make_async_copy(sin_tab.at[place], sin_s.at[span], sem_tab.at[2 * i + 1]))
        for copy in x_copies:
            copy.start()
        w_copies = [
            pltpu.make_async_copy(wq.at[:, pl.ds(c, 256)], wq_s.at[:, pl.ds(c, 256)], sem_w.at[j])
            for j, c in enumerate(range(0, width, 256))
        ]
        w_copies.append(pltpu.make_async_copy(wkv, wkv_s, sem_w.at[len(w_copies)]))
        for copy in w_copies:
            copy.start()
        for copy in tab_copies:
            copy.start()
    key_copy.start()
    val_copy.start()

    if pieces:
        gains = gain[...]
        for i in range(pieces):
            x_copies[i].wait()

        def norm_rows(r, carry):
            span = pl.ds(pl.multiple_of(r * 16, 16), 16)
            values = x_s[span, :].astype(jnp.float32)
            mean_square = jnp.mean(values * values, axis=-1, keepdims=True)
            xn_s[span, :] = (values * lax.rsqrt(mean_square + EPS) * gains).astype(jnp.bfloat16)
            return carry

        lax.fori_loop(0, total // 16, norm_rows, 0, unroll=4)
        for copy in tab_copies:
            copy.wait()
        cosine, sine = cos_s[...], sin_s[...]

        def rotate(v):
            return (v * cosine + pltpu.roll(v, HEAD // 2, 1) * sine).astype(jnp.bfloat16)

        for j, c in enumerate(range(0, width, 256)):
            w_copies[j].wait()
            made = jnp.dot(xn_s[...], wq_s[:, c:c + 256], preferred_element_type=jnp.float32)
            for h in range(2):
                qo_s[c // HEAD + h] = rotate(made[:, h * HEAD:(h + 1) * HEAD])
        w_copies[-1].wait()
        made = jnp.dot(xn_s[...], wkv_s[...], preferred_element_type=jnp.float32)
        kvo_s[:, :HEAD] = rotate(made[:, :HEAD])
        kvo_s[:, HEAD:] = made[:, HEAD:].astype(jnp.bfloat16)
        outs = []
        for i in range(pieces):
            span = pl.ds(i * rows, rows)
            place = pl.ds(pl.multiple_of(ids[i] * TILE, TILE), rows)
            outs.append(pltpu.make_async_copy(qo_s.at[:, span], qb.at[:, place], sem_out.at[2 * i]))
            outs.append(pltpu.make_async_copy(kvo_s.at[span], kvb.at[place], sem_out.at[2 * i + 1]))
        for copy in outs:
            copy.start()
        for copy in outs:
            copy.wait()

    count = ids[2]
    factor = math.log2(math.e) / math.sqrt(HEAD)

    def fetches(i, slot):
        tile = ids[3 + i]
        at = pl.multiple_of(tile * TILE, TILE)
        before = pl.multiple_of(jnp.maximum(tile - 1, 0) * TILE, TILE)
        return [
            pltpu.make_async_copy(qb.at[:, pl.ds(at, TILE)], qt_s.at[slot], sem_tile.at[slot, 0]),
            pltpu.make_async_copy(kvb.at[pl.ds(before, 2 * TILE)], kvt_s.at[slot], sem_tile.at[slot, 1]),
            pltpu.make_async_copy(doc_bias.at[pl.ds(at, TILE)], db_s.at[slot], sem_tile.at[slot, 2]),
            pltpu.make_async_copy(own_bias.at[pl.ds(at, TILE)], ob_s.at[slot], sem_tile.at[slot, 3]),
        ]

    def att_copy(i):
        at = pl.multiple_of(ids[3 + i] * TILE, TILE)
        return pltpu.make_async_copy(at_s, att.at[pl.ds(at, TILE)], sem_att)

    @pl.when(count > 0)
    def _():
        for copy in fetches(0, 0):
            copy.start()

    key_copy.wait()
    val_copy.wait()
    contract_last = (((1,), (1,)), ((), ()))

    def one_tile(i, carry):
        slot = lax.rem(i, 2)

        @pl.when(i + 1 < count)
        def _():
            for copy in fetches(i + 1, 1 - slot):
                copy.start()

        for copy in fetches(i, slot):
            copy.wait()
        tile = ids[3 + i]
        needed = lists[tile * stride]
        for h in range(heads):
            wide_s[h * TILE:(h + 1) * TILE, :HEAD] = qt_s[slot, h]
            wide_s[h * TILE:(h + 1) * TILE, HEAD:] = db_s[slot]
        own = lax.dot_general(
            wide_s[:, :HEAD], kvt_s[slot, :, :HEAD], contract_last, preferred_element_type=jnp.float32
        )
        own = (own.reshape(heads, TILE, HEAD) + ob_s[slot][None]).reshape(heads * TILE, HEAD)
        own_s[...] = own
        m_s[...] = own

        def score_group(g, c):
            top_here = m_s[...]
            for u in range(GROUP):
                block = lists[tile * stride + 1 + g * GROUP + u]
                scores = jnp.dot(wide_s[...], key_s[block], preferred_element_type=jnp.float32)
                sc_s[g * GROUP + u] = scores
                top_here = jnp.maximum(top_here, jnp.maximum(scores[:, :HEAD], scores[:, HEAD:]))
            m_s[...] = top_here
            return c

        lax.fori_loop(0, needed, score_group, 0)
        top = jnp.max(m_s[...], axis=1, keepdims=True)
        weights = jnp.exp2((own_s[...] - top) * factor)
        l_s[...] = weights
        o_s[...] = jnp.dot(weights.astype(jnp.bfloat16), kvt_s[slot, :, HEAD:], preferred_element_type=jnp.float32)

        def value_group(g, c):
            total_here, sum_here = o_s[...], l_s[...]
            for u in range(GROUP):
                block = lists[tile * stride + 1 + g * GROUP + u]
                at = pl.multiple_of(jnp.minimum(block, blocks - 1) * KEY_BLOCK, KEY_BLOCK)
                weights = jnp.exp2((sc_s[g * GROUP + u] - top) * factor)
                sum_here = sum_here + (weights[:, :HEAD] + weights[:, HEAD:])
                total_here = total_here + jnp.dot(
                    weights.astype(jnp.bfloat16), val_s[pl.ds(at, KEY_BLOCK), :], preferred_element_type=jnp.float32
                )
            o_s[...] = total_here
            l_s[...] = sum_here
            return c

        lax.fori_loop(0, needed, value_group, 0)
        result = (o_s[...] / jnp.sum(l_s[...], axis=1, keepdims=True)).astype(jnp.bfloat16)

        @pl.when(i > 0)
        def _():
            att_copy(i - 1).wait()

        for h in range(heads):
            at_s[:, h * HEAD:(h + 1) * HEAD] = result[h * TILE:(h + 1) * TILE]
        att_copy(i).start()
        return carry

    lax.fori_loop(0, count, one_tile, 0)

    @pl.when(count > 0)
    def _():
        att_copy(count - 1).wait()


def run_step(ids, lists, xs, fixed, state, dims):
    tokens, heads, prefix, depth = dims
    pieces = len(xs)
    rows = xs[0].shape[0] if pieces else TILE
    total = max(pieces * rows, 16)
    width = heads * HEAD
    any_spec = pl.BlockSpec(memory_space=pl.ANY)
    vmem_spec = pl.BlockSpec(memory_space=pltpu.VMEM)
    operands = list(xs) + list(fixed)
    specs = [any_spec] * pieces + [vmem_spec] + [any_spec] * (len(fixed) - 1)
    aliases = {}
    if state is not None:
        aliases = {2 + len(operands) + i: i for i in range(3)}
        operands += list(state)
        specs += [any_spec] * 3
    out_shape = [
        jax.ShapeDtypeStruct((heads, tokens, HEAD), jnp.bfloat16),
        jax.ShapeDtypeStruct((tokens, 2 * HEAD), jnp.bfloat16),
        jax.ShapeDtypeStruct((tokens, width), jnp.bfloat16),
    ]
    small = 16
    w_rows = depth if pieces else small
    scratch = [
        pltpu.VMEM((total, depth), jnp.bfloat16),
        pltpu.VMEM((total, depth), jnp.bfloat16),
        pltpu.VMEM((w_rows, width), jnp.bfloat16),
        pltpu.VMEM((w_rows, 2 * HEAD), jnp.bfloat16),
        pltpu.VMEM((total, HEAD), jnp.float32),
        pltpu.VMEM((total, HEAD), jnp.float32),
        pltpu.VMEM((heads, total, HEAD), jnp.bfloat16),
        pltpu.VMEM((total, 2 * HEAD), jnp.bfloat16),
        pltpu.VMEM((prefix // KEY_BLOCK + 1, 2 * HEAD, KEY_BLOCK), jnp.bfloat16),
        pltpu.VMEM((prefix, HEAD), jnp.bfloat16),
        pltpu.VMEM((2, heads, TILE, HEAD), jnp.bfloat16),
        pltpu.VMEM((2, 2 * TILE, 2 * HEAD), jnp.bfloat16),
        pltpu.VMEM((2, TILE, HEAD), jnp.bfloat16),
        pltpu.VMEM((2, TILE, HEAD), jnp.float32),
        pltpu.VMEM((prefix // KEY_BLOCK, heads * TILE, KEY_BLOCK), jnp.float32),
        pltpu.VMEM((TILE, width), jnp.bfloat16),
        pltpu.VMEM((heads * TILE, 2 * HEAD), jnp.bfloat16),
        pltpu.VMEM((heads * TILE, HEAD), jnp.float32),
        pltpu.VMEM((heads * TILE, HEAD), jnp.float32),
        pltpu.VMEM((heads * TILE, HEAD), jnp.float32),
        pltpu.VMEM((heads * TILE, HEAD), jnp.float32),
        pltpu.SemaphoreType.DMA((max(pieces, 1),)),
        pltpu.SemaphoreType.DMA((2 * max(pieces, 1),)),
        pltpu.SemaphoreType.DMA((width // 256 + 1,)),
        pltpu.SemaphoreType.DMA((2,)),
        pltpu.SemaphoreType.DMA((2 * max(pieces, 1),)),
        pltpu.SemaphoreType.DMA((2, 4)),
        pltpu.SemaphoreType.DMA,
    ]
    return pl.pallas_call(
        functools.partial(step_kernel, pieces, rows, heads),
        grid_spec=pltpu.PrefetchScalarGridSpec(
            num_scalar_prefetch=2,
            grid=(),
            in_specs=specs,
            out_specs=[any_spec] * 3,
            scratch_shapes=scratch,
        ),
        out_shape=out_shape,
        input_output_aliases=aliases,
        compiler_params=pltpu.CompilerParams(vmem_limit_bytes=VMEM_LIMIT),
        cost_estimate=pl.CostEstimate(flops=1 << 20, bytes_accessed=1 << 16, transcendentals=0),
    )(ids, lists, *operands)


def send_kernel(added, *refs):
    rest = iter(refs[1:])
    first, second, weights = next(rest), next(rest), next(rest)
    arrived = [next(rest) if has else None for has in added]
    outs = refs[-2:]
    both = jnp.concatenate([first[...], second[...]], axis=0)
    made = jnp.dot(both, weights[...], preferred_element_type=jnp.float32).astype(jnp.bfloat16)
    for i in range(2):
        mine = made[i * TILE:(i + 1) * TILE]
        if arrived[i] is not None:
            mine = (mine.astype(jnp.float32) + arrived[i][...].astype(jnp.float32)).astype(jnp.bfloat16)
        outs[i][...] = mine


def run_send(ids, att, w_out, arrived=(None, None)):
    width, columns = w_out.shape
    block = 1024
    row_block = pl.BlockSpec((TILE, block), lambda b, ids: (0, b))
    in_specs = [pl.BlockSpec((TILE, width), lambda b, ids, i=i: (ids[i], 0)) for i in range(2)]
    in_specs.append(pl.BlockSpec((width, block), lambda b, ids: (0, b)))
    given = [other for other in arrived if other is not None]
    return pl.pallas_call(
        functools.partial(send_kernel, [other is not None for other in arrived]),
        grid_spec=pltpu.PrefetchScalarGridSpec(
            num_scalar_prefetch=1,
            grid=(columns // block,),
            in_specs=in_specs + [row_block] * len(given),
            out_specs=[row_block] * 2,
        ),
        out_shape=[jax.ShapeDtypeStruct((TILE, columns), jnp.bfloat16)] * 2,
        compiler_params=pltpu.CompilerParams(vmem_limit_bytes=VMEM_LIMIT),
        cost_estimate=pl.CostEstimate(flops=1 << 20, bytes_accessed=1 << 16, transcendentals=0),
    )(ids, att, att, w_out, *given)


def tables(seg_ids, seg_doc, doc_lens, prefix, cache):
    tokens = seg_ids.shape[0]
    tiles = tokens // TILE
    blocks = prefix // KEY_BLOCK
    docs = doc_lens.shape[0]
    order = jnp.arange(tokens, dtype=jnp.int32)
    start = jnp.sum((seg_ids[None, :] < seg_ids[:, None]).astype(jnp.int32), axis=1, dtype=jnp.int32)
    positions = prefix + order - start
    segments = jnp.arange(seg_doc.shape[0], dtype=jnp.int32)
    tok_doc = jnp.sum(
        jnp.where(seg_ids[:, None] == segments[None, :], seg_doc[None, :], 0), axis=1, dtype=jnp.int32
    )
    doc_list = jnp.arange(docs, dtype=jnp.int32)
    doc_ends = jnp.sum(jnp.where(doc_list[None, :] <= doc_list[:, None], doc_lens[None, :], 0), axis=1)
    doc_starts = doc_ends - doc_lens
    lanes = jnp.arange(HEAD, dtype=jnp.int32)
    half = HEAD // 2
    inverse = ROPE_THETA ** (-(jnp.arange(half, dtype=jnp.float32) * 2.0 / HEAD))
    inverse = jnp.concatenate([inverse, inverse])
    angles = positions.astype(jnp.float32)[:, None] * inverse[None, :]
    cosine = jnp.cos(angles)
    sine = jnp.sin(angles) * jnp.where(lanes < half, -1.0, 1.0)[None, :]
    doc_bias = jnp.where(lanes[None, :] == tok_doc[:, None], 0.0, MASKED).astype(jnp.bfloat16)
    spot = jnp.arange(prefix + KEY_BLOCK, dtype=jnp.int32).reshape(blocks + 1, 1, KEY_BLOCK)
    low = jnp.pad(doc_starts, (0, HEAD - docs), constant_values=prefix).reshape(1, HEAD, 1)
    high = jnp.pad(doc_ends, (0, HEAD - docs), constant_values=prefix + KEY_BLOCK).reshape(1, HEAD, 1)
    one_hot = ((spot >= low) & (spot < high)).astype(jnp.bfloat16)
    by_block = cache[:, :HEAD].reshape(blocks, KEY_BLOCK, HEAD).transpose(0, 2, 1)
    key_wide = jnp.concatenate([jnp.pad(by_block, ((0, 1), (0, 0), (0, 0))), one_hot], axis=1)
    first_key = jnp.maximum(jnp.arange(tiles, dtype=jnp.int32) - 1, 0) * TILE
    spots = first_key[:, None] + lanes[None, :]
    by_tile = seg_ids.reshape(tiles, TILE)
    earlier = jnp.concatenate([by_tile[:1], by_tile[:-1]], axis=0)
    later = jnp.concatenate([by_tile[1:2], by_tile[1:]], axis=0)
    window_seg = jnp.concatenate([earlier, later], axis=1)
    ok = (window_seg[:, None, :] == by_tile[:, :, None]) & (
        spots[:, None, :] <= order.reshape(tiles, TILE)[:, :, None]
    )
    own_bias = jnp.where(ok, 0.0, MASKED).astype(jnp.float32).reshape(tokens, HEAD)
    present = jnp.any(tok_doc.reshape(tiles, TILE)[:, :, None] == doc_list[None, None, :], axis=1)
    edge = jnp.arange(blocks, dtype=jnp.int32) * KEY_BLOCK
    overlap = (doc_starts[:, None] < edge[None, :] + KEY_BLOCK) & (doc_ends[:, None] > edge[None, :])
    flags = jnp.any(present[:, :, None] & overlap[None, :, :], axis=1).astype(jnp.int32)
    block_ids = jnp.arange(blocks, dtype=jnp.int32)
    rank = jnp.sum(jnp.where(block_ids[None, :, None] > block_ids[None, None, :], flags[:, None, :], 0), axis=2)
    listed = jnp.sum(
        jnp.where((rank[:, :, None] == block_ids[None, None, :]) & (flags[:, :, None] > 0), block_ids[None, :, None], 0),
        axis=1,
    )
    count = jnp.sum(flags, axis=1, keepdims=True)
    listed = jnp.where(block_ids[None, :] < count, listed, blocks)
    groups = (count + GROUP - 1) // GROUP
    lists = jnp.pad(jnp.concatenate([groups, listed], axis=1), ((0, 0), (0, GROUP - 1)))
    lists = lists.astype(jnp.int32).reshape(-1)
    return cosine, sine, key_wide, doc_bias, own_bias, lists


def local(
    hidden_in, norm_gain, w_query, keyvalue_weight, w_out, prefix_keyvalue_cache, seg_ids, seg_doc, doc_lens
):
    size = lax.axis_size("tensor")
    tokens = seg_ids.shape[0]
    prefix = prefix_keyvalue_cache.shape[0]
    chunk_rows, depth = hidden_in.shape
    heads = w_query.shape[1] // HEAD
    order = ring_order(size)
    half = size // 2
    rank = lax.axis_index("tensor")

    forward_pairs = [(order[i], order[(i + 1) % size]) for i in range(size)]
    backward_pairs = [(b, a) for a, b in forward_pairs]

    def forward(x):
        return lax.ppermute(x, "tensor", forward_pairs)

    def backward(x):
        return lax.ppermute(x, "tensor", backward_pairs)

    if keyvalue_weight.shape[1] == HEAD:
        swap = [(i, i ^ 1) for i in range(size)]
        even = rank % 2 == 0
        other_weight, other_cache = lax.ppermute((keyvalue_weight, prefix_keyvalue_cache), "tensor", swap)
        keyvalue_weight = jnp.concatenate(
            [jnp.where(even, keyvalue_weight, other_weight), jnp.where(even, other_weight, keyvalue_weight)], axis=1
        )
        prefix_keyvalue_cache = jnp.concatenate(
            [
                jnp.where(even, prefix_keyvalue_cache, other_cache),
                jnp.where(even, other_cache, prefix_keyvalue_cache),
            ],
            axis=1,
        )

    place = {r: i for i, r in enumerate(order)}
    ready = ready_tiles(order)
    most = max(len(tiles) for by_slot in ready for tiles in by_slot)
    plan = np.zeros((size, size, 3 + most), np.int32)
    sends = np.zeros((size, half + 1, 2, 2), np.int32)
    flips = np.zeros((size,), np.int32)
    for r in range(size):
        flips[r] = int(order[(place[r] - 1) % size] == r - 1)
    for r in range(size):
        for s in range(size):
            d = (s + 1) // 2
            back, ahead = 2 * order[(place[r] - d) % size], 2 * order[(place[r] + d) % size]
            late = int(s % 2 == 0 and s > 0)
            ids = [2 * r, 0] if s == 0 else [back + late, ahead + 1 - late]
            row = ids + [len(ready[r][s])] + ready[r][s]
            plan[r, s, :len(row)] = row
        for d in range(half + 1):
            ahead, back = order[(place[r] + d) % size], order[(place[r] - d) % size]
            sends[r, d, 0] = [2 * ahead + flips[ahead], 2 * back + 1 - flips[back]]
            sends[r, d, 1] = [2 * ahead + 1 - flips[ahead], 2 * back + flips[back]]
    my_plan = jnp.asarray(plan)[rank]
    my_sends = jnp.asarray(sends)[rank]
    flipped = jnp.asarray(flips)[rank] > 0

    cosine, sine, key_wide, doc_bias, own_bias, lists = tables(
        seg_ids, seg_doc, doc_lens, prefix, prefix_keyvalue_cache
    )
    gain = norm_gain.astype(jnp.float32).reshape(1, depth)
    fixed = (gain, w_query, keyvalue_weight, cosine, sine, key_wide, prefix_keyvalue_cache, doc_bias, own_bias)
    dims = (tokens, heads, prefix, depth)

    lower, upper = hidden_in[:TILE], hidden_in[TILE:]
    pieces = {1: (forward(lower), backward(upper)), 2: (forward(upper), backward(lower))}
    state = run_step(my_plan[0], lists, [hidden_in], fixed, None, dims)
    for slot in range(1, size - 1):
        pieces[slot], state = lax.optimization_barrier((pieces[slot], tuple(state)))
        if slot < size - 2:
            following = min(slot + 2, size - 1)
            pieces[following] = (forward(pieces[slot][0]), backward(pieces[slot][1]))
        state = run_step(my_plan[slot], lists, pieces[slot], fixed, state, dims)

    def send(distance, stream, att, arrived=(None, None)):
        made = run_send(my_sends[distance, stream], att, w_out, arrived)
        return (made[0], made[1])

    early = send(half - 1, 1, state[2])
    early, pieces[size - 1], state = lax.optimization_barrier((early, pieces[size - 1], tuple(state)))
    early = (forward(early[0]), backward(early[1]))
    state = run_step(my_plan[size - 1], lists, pieces[size - 1], fixed, state, dims)
    early, state = lax.optimization_barrier((early, tuple(state)))
    made = send(half, 0, state[2])
    far = (forward(made[0]), backward(made[1]))
    early, made = lax.optimization_barrier((early, made))
    att = state[2]
    for distance in range(half - 1, 0, -1):
        if distance > 1:
            made = send(distance - 1, 1, att, early)
            early = (forward(made[0]), backward(made[1]))
            far, made = lax.optimization_barrier((far, made))
        else:
            early, far = lax.optimization_barrier((early, far))
        made = send(distance, 0, att, far)
        far = (forward(made[0]), backward(made[1]))
        early, made = lax.optimization_barrier((early, made))
    own = run_send(jnp.stack([2 * rank, 2 * rank + 1]).astype(jnp.int32), att, w_out)
    wide = [[part.astype(jnp.float32) for part in pair] for pair in (early, far)]
    with_far, with_early = wide[1][0] + wide[0][1], wide[0][0] + wide[1][1]
    halves = [jnp.where(flipped, with_early, with_far), jnp.where(flipped, with_far, with_early)]
    summed = jnp.concatenate([halves[i] + own[i].astype(jnp.float32) for i in range(2)], axis=0)
    return (hidden_in.astype(jnp.float32) + summed).astype(jnp.bfloat16)


def solution(mesh):
    return jax.shard_map(
        local,
        mesh=mesh,
        in_specs=(
            P(("dp", "tensor"), None),
            P(),
            P(None, "tensor"),
            P(None, "tensor"),
            P("tensor", None),
            P(None, "tensor"),
            P("dp"),
            P("dp"),
            P(),
        ),
        out_specs=P(("dp", "tensor"), None),
        check_vma=False,
    )
```

```python
import functools
import math

import jax
import jax.numpy as jnp
import numpy as np
from jax import lax
from jax.experimental import pallas as pl
from jax.experimental.pallas import tpu as pltpu
from jax.sharding import PartitionSpec as P

HEAD = 128
TILE = 64
KEY_BLOCK = 256
GROUP = 4
MASKED = -1e30
EPS = 1e-05
ROPE_THETA = 500000.0
VMEM_LIMIT = 48 * 1024 * 1024


def ring_order(size):
    zs = 4 if size % 8 == 0 else 1
    ys = size // zs
    if zs == 1:
        return list(range(size))
    cycle = [(0, 0)]
    for y in range(ys):
        column = range(1, zs) if y % 2 == 0 else range(zs - 1, 0, -1)
        cycle += [(z, y) for z in column]
    cycle += [(0, y) for y in range(ys - 1, 0, -1)]
    return [z * ys + y for z, y in cycle]


def arrival_slots(order, rank):
    size = len(order)
    half = size // 2
    place = {r: i for i, r in enumerate(order)}
    slots = {}
    for chunk in range(size):
        behind = (place[rank] - place[chunk]) % size
        if behind == 0:
            slots[chunk, 0] = slots[chunk, 1] = 0
        elif behind < half:
            slots[chunk, 0], slots[chunk, 1] = 2 * behind - 1, 2 * behind
        elif behind == half:
            slots[chunk, 0] = slots[chunk, 1] = size - 1
        else:
            slots[chunk, 1], slots[chunk, 0] = 2 * (size - behind) - 1, 2 * (size - behind)
    return slots


def ready_tiles(order):
    size = len(order)
    found = [[[] for _ in range(size)] for _ in range(size)]
    for rank in range(size):
        slots = arrival_slots(order, rank)
        for chunk in range(size):
            before = slots[chunk - 1, 1] if chunk else slots[chunk, 1]
            lower = max(slots[chunk, 0], before)
            found[rank][lower].append(2 * chunk)
            found[rank][max(slots[chunk, 0], slots[chunk, 1])].append(2 * chunk + 1)
    return found


def step_kernel(pieces, rows, heads, *refs):
    total = pieces * rows
    width = heads * HEAD
    it = iter(refs)
    ids, lists = next(it), next(it)
    xs = [next(it) for _ in range(pieces)]
    gain, wq, wkv, cos_tab, sin_tab, key_wide, cache, doc_bias, own_bias = [next(it) for _ in range(9)]
    first = pieces == 1 and rows == 128
    if not first:
        next(it), next(it), next(it)
    qb, kvb, att = next(it), next(it), next(it)
    (x_s, xn_s, wq_s, wkv_s, cos_s, sin_s, qo_s, kvo_s, key_s, val_s, qt_s, kvt_s, db_s, ob_s, sc_s, at_s,
     wide_s, own_s, o_s, sem_in, sem_tab, sem_w, sem_k, sem_out, sem_tile, sem_att) = list(it)
    blocks = key_wide.shape[0] - 1
    stride = blocks + GROUP

    key_copy = pltpu.make_async_copy(key_wide, key_s, sem_k.at[0])
    val_copy = pltpu.make_async_copy(cache.at[:, pl.ds(HEAD, HEAD)], val_s, sem_k.at[1])
    if pieces:
        x_copies, tab_copies = [], []
        for i in range(pieces):
            span = pl.ds(i * rows, rows)
            place = pl.ds(pl.multiple_of(ids[i] * TILE, TILE), rows)
            x_copies.append(pltpu.make_async_copy(xs[i], x_s.at[span], sem_in.at[i]))
            tab_copies.append(pltpu.make_async_copy(cos_tab.at[place], cos_s.at[span], sem_tab.at[2 * i]))
            tab_copies.append(pltpu.make_async_copy(sin_tab.at[place], sin_s.at[span], sem_tab.at[2 * i + 1]))
        for copy in x_copies:
            copy.start()
        w_copies = [
            pltpu.make_async_copy(wq.at[:, pl.ds(c, 256)], wq_s.at[:, pl.ds(c, 256)], sem_w.at[j])
            for j, c in enumerate(range(0, width, 256))
        ]
        w_copies.append(pltpu.make_async_copy(wkv, wkv_s, sem_w.at[len(w_copies)]))
        for copy in w_copies:
            copy.start()
        for copy in tab_copies:
            copy.start()
    if not pieces:
        key_copy.start()
        val_copy.start()
    else:
        gains = gain[...]
        for i in range(pieces):
            x_copies[i].wait()

        def norm_rows(r, carry):
            span = pl.ds(pl.multiple_of(r * 16, 16), 16)
            values = x_s[span, :].astype(jnp.float32)
            mean_square = jnp.mean(values * values, axis=-1, keepdims=True)
            xn_s[span, :] = (values * lax.rsqrt(mean_square + EPS) * gains).astype(jnp.bfloat16)
            return carry

        lax.fori_loop(0, total // 16, norm_rows, 0, unroll=4)
        key_copy.start()
        val_copy.start()
        for copy in tab_copies:
            copy.wait()
        cosine, sine = cos_s[...], sin_s[...]

        def rotate(v):
            return (v * cosine + pltpu.roll(v, HEAD // 2, 1) * sine).astype(jnp.bfloat16)

        for j, c in enumerate(range(0, width, 256)):
            w_copies[j].wait()
            made = jnp.dot(xn_s[...], wq_s[:, c:c + 256], preferred_element_type=jnp.float32)
            for h in range(2):
                qo_s[c // HEAD + h] = rotate(made[:, h * HEAD:(h + 1) * HEAD])
        w_copies[-1].wait()
        made = jnp.dot(xn_s[...], wkv_s[...], preferred_element_type=jnp.float32)
        kvo_s[:, :HEAD] = rotate(made[:, :HEAD])
        kvo_s[:, HEAD:] = made[:, HEAD:].astype(jnp.bfloat16)
        outs = []
        for i in range(pieces):
            span = pl.ds(i * rows, rows)
            place = pl.ds(pl.multiple_of(ids[i] * TILE, TILE), rows)
            outs.append(pltpu.make_async_copy(qo_s.at[:, span], qb.at[:, place], sem_out.at[2 * i]))
            outs.append(pltpu.make_async_copy(kvo_s.at[span], kvb.at[place], sem_out.at[2 * i + 1]))
        for copy in outs:
            copy.start()
        for copy in outs:
            copy.wait()

    count = ids[2]
    factor = math.log2(math.e) / math.sqrt(HEAD)

    def fetches(i, slot):
        tile = ids[3 + i]
        at = pl.multiple_of(tile * TILE, TILE)
        before = pl.multiple_of(jnp.maximum(tile - 1, 0) * TILE, TILE)
        return [
            pltpu.make_async_copy(qb.at[:, pl.ds(at, TILE)], qt_s.at[slot], sem_tile.at[slot, 0]),
            pltpu.make_async_copy(kvb.at[pl.ds(before, 2 * TILE)], kvt_s.at[slot], sem_tile.at[slot, 1]),
            pltpu.make_async_copy(doc_bias.at[pl.ds(at, TILE)], db_s.at[slot], sem_tile.at[slot, 2]),
            pltpu.make_async_copy(own_bias.at[pl.ds(at, TILE)], ob_s.at[slot], sem_tile.at[slot, 3]),
        ]

    def att_copy(i):
        at = pl.multiple_of(ids[3 + i] * TILE, TILE)
        return pltpu.make_async_copy(at_s, att.at[pl.ds(at, TILE)], sem_att)

    @pl.when(count > 0)
    def _():
        for copy in fetches(0, 0):
            copy.start()

    key_copy.wait()
    val_copy.wait()
    contract_last = (((1,), (1,)), ((), ()))

    def one_tile(i, carry):
        slot = lax.rem(i, 2)

        @pl.when(i + 1 < count)
        def _():
            for copy in fetches(i + 1, 1 - slot):
                copy.start()

        for copy in fetches(i, slot):
            copy.wait()
        tile = ids[3 + i]
        needed = lists[tile * stride]
        for h in range(heads):
            wide_s[h * TILE:(h + 1) * TILE, :HEAD] = qt_s[slot, h]
            wide_s[h * TILE:(h + 1) * TILE, HEAD:] = db_s[slot]
        own = lax.dot_general(
            wide_s[:, :HEAD], kvt_s[slot, :, :HEAD], contract_last, preferred_element_type=jnp.float32
        )
        own = (own.reshape(heads, TILE, HEAD) + ob_s[slot][None]).reshape(heads * TILE, HEAD)
        own_s[...] = own

        def attend(count):
            blocks_here = [lists[tile * stride + 1 + j] for j in range(count)]
            top = own_s[...]
            for j, block in enumerate(blocks_here):
                scores = jnp.dot(wide_s[...], key_s[block], preferred_element_type=jnp.float32)
                sc_s[j] = scores
                top = jnp.maximum(top, jnp.maximum(scores[:, :HEAD], scores[:, HEAD:]))
            top = jnp.max(top, axis=1, keepdims=True) * factor
            weights = jnp.exp2(own_s[...] * factor - top)
            sums = weights
            made = jnp.dot(weights.astype(jnp.bfloat16), kvt_s[slot, :, HEAD:], preferred_element_type=jnp.float32)
            for j, block in enumerate(blocks_here):
                at = pl.multiple_of(jnp.minimum(block, blocks - 1) * KEY_BLOCK, KEY_BLOCK)
                weights = jnp.exp2(sc_s[j] * factor - top)
                sums = sums + (weights[:, :HEAD] + weights[:, HEAD:])
                made = made + jnp.dot(
                    weights.astype(jnp.bfloat16), val_s[pl.ds(at, KEY_BLOCK), :], preferred_element_type=jnp.float32
                )
            o_s[...] = (made / jnp.sum(sums, axis=1, keepdims=True)).astype(jnp.bfloat16)

        for groups in range(1, blocks // GROUP + 1):

            @pl.when(needed == groups)
            def _(groups=groups):
                attend(groups * GROUP)

        @pl.when(i > 0)
        def _():
            att_copy(i - 1).wait()

        for h in range(heads):
            at_s[:, h * HEAD:(h + 1) * HEAD] = o_s[h * TILE:(h + 1) * TILE]
        att_copy(i).start()
        return carry

    lax.fori_loop(0, count, one_tile, 0)

    @pl.when(count > 0)
    def _():
        att_copy(count - 1).wait()


def run_step(ids, lists, xs, fixed, state, dims):
    tokens, heads, prefix, depth = dims
    pieces = len(xs)
    rows = xs[0].shape[0] if pieces else TILE
    total = max(pieces * rows, 16)
    width = heads * HEAD
    any_spec = pl.BlockSpec(memory_space=pl.ANY)
    vmem_spec = pl.BlockSpec(memory_space=pltpu.VMEM)
    operands = list(xs) + list(fixed)
    specs = [any_spec] * pieces + [vmem_spec] + [any_spec] * (len(fixed) - 1)
    aliases = {}
    if state is not None:
        aliases = {2 + len(operands) + i: i for i in range(3)}
        operands += list(state)
        specs += [any_spec] * 3
    out_shape = [
        jax.ShapeDtypeStruct((heads, tokens, HEAD), jnp.bfloat16),
        jax.ShapeDtypeStruct((tokens, 2 * HEAD), jnp.bfloat16),
        jax.ShapeDtypeStruct((tokens, width), jnp.bfloat16),
    ]
    small = 16
    w_rows = depth if pieces else small
    scratch = [
        pltpu.VMEM((total, depth), jnp.bfloat16),
        pltpu.VMEM((total, depth), jnp.bfloat16),
        pltpu.VMEM((w_rows, width), jnp.bfloat16),
        pltpu.VMEM((w_rows, 2 * HEAD), jnp.bfloat16),
        pltpu.VMEM((total, HEAD), jnp.float32),
        pltpu.VMEM((total, HEAD), jnp.float32),
        pltpu.VMEM((heads, total, HEAD), jnp.bfloat16),
        pltpu.VMEM((total, 2 * HEAD), jnp.bfloat16),
        pltpu.VMEM((prefix // KEY_BLOCK + 1, 2 * HEAD, KEY_BLOCK), jnp.bfloat16),
        pltpu.VMEM((prefix, HEAD), jnp.bfloat16),
        pltpu.VMEM((2, heads, TILE, HEAD), jnp.bfloat16),
        pltpu.VMEM((2, 2 * TILE, 2 * HEAD), jnp.bfloat16),
        pltpu.VMEM((2, TILE, HEAD), jnp.bfloat16),
        pltpu.VMEM((2, TILE, HEAD), jnp.float32),
        pltpu.VMEM((prefix // KEY_BLOCK, heads * TILE, KEY_BLOCK), jnp.float32),
        pltpu.VMEM((TILE, width), jnp.bfloat16),
        pltpu.VMEM((heads * TILE, 2 * HEAD), jnp.bfloat16),
        pltpu.VMEM((heads * TILE, HEAD), jnp.float32),
        pltpu.VMEM((heads * TILE, HEAD), jnp.bfloat16),
        pltpu.SemaphoreType.DMA((max(pieces, 1),)),
        pltpu.SemaphoreType.DMA((2 * max(pieces, 1),)),
        pltpu.SemaphoreType.DMA((width // 256 + 1,)),
        pltpu.SemaphoreType.DMA((2,)),
        pltpu.SemaphoreType.DMA((2 * max(pieces, 1),)),
        pltpu.SemaphoreType.DMA((2, 4)),
        pltpu.SemaphoreType.DMA,
    ]
    return pl.pallas_call(
        functools.partial(step_kernel, pieces, rows, heads),
        grid_spec=pltpu.PrefetchScalarGridSpec(
            num_scalar_prefetch=2,
            grid=(),
            in_specs=specs,
            out_specs=[any_spec] * 3,
            scratch_shapes=scratch,
        ),
        out_shape=out_shape,
        input_output_aliases=aliases,
        compiler_params=pltpu.CompilerParams(vmem_limit_bytes=VMEM_LIMIT),
        cost_estimate=pl.CostEstimate(flops=1 << 20, bytes_accessed=1 << 16, transcendentals=0),
    )(ids, lists, *operands)


def product_kernel(ids, first, second, weights, *outs):
    both = jnp.concatenate([first[...], second[...]], axis=0)
    made = jnp.dot(both, weights[...], preferred_element_type=jnp.float32).astype(jnp.bfloat16)
    for i in range(2):
        outs[i][...] = made[i * TILE:(i + 1) * TILE]


def product(ids, att, w_out):
    width, columns = w_out.shape
    block = 1024
    row_block = pl.BlockSpec((TILE, block), lambda b, ids: (0, b))
    in_specs = [pl.BlockSpec((TILE, width), lambda b, ids, i=i: (ids[i], 0)) for i in range(2)]
    in_specs.append(pl.BlockSpec((width, block), lambda b, ids: (0, b)))
    return pl.pallas_call(
        product_kernel,
        grid_spec=pltpu.PrefetchScalarGridSpec(
            num_scalar_prefetch=1, grid=(columns // block,), in_specs=in_specs, out_specs=[row_block] * 2
        ),
        out_shape=[jax.ShapeDtypeStruct((TILE, columns), jnp.bfloat16)] * 2,
        compiler_params=pltpu.CompilerParams(vmem_limit_bytes=VMEM_LIMIT),
        cost_estimate=pl.CostEstimate(flops=1 << 20, bytes_accessed=1 << 16, transcendentals=0),
    )(ids, att, att, w_out)


def tables(seg_ids, seg_doc, doc_lens, prefix, cache):
    tokens = seg_ids.shape[0]
    tiles = tokens // TILE
    blocks = prefix // KEY_BLOCK
    docs = doc_lens.shape[0]
    order = jnp.arange(tokens, dtype=jnp.int32)
    start = jnp.sum((seg_ids[None, :] < seg_ids[:, None]).astype(jnp.int32), axis=1, dtype=jnp.int32)
    positions = prefix + order - start
    segments = jnp.arange(seg_doc.shape[0], dtype=jnp.int32)
    tok_doc = jnp.sum(
        jnp.where(seg_ids[:, None] == segments[None, :], seg_doc[None, :], 0), axis=1, dtype=jnp.int32
    )
    doc_list = jnp.arange(docs, dtype=jnp.int32)
    doc_ends = jnp.sum(jnp.where(doc_list[None, :] <= doc_list[:, None], doc_lens[None, :], 0), axis=1)
    doc_starts = doc_ends - doc_lens
    lanes = jnp.arange(HEAD, dtype=jnp.int32)
    half = HEAD // 2
    inverse = ROPE_THETA ** (-(jnp.arange(half, dtype=jnp.float32) * 2.0 / HEAD))
    inverse = jnp.concatenate([inverse, inverse])
    angles = positions.astype(jnp.float32)[:, None] * inverse[None, :]
    cosine = jnp.cos(angles)
    sine = jnp.sin(angles) * jnp.where(lanes < half, -1.0, 1.0)[None, :]
    doc_bias = jnp.where(lanes[None, :] == tok_doc[:, None], 0.0, MASKED).astype(jnp.bfloat16)
    spot = jnp.arange(prefix + KEY_BLOCK, dtype=jnp.int32).reshape(blocks + 1, 1, KEY_BLOCK)
    low = jnp.pad(doc_starts, (0, HEAD - docs), constant_values=prefix).reshape(1, HEAD, 1)
    high = jnp.pad(doc_ends, (0, HEAD - docs), constant_values=prefix + KEY_BLOCK).reshape(1, HEAD, 1)
    one_hot = ((spot >= low) & (spot < high)).astype(jnp.bfloat16)
    by_block = cache[:, :HEAD].reshape(blocks, KEY_BLOCK, HEAD).transpose(0, 2, 1)
    key_wide = jnp.concatenate([jnp.pad(by_block, ((0, 1), (0, 0), (0, 0))), one_hot], axis=1)
    first_key = jnp.maximum(jnp.arange(tiles, dtype=jnp.int32) - 1, 0) * TILE
    spots = first_key[:, None] + lanes[None, :]
    by_tile = seg_ids.reshape(tiles, TILE)
    earlier = jnp.concatenate([by_tile[:1], by_tile[:-1]], axis=0)
    later = jnp.concatenate([by_tile[1:2], by_tile[1:]], axis=0)
    window_seg = jnp.concatenate([earlier, later], axis=1)
    ok = (window_seg[:, None, :] == by_tile[:, :, None]) & (
        spots[:, None, :] <= order.reshape(tiles, TILE)[:, :, None]
    )
    own_bias = jnp.where(ok, 0.0, MASKED).astype(jnp.float32).reshape(tokens, HEAD)
    present = jnp.any(tok_doc.reshape(tiles, TILE)[:, :, None] == doc_list[None, None, :], axis=1)
    edge = jnp.arange(blocks, dtype=jnp.int32) * KEY_BLOCK
    overlap = (doc_starts[:, None] < edge[None, :] + KEY_BLOCK) & (doc_ends[:, None] > edge[None, :])
    flags = jnp.any(present[:, :, None] & overlap[None, :, :], axis=1).astype(jnp.int32)
    block_ids = jnp.arange(blocks, dtype=jnp.int32)
    rank = jnp.sum(jnp.where(block_ids[None, :, None] > block_ids[None, None, :], flags[:, None, :], 0), axis=2)
    listed = jnp.sum(
        jnp.where((rank[:, :, None] == block_ids[None, None, :]) & (flags[:, :, None] > 0), block_ids[None, :, None], 0),
        axis=1,
    )
    count = jnp.sum(flags, axis=1, keepdims=True)
    listed = jnp.where(block_ids[None, :] < count, listed, blocks)
    groups = (count + GROUP - 1) // GROUP
    lists = jnp.pad(jnp.concatenate([groups, listed], axis=1), ((0, 0), (0, GROUP - 1)))
    lists = lists.astype(jnp.int32).reshape(-1)
    return cosine, sine, key_wide, doc_bias, own_bias, lists


def local(
    hidden_in, norm_gain, w_query, keyvalue_weight, w_out, prefix_keyvalue_cache, seg_ids, seg_doc, doc_lens
):
    size = lax.axis_size("tensor")
    tokens = seg_ids.shape[0]
    prefix = prefix_keyvalue_cache.shape[0]
    chunk_rows, depth = hidden_in.shape
    heads = w_query.shape[1] // HEAD
    order = ring_order(size)
    half = size // 2
    rank = lax.axis_index("tensor")

    forward_pairs = [(order[i], order[(i + 1) % size]) for i in range(size)]
    backward_pairs = [(b, a) for a, b in forward_pairs]

    def forward(x):
        return lax.ppermute(x, "tensor", forward_pairs)

    def backward(x):
        return lax.ppermute(x, "tensor", backward_pairs)

    if keyvalue_weight.shape[1] == HEAD:
        swap = [(i, i ^ 1) for i in range(size)]
        even = rank % 2 == 0
        other_weight, other_cache = lax.ppermute((keyvalue_weight, prefix_keyvalue_cache), "tensor", swap)
        keyvalue_weight = jnp.concatenate(
            [jnp.where(even, keyvalue_weight, other_weight), jnp.where(even, other_weight, keyvalue_weight)], axis=1
        )
        prefix_keyvalue_cache = jnp.concatenate(
            [
                jnp.where(even, prefix_keyvalue_cache, other_cache),
                jnp.where(even, other_cache, prefix_keyvalue_cache),
            ],
            axis=1,
        )

    place = {r: i for i, r in enumerate(order)}
    ready = ready_tiles(order)
    most = max(len(tiles) for by_slot in ready for tiles in by_slot)
    plan = np.zeros((size, size, 3 + most), np.int32)
    sends = np.zeros((size, half + 1, 2, 2), np.int32)
    flips = np.zeros((size,), np.int32)
    for r in range(size):
        flips[r] = int(order[(place[r] - 1) % size] == r - 1)
    for r in range(size):
        for s in range(size):
            d = (s + 1) // 2
            back, ahead = 2 * order[(place[r] - d) % size], 2 * order[(place[r] + d) % size]
            late = int(s % 2 == 0 and s > 0)
            ids = [2 * r, 0] if s == 0 else [back + late, ahead + 1 - late]
            row = ids + [len(ready[r][s])] + ready[r][s]
            plan[r, s, :len(row)] = row
        for d in range(half + 1):
            ahead, back = order[(place[r] + d) % size], order[(place[r] - d) % size]
            sends[r, d, 0] = [2 * ahead + flips[ahead], 2 * back + 1 - flips[back]]
            sends[r, d, 1] = [2 * ahead + 1 - flips[ahead], 2 * back + flips[back]]
    my_plan = jnp.asarray(plan)[rank]
    my_sends = jnp.asarray(sends)[rank]
    flipped = jnp.asarray(flips)[rank] > 0

    cosine, sine, key_wide, doc_bias, own_bias, lists = tables(
        seg_ids, seg_doc, doc_lens, prefix, prefix_keyvalue_cache
    )
    gain = norm_gain.astype(jnp.float32).reshape(1, depth)
    fixed = (gain, w_query, keyvalue_weight, cosine, sine, key_wide, prefix_keyvalue_cache, doc_bias, own_bias)
    dims = (tokens, heads, prefix, depth)

    lower, upper = hidden_in[:TILE], hidden_in[TILE:]
    pieces = {1: (forward(lower), backward(upper)), 2: (forward(upper), backward(lower))}
    state = run_step(my_plan[0], lists, [hidden_in], fixed, None, dims)
    for slot in range(1, size - 1):
        pieces[slot], state = lax.optimization_barrier((pieces[slot], tuple(state)))
        if slot < size - 2:
            following = min(slot + 2, size - 1)
            pieces[following] = (forward(pieces[slot][0]), backward(pieces[slot][1]))
        state = run_step(my_plan[slot], lists, pieces[slot], fixed, state, dims)

    def term(distance, stream, att):
        return tuple(product(my_sends[distance, stream], att, w_out))

    def pass_on(pair):
        return forward(pair[0]), backward(pair[1])

    def add(pair, arrived):
        return tuple((a.astype(jnp.float32) + b.astype(jnp.float32)).astype(jnp.bfloat16) for a, b in zip(pair, arrived))

    made = term(half - 1, 1, state[2])
    made, pieces[size - 1], state = lax.optimization_barrier((made, pieces[size - 1], tuple(state)))
    early = pass_on(made)
    att = run_step(my_plan[size - 1], lists, pieces[size - 1], fixed, state, dims)[2]
    made = term(half, 0, att)
    far = pass_on(made)
    for distance in range(half - 1, 0, -1):
        if distance > 1:
            made, att = lax.optimization_barrier((made, att))
            ahead = term(distance - 1, 1, att)
            early, ahead = lax.optimization_barrier((early, ahead))
            made = add(ahead, early)
            early = pass_on(made)
        if distance > 1:
            made, att = lax.optimization_barrier((made, att))
        else:
            early, made, att = lax.optimization_barrier((early, made, att))
        ahead = term(distance, 0, att)
        if distance == 1:
            own = product(jnp.stack([2 * rank, 2 * rank + 1]).astype(jnp.int32), att, w_out)
            ahead, own = lax.optimization_barrier((ahead, tuple(own)))
        far, ahead = lax.optimization_barrier((far, ahead))
        made = add(ahead, far)
        far = pass_on(made)
    wide = [[part.astype(jnp.float32) for part in pair] for pair in (early, far)]
    with_far, with_early = wide[1][0] + wide[0][1], wide[0][0] + wide[1][1]
    halves = [jnp.where(flipped, with_early, with_far), jnp.where(flipped, with_far, with_early)]
    summed = jnp.concatenate([halves[i] + own[i].astype(jnp.float32) for i in range(2)], axis=0)
    return (hidden_in.astype(jnp.float32) + summed).astype(jnp.bfloat16)


def solution(mesh):
    return jax.shard_map(
        local,
        mesh=mesh,
        in_specs=(
            P(("dp", "tensor"), None),
            P(),
            P(None, "tensor"),
            P(None, "tensor"),
            P("tensor", None),
            P(None, "tensor"),
            P("dp"),
            P("dp"),
            P(),
        ),
        out_specs=P(("dp", "tensor"), None),
        check_vma=False,
    )
```

```python
import functools
import math

import jax
import jax.numpy as jnp
import numpy as np
from jax import lax
from jax.experimental import pallas as pl
from jax.experimental.pallas import tpu as pltpu
from jax.sharding import PartitionSpec as P

HEAD = 128
TILE = 64
KEY_BLOCK = 128
GROUP = 4
CLASSES = (2, 3, 4, 6, 8)
MASKED = -1e30
EPS = 1e-05
ROPE_THETA = 500000.0
VMEM_LIMIT = 48 * 1024 * 1024


def ring_order(size):
    zs = 4 if size % 8 == 0 else 1
    ys = size // zs
    if zs == 1:
        return list(range(size))
    cycle = [(0, 0)]
    for y in range(ys):
        column = range(1, zs) if y % 2 == 0 else range(zs - 1, 0, -1)
        cycle += [(z, y) for z in column]
    cycle += [(0, y) for y in range(ys - 1, 0, -1)]
    return [z * ys + y for z, y in cycle]


def arrival_slots(order, rank):
    size = len(order)
    half = size // 2
    place = {r: i for i, r in enumerate(order)}
    slots = {}
    for chunk in range(size):
        behind = (place[rank] - place[chunk]) % size
        if behind == 0:
            slots[chunk, 0] = slots[chunk, 1] = 0
        elif behind < half:
            slots[chunk, 0], slots[chunk, 1] = 2 * behind - 1, 2 * behind
        elif behind == half:
            slots[chunk, 0] = slots[chunk, 1] = size - 1
        else:
            slots[chunk, 1], slots[chunk, 0] = 2 * (size - behind) - 1, 2 * (size - behind)
    return slots


def ready_tiles(order):
    size = len(order)
    found = [[[] for _ in range(size)] for _ in range(size)]
    for rank in range(size):
        slots = arrival_slots(order, rank)
        for chunk in range(size):
            before = slots[chunk - 1, 1] if chunk else slots[chunk, 1]
            lower = max(slots[chunk, 0], before)
            found[rank][lower].append(2 * chunk)
            found[rank][max(slots[chunk, 0], slots[chunk, 1])].append(2 * chunk + 1)
    return found


def step_kernel(pieces, rows, heads, *refs):
    total = pieces * rows
    width = heads * HEAD
    queries = heads * TILE
    it = iter(refs)
    ids, lists = next(it), next(it)
    xs = [next(it) for _ in range(pieces)]
    gain, starts, wq, wkv, cos_tab, sin_tab, one_hot, cache, values_t, doc_bias = [next(it) for _ in range(10)]
    if pieces > 1:
        next(it), next(it), next(it)
    qb, kvb, att = next(it), next(it), next(it)
    (x_s, xn_s, wq_s, wkv_s, cos_s, sin_s, qo_s, kvo_s, kg_s, vg_s, qt_s, kvt_s, db_s, sc_s, at_s, wide_s, own_s,
     sem_in, sem_tab, sem_w, sem_g, sem_out, sem_tile, sem_att) = list(it)
    blocks = cache.shape[0] // KEY_BLOCK
    stride = blocks + 1
    count = ids[2]
    factor = math.log2(math.e) / math.sqrt(HEAD)

    def gathers(i, slot, j):
        block = lists[ids[3 + i] * stride + 1 + j]
        mask_at = pl.ds(pl.multiple_of(block * KEY_BLOCK, KEY_BLOCK), KEY_BLOCK)
        at = pl.ds(pl.multiple_of(jnp.minimum(block, blocks - 1) * KEY_BLOCK, KEY_BLOCK), KEY_BLOCK)
        to = pl.ds(pl.multiple_of(j * KEY_BLOCK, KEY_BLOCK), KEY_BLOCK)
        return [
            pltpu.make_async_copy(cache.at[at, pl.ds(0, HEAD)], kg_s.at[slot, to, pl.ds(0, HEAD)], sem_g.at[slot, 0, j]),
            pltpu.make_async_copy(one_hot.at[mask_at], kg_s.at[slot, to, pl.ds(HEAD, HEAD)], sem_g.at[slot, 1, j]),
            pltpu.make_async_copy(values_t.at[:, at], vg_s.at[slot, :, to], sem_g.at[slot, 2, j]),
        ]

    def gather_count(i):
        return lists[ids[3 + i] * stride] * GROUP

    def start_gather(i, slot):
        def body(j, c):
            for copy in gathers(i, slot, j):
                copy.start()
            return c

        lax.fori_loop(0, gather_count(i), body, 0)

    def wait_gather(i, slot):
        def body(j, c):
            for copy in gathers(i, slot, j):
                copy.wait()
            return c

        lax.fori_loop(0, gather_count(i), body, 0)

    x_copies, tab_copies = [], []
    for i in range(pieces):
        span = pl.ds(i * rows, rows)
        place = pl.ds(pl.multiple_of(ids[i] * TILE, TILE), rows)
        x_copies.append(pltpu.make_async_copy(xs[i], x_s.at[span], sem_in.at[i]))
        tab_copies.append(pltpu.make_async_copy(cos_tab.at[place], cos_s.at[span], sem_tab.at[2 * i]))
        tab_copies.append(pltpu.make_async_copy(sin_tab.at[place], sin_s.at[span], sem_tab.at[2 * i + 1]))
    for copy in x_copies:
        copy.start()
    w_copies = [
        pltpu.make_async_copy(wq.at[:, pl.ds(c, 256)], wq_s.at[:, pl.ds(c, 256)], sem_w.at[j])
        for j, c in enumerate(range(0, width, 256))
    ]
    w_copies.append(pltpu.make_async_copy(wkv, wkv_s, sem_w.at[len(w_copies)]))
    for copy in w_copies:
        copy.start()
    for copy in tab_copies:
        copy.start()
    gains = gain[...]
    for copy in x_copies:
        copy.wait()

    def norm_rows(r, carry):
        span = pl.ds(pl.multiple_of(r * 16, 16), 16)
        values = x_s[span, :].astype(jnp.float32)
        mean_square = jnp.mean(values * values, axis=-1, keepdims=True)
        xn_s[span, :] = (values * lax.rsqrt(mean_square + EPS) * gains).astype(jnp.bfloat16)
        return carry

    lax.fori_loop(0, total // 16, norm_rows, 0, unroll=4)

    @pl.when(count > 0)
    def _():
        start_gather(0, 0)

    for copy in tab_copies:
        copy.wait()
    cosine, sine = cos_s[...], sin_s[...]

    def rotate(v):
        return (v * cosine + pltpu.roll(v, HEAD // 2, 1) * sine).astype(jnp.bfloat16)

    for j, c in enumerate(range(0, width, 256)):
        w_copies[j].wait()
        made = jnp.dot(xn_s[...], wq_s[:, c:c + 256], preferred_element_type=jnp.float32)
        for h in range(2):
            qo_s[c // HEAD + h] = rotate(made[:, h * HEAD:(h + 1) * HEAD])
    w_copies[-1].wait()
    made = jnp.dot(xn_s[...], wkv_s[...], preferred_element_type=jnp.float32)
    kvo_s[:, :HEAD] = rotate(made[:, :HEAD])
    kvo_s[:, HEAD:] = made[:, HEAD:].astype(jnp.bfloat16)
    outs = []
    for i in range(pieces):
        span = pl.ds(i * rows, rows)
        place = pl.ds(pl.multiple_of(ids[i] * TILE, TILE), rows)
        outs.append(pltpu.make_async_copy(qo_s.at[:, span], qb.at[:, place], sem_out.at[2 * i]))
        outs.append(pltpu.make_async_copy(kvo_s.at[span], kvb.at[place], sem_out.at[2 * i + 1]))
    for copy in outs:
        copy.start()
    for copy in outs:
        copy.wait()

    def fetches(i, slot):
        tile = ids[3 + i]
        at = pl.multiple_of(tile * TILE, TILE)
        before = pl.multiple_of(jnp.maximum(tile - 1, 0) * TILE, TILE)
        return [
            pltpu.make_async_copy(qb.at[:, pl.ds(at, TILE)], qt_s.at[slot], sem_tile.at[slot, 0]),
            pltpu.make_async_copy(kvb.at[pl.ds(before, 2 * TILE)], kvt_s.at[slot], sem_tile.at[slot, 1]),
            pltpu.make_async_copy(doc_bias.at[pl.ds(at, TILE)], db_s.at[slot], sem_tile.at[slot, 2]),
        ]

    def att_copy(i):
        at = pl.multiple_of(ids[3 + i] * TILE, TILE)
        return pltpu.make_async_copy(at_s, att.at[pl.ds(at, TILE)], sem_att)

    @pl.when(count > 0)
    def _():
        for copy in fetches(0, 0):
            copy.start()

    contract_last = (((1,), (1,)), ((), ()))

    def fold(x, op):
        return op(x.reshape(x.shape[0] // 8, 8, queries), axis=0)

    def one_tile(i, carry):
        slot = lax.rem(i, 2)

        @pl.when(i + 1 < count)
        def _():
            for copy in fetches(i + 1, 1 - slot):
                copy.start()
            start_gather(i + 1, 1 - slot)

        for copy in fetches(i, slot):
            copy.wait()
        tile = ids[3 + i]
        for h in range(heads):
            wide_s[h * TILE:(h + 1) * TILE, :HEAD] = qt_s[slot, h]
            wide_s[h * TILE:(h + 1) * TILE, HEAD:] = db_s[slot]
        own = lax.dot_general(
            kvt_s[slot, :, :HEAD], wide_s[:, :HEAD], contract_last, preferred_element_type=jnp.float32
        )
        key_at = jnp.maximum(tile - 1, 0) * TILE + lax.broadcasted_iota(jnp.int32, own.shape, 0)
        token = tile * TILE + lax.rem(lax.broadcasted_iota(jnp.int32, own.shape, 1), TILE)
        own_s[...] = jnp.where((key_at >= starts[tile]) & (key_at <= token), own, MASKED)
        own_values = jnp.transpose(kvt_s[slot, :, HEAD:].astype(jnp.float32)).astype(jnp.bfloat16)
        wait_gather(i, slot)
        step = GROUP * KEY_BLOCK

        def attend(groups):
            top = fold(own_s[...], jnp.max)
            for u in range(groups):
                span = slice(u * step, (u + 1) * step)
                scores = lax.dot_general(
                    kg_s[slot, span, :], wide_s[...], contract_last, preferred_element_type=jnp.float32
                )
                sc_s[span, :] = scores
                top = jnp.maximum(top, fold(scores, jnp.max))
            top = jnp.max(top, axis=0, keepdims=True) * factor
            weights = jnp.exp2(own_s[...] * factor - top)
            sums = fold(weights, jnp.sum)
            made = jnp.dot(own_values, weights.astype(jnp.bfloat16), preferred_element_type=jnp.float32)
            for u in range(groups):
                span = slice(u * step, (u + 1) * step)
                weights = jnp.exp2(sc_s[span, :] * factor - top)
                sums = sums + fold(weights, jnp.sum)
                made = made + jnp.dot(
                    vg_s[slot, :, span], weights.astype(jnp.bfloat16), preferred_element_type=jnp.float32
                )
            made = made / jnp.sum(sums, axis=0, keepdims=True)
            result = jnp.transpose(made).astype(jnp.bfloat16)

            @pl.when(i > 0)
            def _():
                att_copy(i - 1).wait()

            for h in range(heads):
                at_s[:, h * HEAD:(h + 1) * HEAD] = result[h * TILE:(h + 1) * TILE]

        needed = lists[tile * stride]
        for groups in CLASSES:

            @pl.when(needed == groups)
            def _(groups=groups):
                attend(groups)

        att_copy(i).start()
        return carry

    lax.fori_loop(0, count, one_tile, 0)

    @pl.when(count > 0)
    def _():
        att_copy(count - 1).wait()


def run_step(ids, lists, xs, fixed, state, dims):
    tokens, heads, prefix, depth = dims
    pieces = len(xs)
    rows = xs[0].shape[0]
    total = pieces * rows
    width = heads * HEAD
    queries = heads * TILE
    any_spec = pl.BlockSpec(memory_space=pl.ANY)
    vmem_spec = pl.BlockSpec(memory_space=pltpu.VMEM)
    operands = list(xs) + list(fixed)
    specs = [any_spec] * pieces + [vmem_spec] * 2 + [any_spec] * (len(fixed) - 2)
    aliases = {}
    if state is not None:
        aliases = {2 + len(operands) + i: i for i in range(3)}
        operands += list(state)
        specs += [any_spec] * 3
    out_shape = [
        jax.ShapeDtypeStruct((heads, tokens, HEAD), jnp.bfloat16),
        jax.ShapeDtypeStruct((tokens, 2 * HEAD), jnp.bfloat16),
        jax.ShapeDtypeStruct((tokens, width), jnp.bfloat16),
    ]
    scratch = [
        pltpu.VMEM((total, depth), jnp.bfloat16),
        pltpu.VMEM((total, depth), jnp.bfloat16),
        pltpu.VMEM((depth, width), jnp.bfloat16),
        pltpu.VMEM((depth, 2 * HEAD), jnp.bfloat16),
        pltpu.VMEM((total, HEAD), jnp.float32),
        pltpu.VMEM((total, HEAD), jnp.float32),
        pltpu.VMEM((heads, total, HEAD), jnp.bfloat16),
        pltpu.VMEM((total, 2 * HEAD), jnp.bfloat16),
        pltpu.VMEM((2, prefix, 2 * HEAD), jnp.bfloat16),
        pltpu.VMEM((2, HEAD, prefix), jnp.bfloat16),
        pltpu.VMEM((2, heads, TILE, HEAD), jnp.bfloat16),
        pltpu.VMEM((2, 2 * TILE, 2 * HEAD), jnp.bfloat16),
        pltpu.VMEM((2, TILE, HEAD), jnp.bfloat16),
        pltpu.VMEM((prefix, queries), jnp.float32),
        pltpu.VMEM((TILE, width), jnp.bfloat16),
        pltpu.VMEM((queries, 2 * HEAD), jnp.bfloat16),
        pltpu.VMEM((2 * TILE, queries), jnp.float32),
        pltpu.SemaphoreType.DMA((pieces,)),
        pltpu.SemaphoreType.DMA((2 * pieces,)),
        pltpu.SemaphoreType.DMA((width // 256 + 1,)),
        pltpu.SemaphoreType.DMA((2, 3, prefix // KEY_BLOCK)),
        pltpu.SemaphoreType.DMA((2 * pieces,)),
        pltpu.SemaphoreType.DMA((2, 3)),
        pltpu.SemaphoreType.DMA,
    ]
    return pl.pallas_call(
        functools.partial(step_kernel, pieces, rows, heads),
        grid_spec=pltpu.PrefetchScalarGridSpec(
            num_scalar_prefetch=2,
            grid=(),
            in_specs=specs,
            out_specs=[any_spec] * 3,
            scratch_shapes=scratch,
        ),
        out_shape=out_shape,
        input_output_aliases=aliases,
        compiler_params=pltpu.CompilerParams(vmem_limit_bytes=VMEM_LIMIT),
        cost_estimate=pl.CostEstimate(flops=1 << 20, bytes_accessed=1 << 16, transcendentals=0),
    )(ids, lists, *operands)


def product_kernel(ids, first, second, weights, *outs):
    both = jnp.concatenate([first[...], second[...]], axis=0)
    made = jnp.dot(both, weights[...], preferred_element_type=jnp.float32).astype(jnp.bfloat16)
    for i in range(2):
        outs[i][...] = made[i * TILE:(i + 1) * TILE]


def product(ids, att, w_out):
    width, columns = w_out.shape
    block = 1024
    row_block = pl.BlockSpec((TILE, block), lambda b, ids: (0, b))
    in_specs = [pl.BlockSpec((TILE, width), lambda b, ids, i=i: (ids[i], 0)) for i in range(2)]
    in_specs.append(pl.BlockSpec((width, block), lambda b, ids: (0, b)))
    return pl.pallas_call(
        product_kernel,
        grid_spec=pltpu.PrefetchScalarGridSpec(
            num_scalar_prefetch=1, grid=(columns // block,), in_specs=in_specs, out_specs=[row_block] * 2
        ),
        out_shape=[jax.ShapeDtypeStruct((TILE, columns), jnp.bfloat16)] * 2,
        compiler_params=pltpu.CompilerParams(vmem_limit_bytes=VMEM_LIMIT),
        cost_estimate=pl.CostEstimate(flops=1 << 20, bytes_accessed=1 << 16, transcendentals=0),
    )(ids, att, att, w_out)


def tables(seg_ids, seg_doc, doc_lens, prefix, cache, heads):
    tokens = seg_ids.shape[0]
    tiles = tokens // TILE
    blocks = prefix // KEY_BLOCK
    docs = doc_lens.shape[0]
    order = jnp.arange(tokens, dtype=jnp.int32)
    start = jnp.sum((seg_ids[None, :] < seg_ids[:, None]).astype(jnp.int32), axis=1, dtype=jnp.int32)
    positions = prefix + order - start
    segments = jnp.arange(seg_doc.shape[0], dtype=jnp.int32)
    tok_doc = jnp.sum(
        jnp.where(seg_ids[:, None] == segments[None, :], seg_doc[None, :], 0), axis=1, dtype=jnp.int32
    )
    doc_list = jnp.arange(docs, dtype=jnp.int32)
    doc_ends = jnp.sum(jnp.where(doc_list[None, :] <= doc_list[:, None], doc_lens[None, :], 0), axis=1)
    doc_starts = doc_ends - doc_lens
    lanes = jnp.arange(HEAD, dtype=jnp.int32)
    half = HEAD // 2
    inverse = ROPE_THETA ** (-(jnp.arange(half, dtype=jnp.float32) * 2.0 / HEAD))
    inverse = jnp.concatenate([inverse, inverse])
    angles = positions.astype(jnp.float32)[:, None] * inverse[None, :]
    cosine = jnp.cos(angles)
    sine = jnp.sin(angles) * jnp.where(lanes < half, -1.0, 1.0)[None, :]
    doc_bias = jnp.where(lanes[None, :] == tok_doc[:, None], 0.0, MASKED).astype(jnp.bfloat16)
    spot = jnp.arange(prefix + KEY_BLOCK, dtype=jnp.int32)[:, None]
    low = jnp.pad(doc_starts, (0, HEAD - docs), constant_values=prefix)[None, :]
    high = jnp.pad(doc_ends, (0, HEAD - docs), constant_values=prefix + KEY_BLOCK)[None, :]
    one_hot = ((spot >= low) & (spot < high)).astype(jnp.bfloat16)
    values_t = cache[:, HEAD:].T
    starts = jnp.tile(start.reshape(tiles, 1, TILE), (1, 1, heads))
    present = jnp.any(tok_doc.reshape(tiles, TILE)[:, :, None] == doc_list[None, None, :], axis=1)
    edge = jnp.arange(blocks, dtype=jnp.int32) * KEY_BLOCK
    overlap = (doc_starts[:, None] < edge[None, :] + KEY_BLOCK) & (doc_ends[:, None] > edge[None, :])
    flags = jnp.any(present[:, :, None] & overlap[None, :, :], axis=1).astype(jnp.int32)
    block_ids = jnp.arange(blocks, dtype=jnp.int32)
    rank = jnp.sum(jnp.where(block_ids[None, :, None] > block_ids[None, None, :], flags[:, None, :], 0), axis=2)
    listed = jnp.sum(
        jnp.where((rank[:, :, None] == block_ids[None, None, :]) & (flags[:, :, None] > 0), block_ids[None, :, None], 0),
        axis=1,
    )
    count = jnp.sum(flags, axis=1, keepdims=True)
    listed = jnp.where(block_ids[None, :] < count, listed, blocks)
    groups = (count + GROUP - 1) // GROUP
    needed = jnp.full_like(groups, CLASSES[-1])
    for size in CLASSES[-2::-1]:
        needed = jnp.where(groups <= size, size, needed)
    lists = jnp.concatenate([needed, listed], axis=1).astype(jnp.int32).reshape(-1)
    return starts, cosine, sine, one_hot, values_t, doc_bias, lists


def local(
    hidden_in, norm_gain, w_query, keyvalue_weight, w_out, prefix_keyvalue_cache, seg_ids, seg_doc, doc_lens
):
    size = lax.axis_size("tensor")
    tokens = seg_ids.shape[0]
    prefix = prefix_keyvalue_cache.shape[0]
    chunk_rows, depth = hidden_in.shape
    heads = w_query.shape[1] // HEAD
    order = ring_order(size)
    half = size // 2
    rank = lax.axis_index("tensor")

    forward_pairs = [(order[i], order[(i + 1) % size]) for i in range(size)]
    backward_pairs = [(b, a) for a, b in forward_pairs]

    def forward(x):
        return lax.ppermute(x, "tensor", forward_pairs)

    def backward(x):
        return lax.ppermute(x, "tensor", backward_pairs)

    if keyvalue_weight.shape[1] == HEAD:
        swap = [(i, i ^ 1) for i in range(size)]
        even = rank % 2 == 0
        other_weight, other_cache = lax.ppermute((keyvalue_weight, prefix_keyvalue_cache), "tensor", swap)
        keyvalue_weight = jnp.concatenate(
            [jnp.where(even, keyvalue_weight, other_weight), jnp.where(even, other_weight, keyvalue_weight)], axis=1
        )
        prefix_keyvalue_cache = jnp.concatenate(
            [
                jnp.where(even, prefix_keyvalue_cache, other_cache),
                jnp.where(even, other_cache, prefix_keyvalue_cache),
            ],
            axis=1,
        )

    place = {r: i for i, r in enumerate(order)}
    ready = ready_tiles(order)
    most = max(len(tiles) for by_slot in ready for tiles in by_slot)
    plan = np.zeros((size, size, 3 + most), np.int32)
    sends = np.zeros((size, half + 1, 2, 2), np.int32)
    flips = np.zeros((size,), np.int32)
    for r in range(size):
        flips[r] = int(order[(place[r] - 1) % size] == r - 1)
    for r in range(size):
        for s in range(size):
            d = (s + 1) // 2
            back, ahead = 2 * order[(place[r] - d) % size], 2 * order[(place[r] + d) % size]
            late = int(s % 2 == 0 and s > 0)
            ids = [2 * r, 0] if s == 0 else [back + late, ahead + 1 - late]
            row = ids + [len(ready[r][s])] + ready[r][s]
            plan[r, s, :len(row)] = row
        for d in range(half + 1):
            ahead, back = order[(place[r] + d) % size], order[(place[r] - d) % size]
            sends[r, d, 0] = [2 * ahead + flips[ahead], 2 * back + 1 - flips[back]]
            sends[r, d, 1] = [2 * ahead + 1 - flips[ahead], 2 * back + flips[back]]
    my_plan = jnp.asarray(plan)[rank]
    my_sends = jnp.asarray(sends)[rank]
    flipped = jnp.asarray(flips)[rank] > 0

    starts, cosine, sine, one_hot, values_t, doc_bias, lists = tables(
        seg_ids, seg_doc, doc_lens, prefix, prefix_keyvalue_cache, heads
    )
    gain = norm_gain.astype(jnp.float32).reshape(1, depth)
    fixed = (
        gain, starts, w_query, keyvalue_weight, cosine, sine, one_hot, prefix_keyvalue_cache, values_t, doc_bias
    )
    dims = (tokens, heads, prefix, depth)

    lower, upper = hidden_in[:TILE], hidden_in[TILE:]
    pieces = {1: (forward(lower), backward(upper)), 2: (forward(upper), backward(lower))}
    pieces[1], own_rows = lax.optimization_barrier((pieces[1], hidden_in))
    pieces[3] = (forward(pieces[1][0]), backward(pieces[1][1]))
    state = run_step(my_plan[0], lists, [own_rows], fixed, None, dims)
    for slot in range(1, size - 1):
        pieces[slot], state = lax.optimization_barrier((pieces[slot], tuple(state)))
        if 1 < slot < size - 2:
            following = min(slot + 2, size - 1)
            pieces[following] = (forward(pieces[slot][0]), backward(pieces[slot][1]))
        state = run_step(my_plan[slot], lists, pieces[slot], fixed, state, dims)

    def term(distance, stream, att):
        return tuple(product(my_sends[distance, stream], att, w_out))

    def pass_on(pair):
        return forward(pair[0]), backward(pair[1])

    def add(pair, arrived):
        return tuple((a.astype(jnp.float32) + b.astype(jnp.float32)).astype(jnp.bfloat16) for a, b in zip(pair, arrived))

    made = term(half - 1, 1, state[2])
    made, pieces[size - 1], state = lax.optimization_barrier((made, pieces[size - 1], tuple(state)))
    early = pass_on(made)
    att = run_step(my_plan[size - 1], lists, pieces[size - 1], fixed, state, dims)[2]
    made = term(half, 0, att)
    far = pass_on(made)
    for distance in range(half - 1, 0, -1):
        if distance > 1:
            made, att = lax.optimization_barrier((made, att))
            ahead = term(distance - 1, 1, att)
            early, ahead = lax.optimization_barrier((early, ahead))
            made = add(ahead, early)
            early = pass_on(made)
        if distance > 1:
            made, att = lax.optimization_barrier((made, att))
        else:
            early, made, att = lax.optimization_barrier((early, made, att))
        ahead = term(distance, 0, att)
        if distance == 1:
            own = product(jnp.stack([2 * rank, 2 * rank + 1]).astype(jnp.int32), att, w_out)
            ahead, own = lax.optimization_barrier((ahead, tuple(own)))
        far, ahead = lax.optimization_barrier((far, ahead))
        made = add(ahead, far)
        far = pass_on(made)
    wide = [[part.astype(jnp.float32) for part in pair] for pair in (early, far)]
    with_far, with_early = wide[1][0] + wide[0][1], wide[0][0] + wide[1][1]
    halves = [jnp.where(flipped, with_early, with_far), jnp.where(flipped, with_far, with_early)]
    summed = jnp.concatenate([halves[i] + own[i].astype(jnp.float32) for i in range(2)], axis=0)
    return (hidden_in.astype(jnp.float32) + summed).astype(jnp.bfloat16)


def solution(mesh):
    return jax.shard_map(
        local,
        mesh=mesh,
        in_specs=(
            P(("dp", "tensor"), None),
            P(),
            P(None, "tensor"),
            P(None, "tensor"),
            P("tensor", None),
            P(None, "tensor"),
            P("dp"),
            P("dp"),
            P(),
        ),
        out_specs=P(("dp", "tensor"), None),
        check_vma=False,
    )
```

```python
import functools
import math

import jax
import jax.numpy as jnp
import numpy as np
from jax import lax
from jax.experimental import pallas as pl
from jax.experimental.pallas import tpu as pltpu
from jax.sharding import PartitionSpec as P

HEAD = 128
TILE = 64
KEY_BLOCK = 256
GROUP = 4
MASKED = -1e30
EPS = 1e-05
ROPE_THETA = 500000.0
VMEM_LIMIT = 48 * 1024 * 1024


def ring_order(size):
    zs = 4 if size % 8 == 0 else 1
    ys = size // zs
    if zs == 1:
        return list(range(size))
    cycle = [(0, 0)]
    for y in range(ys):
        column = range(1, zs) if y % 2 == 0 else range(zs - 1, 0, -1)
        cycle += [(z, y) for z in column]
    cycle += [(0, y) for y in range(ys - 1, 0, -1)]
    return [z * ys + y for z, y in cycle]


def tile_plan(order, early_halves):
    size = len(order)
    half = size // 2
    place = {r: i for i, r in enumerate(order)}
    spare = [0] + [4] * (half - 2) + [2] + [0] * (size - half)
    plans = []
    for rank in range(size):
        arrival, due = {}, {}
        for chunk in range(size):
            behind = (place[rank] - place[chunk]) % size
            distance = min(behind, size - behind)
            for upper in range(2):
                if distance == half:
                    arrival[chunk, upper] = due[chunk, upper] = half + 1
                elif distance == half - 1:
                    arrival[chunk, upper] = half - 1 if upper == int(behind != distance) else half
                    due[chunk, upper] = half if (chunk, upper) in early_halves[rank] else half + 1
                else:
                    arrival[chunk, upper] = distance
                    due[chunk, upper] = size - max(distance, 1)
        ready = {}
        for chunk in range(size):
            both = max(arrival[chunk, 0], arrival[chunk, 1])
            ready[chunk, 1] = both
            ready[chunk, 0] = max(arrival[chunk, 0], arrival[chunk - 1, 1]) if chunk else both
        calls, left = [], set(ready)
        for call in range(size):
            able = sorted((due[t], t) for t in left if ready[t] <= call)
            must = [t for when, t in able if when <= call]
            more = [t for when, t in able if when > call][:max(spare[call] - len(must), 0)]
            calls.append([2 * chunk + upper for chunk, upper in must + more])
            left -= set(must + more)
        assert not left and all(ready[t] <= due[t] for t in ready)
        plans.append(calls)
    return plans


def step_kernel(pieces, rows, heads, *refs):
    total = pieces * rows
    width = heads * HEAD
    it = iter(refs)
    ids, lists = next(it), next(it)
    xs = [next(it) for _ in range(pieces)]
    gain, wq, wkv, cos_tab, sin_tab, key_wide, cache, doc_bias, own_bias = [next(it) for _ in range(9)]
    first = pieces == 1 and rows == 128
    if not first:
        next(it), next(it), next(it)
    qb, kvb, att = next(it), next(it), next(it)
    (x_s, xn_s, wq_s, wkv_s, cos_s, sin_s, qo_s, kvo_s, key_s, val_s, qt_s, kvt_s, db_s, ob_s, sc_s, at_s,
     wide_s, own_s, o_s, sem_in, sem_tab, sem_w, sem_k, sem_out, sem_tile, sem_att) = list(it)
    blocks = key_wide.shape[0] - 1
    stride = blocks + GROUP

    key_copy = pltpu.make_async_copy(key_wide, key_s, sem_k.at[0])
    val_copy = pltpu.make_async_copy(cache.at[:, pl.ds(HEAD, HEAD)], val_s, sem_k.at[1])
    if pieces:
        x_copies, tab_copies = [], []
        for i in range(pieces):
            span = pl.ds(i * rows, rows)
            place = pl.ds(pl.multiple_of(ids[i] * TILE, TILE), rows)
            x_copies.append(pltpu.make_async_copy(xs[i], x_s.at[span], sem_in.at[i]))
            tab_copies.append(pltpu.make_async_copy(cos_tab.at[place], cos_s.at[span], sem_tab.at[2 * i]))
            tab_copies.append(pltpu.make_async_copy(sin_tab.at[place], sin_s.at[span], sem_tab.at[2 * i + 1]))
        for copy in x_copies:
            copy.start()
        w_copies = [
            pltpu.make_async_copy(wq.at[:, pl.ds(c, 256)], wq_s.at[:, pl.ds(c, 256)], sem_w.at[j])
            for j, c in enumerate(range(0, width, 256))
        ]
        w_copies.append(pltpu.make_async_copy(wkv, wkv_s, sem_w.at[len(w_copies)]))
        for copy in w_copies:
            copy.start()
        for copy in tab_copies:
            copy.start()
    count = ids[2]

    def load_cache():
        @pl.when(count > 0)
        def _():
            key_copy.start()
            val_copy.start()

    if not pieces:
        load_cache()
    else:
        gains = gain[...]
        for i in range(pieces):
            x_copies[i].wait()

        def norm_rows(r, carry):
            span = pl.ds(pl.multiple_of(r * 16, 16), 16)
            values = x_s[span, :].astype(jnp.float32)
            mean_square = jnp.mean(values * values, axis=-1, keepdims=True)
            xn_s[span, :] = (values * lax.rsqrt(mean_square + EPS) * gains).astype(jnp.bfloat16)
            return carry

        lax.fori_loop(0, total // 16, norm_rows, 0, unroll=4)
        load_cache()
        for copy in tab_copies:
            copy.wait()
        cosine, sine = cos_s[...], sin_s[...]

        def rotate(v):
            return (v * cosine + pltpu.roll(v, HEAD // 2, 1) * sine).astype(jnp.bfloat16)

        for j, c in enumerate(range(0, width, 256)):
            w_copies[j].wait()
            made = jnp.dot(xn_s[...], wq_s[:, c:c + 256], preferred_element_type=jnp.float32)
            for h in range(2):
                qo_s[c // HEAD + h] = rotate(made[:, h * HEAD:(h + 1) * HEAD])
        w_copies[-1].wait()
        made = jnp.dot(xn_s[...], wkv_s[...], preferred_element_type=jnp.float32)
        kvo_s[:, :HEAD] = rotate(made[:, :HEAD])
        kvo_s[:, HEAD:] = made[:, HEAD:].astype(jnp.bfloat16)
        outs = []
        for i in range(pieces):
            span = pl.ds(i * rows, rows)
            place = pl.ds(pl.multiple_of(ids[i] * TILE, TILE), rows)
            outs.append(pltpu.make_async_copy(qo_s.at[:, span], qb.at[:, place], sem_out.at[2 * i]))
            outs.append(pltpu.make_async_copy(kvo_s.at[span], kvb.at[place], sem_out.at[2 * i + 1]))
        for copy in outs:
            copy.start()
        for copy in outs:
            copy.wait()

    factor = math.log2(math.e) / math.sqrt(HEAD)

    def fetches(i, slot):
        tile = ids[3 + i]
        at = pl.multiple_of(tile * TILE, TILE)
        before = pl.multiple_of(jnp.maximum(tile - 1, 0) * TILE, TILE)
        return [
            pltpu.make_async_copy(qb.at[:, pl.ds(at, TILE)], qt_s.at[slot], sem_tile.at[slot, 0]),
            pltpu.make_async_copy(kvb.at[pl.ds(before, 2 * TILE)], kvt_s.at[slot], sem_tile.at[slot, 1]),
            pltpu.make_async_copy(doc_bias.at[pl.ds(at, TILE)], db_s.at[slot], sem_tile.at[slot, 2]),
            pltpu.make_async_copy(own_bias.at[pl.ds(at, TILE)], ob_s.at[slot], sem_tile.at[slot, 3]),
        ]

    def att_copy(i):
        at = pl.multiple_of(ids[3 + i] * TILE, TILE)
        return pltpu.make_async_copy(at_s, att.at[pl.ds(at, TILE)], sem_att)

    @pl.when(count > 0)
    def _():
        for copy in fetches(0, 0):
            copy.start()
        key_copy.wait()
        val_copy.wait()

    contract_last = (((1,), (1,)), ((), ()))

    def one_tile(i, carry):
        slot = lax.rem(i, 2)

        @pl.when(i + 1 < count)
        def _():
            for copy in fetches(i + 1, 1 - slot):
                copy.start()

        for copy in fetches(i, slot):
            copy.wait()
        tile = ids[3 + i]
        needed = lists[tile * stride]
        for h in range(heads):
            wide_s[h * TILE:(h + 1) * TILE, :HEAD] = qt_s[slot, h]
            wide_s[h * TILE:(h + 1) * TILE, HEAD:] = db_s[slot]
        own = lax.dot_general(
            wide_s[:, :HEAD], kvt_s[slot, :, :HEAD], contract_last, preferred_element_type=jnp.float32
        )
        own = (own.reshape(heads, TILE, HEAD) + ob_s[slot][None]).reshape(heads * TILE, HEAD)
        own_s[...] = own

        def attend(count):
            blocks_here = [lists[tile * stride + 1 + j] for j in range(count)]
            top = own_s[...]
            for j, block in enumerate(blocks_here):
                scores = jnp.dot(wide_s[...], key_s[block], preferred_element_type=jnp.float32)
                sc_s[j] = scores
                top = jnp.maximum(top, jnp.maximum(scores[:, :HEAD], scores[:, HEAD:]))
            top = jnp.max(top, axis=1, keepdims=True) * factor
            weights = jnp.exp2(own_s[...] * factor - top)
            sums = weights
            made = jnp.dot(weights.astype(jnp.bfloat16), kvt_s[slot, :, HEAD:], preferred_element_type=jnp.float32)
            for j, block in enumerate(blocks_here):
                at = pl.multiple_of(jnp.minimum(block, blocks - 1) * KEY_BLOCK, KEY_BLOCK)
                weights = jnp.exp2(sc_s[j] * factor - top)
                sums = sums + (weights[:, :HEAD] + weights[:, HEAD:])
                made = made + jnp.dot(
                    weights.astype(jnp.bfloat16), val_s[pl.ds(at, KEY_BLOCK), :], preferred_element_type=jnp.float32
                )
            o_s[...] = (made / jnp.sum(sums, axis=1, keepdims=True)).astype(jnp.bfloat16)

        for groups in range(1, blocks // GROUP + 1):

            @pl.when(needed == groups)
            def _(groups=groups):
                attend(groups * GROUP)

        @pl.when(i > 0)
        def _():
            att_copy(i - 1).wait()

        for h in range(heads):
            at_s[:, h * HEAD:(h + 1) * HEAD] = o_s[h * TILE:(h + 1) * TILE]
        att_copy(i).start()
        return carry

    lax.fori_loop(0, count, one_tile, 0)

    @pl.when(count > 0)
    def _():
        att_copy(count - 1).wait()


def run_step(ids, lists, xs, fixed, state, dims):
    tokens, heads, prefix, depth = dims
    pieces = len(xs)
    rows = xs[0].shape[0] if pieces else TILE
    total = max(pieces * rows, 16)
    width = heads * HEAD
    any_spec = pl.BlockSpec(memory_space=pl.ANY)
    vmem_spec = pl.BlockSpec(memory_space=pltpu.VMEM)
    operands = list(xs) + list(fixed)
    specs = [any_spec] * pieces + [vmem_spec] + [any_spec] * (len(fixed) - 1)
    aliases = {}
    if state is not None:
        aliases = {2 + len(operands) + i: i for i in range(3)}
        operands += list(state)
        specs += [any_spec] * 3
    out_shape = [
        jax.ShapeDtypeStruct((heads, tokens, HEAD), jnp.bfloat16),
        jax.ShapeDtypeStruct((tokens, 2 * HEAD), jnp.bfloat16),
        jax.ShapeDtypeStruct((tokens, width), jnp.bfloat16),
    ]
    small = 16
    w_rows = depth if pieces else small
    scratch = [
        pltpu.VMEM((total, depth), jnp.bfloat16),
        pltpu.VMEM((total, depth), jnp.bfloat16),
        pltpu.VMEM((w_rows, width), jnp.bfloat16),
        pltpu.VMEM((w_rows, 2 * HEAD), jnp.bfloat16),
        pltpu.VMEM((total, HEAD), jnp.float32),
        pltpu.VMEM((total, HEAD), jnp.float32),
        pltpu.VMEM((heads, total, HEAD), jnp.bfloat16),
        pltpu.VMEM((total, 2 * HEAD), jnp.bfloat16),
        pltpu.VMEM((prefix // KEY_BLOCK + 1, 2 * HEAD, KEY_BLOCK), jnp.bfloat16),
        pltpu.VMEM((prefix, HEAD), jnp.bfloat16),
        pltpu.VMEM((2, heads, TILE, HEAD), jnp.bfloat16),
        pltpu.VMEM((2, 2 * TILE, 2 * HEAD), jnp.bfloat16),
        pltpu.VMEM((2, TILE, HEAD), jnp.bfloat16),
        pltpu.VMEM((2, TILE, HEAD), jnp.float32),
        pltpu.VMEM((prefix // KEY_BLOCK, heads * TILE, KEY_BLOCK), jnp.float32),
        pltpu.VMEM((TILE, width), jnp.bfloat16),
        pltpu.VMEM((heads * TILE, 2 * HEAD), jnp.bfloat16),
        pltpu.VMEM((heads * TILE, HEAD), jnp.float32),
        pltpu.VMEM((heads * TILE, HEAD), jnp.bfloat16),
        pltpu.SemaphoreType.DMA((max(pieces, 1),)),
        pltpu.SemaphoreType.DMA((2 * max(pieces, 1),)),
        pltpu.SemaphoreType.DMA((width // 256 + 1,)),
        pltpu.SemaphoreType.DMA((2,)),
        pltpu.SemaphoreType.DMA((2 * max(pieces, 1),)),
        pltpu.SemaphoreType.DMA((2, 4)),
        pltpu.SemaphoreType.DMA,
    ]
    return pl.pallas_call(
        functools.partial(step_kernel, pieces, rows, heads),
        grid_spec=pltpu.PrefetchScalarGridSpec(
            num_scalar_prefetch=2,
            grid=(),
            in_specs=specs,
            out_specs=[any_spec] * 3,
            scratch_shapes=scratch,
        ),
        out_shape=out_shape,
        input_output_aliases=aliases,
        compiler_params=pltpu.CompilerParams(vmem_limit_bytes=VMEM_LIMIT),
        cost_estimate=pl.CostEstimate(flops=1 << 20, bytes_accessed=1 << 16, transcendentals=0),
    )(ids, lists, *operands)


def product_kernel(count, ids, *refs):
    parts, weights, outs = refs[:count], refs[count], refs[count + 1:]
    rows = jnp.concatenate([part[...] for part in parts], axis=0)
    made = jnp.dot(rows, weights[...], preferred_element_type=jnp.float32).astype(jnp.bfloat16)
    for i in range(count):
        outs[i][...] = made[i * TILE:(i + 1) * TILE]


def product(ids, count, att, w_out):
    width, columns = w_out.shape
    block = 1024
    row_block = pl.BlockSpec((TILE, block), lambda b, ids: (0, b))
    in_specs = [pl.BlockSpec((TILE, width), lambda b, ids, i=i: (ids[i], 0)) for i in range(count)]
    in_specs.append(pl.BlockSpec((width, block), lambda b, ids: (0, b)))
    return pl.pallas_call(
        functools.partial(product_kernel, count),
        grid_spec=pltpu.PrefetchScalarGridSpec(
            num_scalar_prefetch=1, grid=(columns // block,), in_specs=in_specs, out_specs=[row_block] * count
        ),
        out_shape=[jax.ShapeDtypeStruct((TILE, columns), jnp.bfloat16)] * count,
        compiler_params=pltpu.CompilerParams(vmem_limit_bytes=VMEM_LIMIT),
        cost_estimate=pl.CostEstimate(flops=1 << 20, bytes_accessed=1 << 16, transcendentals=0),
    )(ids, *[att] * count, w_out)


def tables(seg_ids, seg_doc, doc_lens, prefix, cache):
    tokens = seg_ids.shape[0]
    tiles = tokens // TILE
    blocks = prefix // KEY_BLOCK
    docs = doc_lens.shape[0]
    order = jnp.arange(tokens, dtype=jnp.int32)
    start = jnp.sum((seg_ids[None, :] < seg_ids[:, None]).astype(jnp.int32), axis=1, dtype=jnp.int32)
    positions = prefix + order - start
    segments = jnp.arange(seg_doc.shape[0], dtype=jnp.int32)
    tok_doc = jnp.sum(
        jnp.where(seg_ids[:, None] == segments[None, :], seg_doc[None, :], 0), axis=1, dtype=jnp.int32
    )
    doc_list = jnp.arange(docs, dtype=jnp.int32)
    doc_ends = jnp.sum(jnp.where(doc_list[None, :] <= doc_list[:, None], doc_lens[None, :], 0), axis=1)
    doc_starts = doc_ends - doc_lens
    lanes = jnp.arange(HEAD, dtype=jnp.int32)
    half = HEAD // 2
    inverse = ROPE_THETA ** (-(jnp.arange(half, dtype=jnp.float32) * 2.0 / HEAD))
    inverse = jnp.concatenate([inverse, inverse])
    angles = positions.astype(jnp.float32)[:, None] * inverse[None, :]
    cosine = jnp.cos(angles)
    sine = jnp.sin(angles) * jnp.where(lanes < half, -1.0, 1.0)[None, :]
    doc_bias = jnp.where(lanes[None, :] == tok_doc[:, None], 0.0, MASKED).astype(jnp.bfloat16)
    spot = jnp.arange(prefix + KEY_BLOCK, dtype=jnp.int32).reshape(blocks + 1, 1, KEY_BLOCK)
    low = jnp.pad(doc_starts, (0, HEAD - docs), constant_values=prefix).reshape(1, HEAD, 1)
    high = jnp.pad(doc_ends, (0, HEAD - docs), constant_values=prefix + KEY_BLOCK).reshape(1, HEAD, 1)
    one_hot = ((spot >= low) & (spot < high)).astype(jnp.bfloat16)
    by_block = cache[:, :HEAD].reshape(blocks, KEY_BLOCK, HEAD).transpose(0, 2, 1)
    key_wide = jnp.concatenate([jnp.pad(by_block, ((0, 1), (0, 0), (0, 0))), one_hot], axis=1)
    first_key = jnp.maximum(jnp.arange(tiles, dtype=jnp.int32) - 1, 0) * TILE
    spots = first_key[:, None] + lanes[None, :]
    by_tile = seg_ids.reshape(tiles, TILE)
    earlier = jnp.concatenate([by_tile[:1], by_tile[:-1]], axis=0)
    later = jnp.concatenate([by_tile[1:2], by_tile[1:]], axis=0)
    window_seg = jnp.concatenate([earlier, later], axis=1)
    ok = (window_seg[:, None, :] == by_tile[:, :, None]) & (
        spots[:, None, :] <= order.reshape(tiles, TILE)[:, :, None]
    )
    own_bias = jnp.where(ok, 0.0, MASKED).astype(jnp.float32).reshape(tokens, HEAD)
    present = jnp.any(tok_doc.reshape(tiles, TILE)[:, :, None] == doc_list[None, None, :], axis=1)
    edge = jnp.arange(blocks, dtype=jnp.int32) * KEY_BLOCK
    overlap = (doc_starts[:, None] < edge[None, :] + KEY_BLOCK) & (doc_ends[:, None] > edge[None, :])
    flags = jnp.any(present[:, :, None] & overlap[None, :, :], axis=1).astype(jnp.int32)
    block_ids = jnp.arange(blocks, dtype=jnp.int32)
    rank = jnp.sum(jnp.where(block_ids[None, :, None] > block_ids[None, None, :], flags[:, None, :], 0), axis=2)
    listed = jnp.sum(
        jnp.where((rank[:, :, None] == block_ids[None, None, :]) & (flags[:, :, None] > 0), block_ids[None, :, None], 0),
        axis=1,
    )
    count = jnp.sum(flags, axis=1, keepdims=True)
    listed = jnp.where(block_ids[None, :] < count, listed, blocks)
    groups = (count + GROUP - 1) // GROUP
    lists = jnp.pad(jnp.concatenate([groups, listed], axis=1), ((0, 0), (0, GROUP - 1)))
    lists = lists.astype(jnp.int32).reshape(-1)
    return cosine, sine, key_wide, doc_bias, own_bias, lists


def local(
    hidden_in, norm_gain, w_query, keyvalue_weight, w_out, prefix_keyvalue_cache, seg_ids, seg_doc, doc_lens
):
    size = lax.axis_size("tensor")
    tokens = seg_ids.shape[0]
    prefix = prefix_keyvalue_cache.shape[0]
    chunk_rows, depth = hidden_in.shape
    heads = w_query.shape[1] // HEAD
    order = ring_order(size)
    half = size // 2
    rank = lax.axis_index("tensor")

    forward_pairs = [(order[i], order[(i + 1) % size]) for i in range(size)]
    backward_pairs = [(b, a) for a, b in forward_pairs]

    def forward(x):
        return lax.ppermute(x, "tensor", forward_pairs)

    def backward(x):
        return lax.ppermute(x, "tensor", backward_pairs)

    if keyvalue_weight.shape[1] == HEAD:
        swap = [(i, i ^ 1) for i in range(size)]
        even = rank % 2 == 0
        other_weight, other_cache = lax.ppermute((keyvalue_weight, prefix_keyvalue_cache), "tensor", swap)
        keyvalue_weight = jnp.concatenate(
            [jnp.where(even, keyvalue_weight, other_weight), jnp.where(even, other_weight, keyvalue_weight)], axis=1
        )
        prefix_keyvalue_cache = jnp.concatenate(
            [
                jnp.where(even, prefix_keyvalue_cache, other_cache),
                jnp.where(even, other_cache, prefix_keyvalue_cache),
            ],
            axis=1,
        )

    place = {r: i for i, r in enumerate(order)}
    flips = np.zeros((size,), np.int32)
    for r in range(size):
        flips[r] = int(order[(place[r] - 1) % size] == r - 1)
    sends = np.zeros((size, half + 1, 6), np.int32)
    early_halves = []
    for r in range(size):
        for d in range(half + 1):
            ahead, back = order[(place[r] + d) % size], order[(place[r] - d) % size]
            late = [2 * ahead + flips[ahead], 2 * back + 1 - flips[back]]
            sends[r, d] = late + [2 * ahead + 1 - flips[ahead], 2 * back + flips[back], 2 * r, 2 * r + 1]
        early_halves.append({(int(i) // 2, int(i) % 2) for i in sends[r, half - 1, 2:4]})
    tiles = tile_plan(order, early_halves)
    most = max(len(call) for calls in tiles for call in calls)
    plan = np.zeros((size, size, 3 + most), np.int32)
    for r in range(size):
        for call in range(size):
            d = min(call, half - 1) if call <= half else half
            back, ahead = 2 * order[(place[r] - d) % size], 2 * order[(place[r] + d) % size]
            if call == half - 1 or call == half + 1:
                ahead += 1
            elif call == half:
                back += 1
            row = [back, ahead, len(tiles[r][call])] + tiles[r][call]
            plan[r, call, :len(row)] = row
    my_plan = jnp.asarray(plan)[rank]
    my_sends = jnp.asarray(sends)[rank]
    flipped = jnp.asarray(flips)[rank] > 0

    cosine, sine, key_wide, doc_bias, own_bias, lists = tables(
        seg_ids, seg_doc, doc_lens, prefix, prefix_keyvalue_cache
    )
    gain = norm_gain.astype(jnp.float32).reshape(1, depth)
    fixed = (gain, w_query, keyvalue_weight, cosine, sine, key_wide, prefix_keyvalue_cache, doc_bias, own_bias)
    dims = (tokens, heads, prefix, depth)

    def pass_on(pair):
        return forward(pair[0]), backward(pair[1])

    def add(pair, arrived):
        return tuple((a.astype(jnp.float32) + b.astype(jnp.float32)).astype(jnp.bfloat16) for a, b in zip(pair, arrived))

    def step(call, parts, state):
        return tuple(run_step(my_plan[call], lists, parts, fixed, state, dims))

    held = pass_on((hidden_in, hidden_in))
    state = step(0, [hidden_in], None)
    for distance in range(1, half - 1):
        held, state = lax.optimization_barrier((held, state))
        if distance < half - 2:
            following = pass_on(held)
        else:
            following = pass_on((held[0][:TILE], held[1][TILE:])), pass_on((held[0][TILE:], held[1][:TILE]))
        state = step(distance, held, state)
        held = following
    first, second = held
    first, state = lax.optimization_barrier((first, state))
    last = pass_on(first)
    state = step(half - 1, first, state)
    second, state = lax.optimization_barrier((second, state))
    state = step(half, second, state)

    made = tuple(product(my_sends[half - 1, 2:4], 2, state[2], w_out))
    made, last, state = lax.optimization_barrier((made, last, state))
    early = pass_on(made)
    state = step(half + 1, last, state)
    terms = product(jnp.concatenate([my_sends[half, :2], my_sends[half - 1, :2]]), 4, state[2], w_out)
    made, late = tuple(terms[:2]), tuple(terms[2:])
    far = pass_on(made)
    for distance in range(half - 1, 0, -1):
        if distance > 1:
            made, state = lax.optimization_barrier((made, state))
            state = step(size - distance + 1, [], state)
            near = distance - 1
            terms = tuple(product(my_sends[near], 4, state[2], w_out))
            early, terms = lax.optimization_barrier((early, terms))
            made = add(terms[2:], early)
            early = pass_on(made)
            if near == 1:
                made, state = lax.optimization_barrier((made, state))
                own = tuple(product(my_sends[near, 4:], 2, state[2], w_out))
                far, own = lax.optimization_barrier((far, own))
            else:
                made, far = lax.optimization_barrier((made, far))
            made = add(late, far)
            late = terms[:2]
        else:
            early, far = lax.optimization_barrier((early, far))
            made = add(late, far)
        far = pass_on(made)
    wide = [[part.astype(jnp.float32) for part in pair] for pair in (early, far)]
    with_far, with_early = wide[1][0] + wide[0][1], wide[0][0] + wide[1][1]
    halves = [jnp.where(flipped, with_early, with_far), jnp.where(flipped, with_far, with_early)]
    summed = jnp.concatenate([halves[i] + own[i].astype(jnp.float32) for i in range(2)], axis=0)
    return (hidden_in.astype(jnp.float32) + summed).astype(jnp.bfloat16)


def solution(mesh):
    return jax.shard_map(
        local,
        mesh=mesh,
        in_specs=(
            P(("dp", "tensor"), None),
            P(),
            P(None, "tensor"),
            P(None, "tensor"),
            P("tensor", None),
            P(None, "tensor"),
            P("dp"),
            P("dp"),
            P(),
        ),
        out_specs=P(("dp", "tensor"), None),
        check_vma=False,
    )
```

```python
import functools
import math

import jax
import jax.numpy as jnp
import numpy as np
from jax import lax
from jax.experimental import pallas as pl
from jax.experimental.pallas import tpu as pltpu
from jax.sharding import PartitionSpec as P

HEAD = 128
TILE = 64
KEY_BLOCK = 256
GROUP = 4
DEPTH_CHUNKS = 4
COLUMN_CHUNKS = 4
MASKED = -1e30
EPS = 1e-05
ROPE_THETA = 500000.0
VMEM_LIMIT = 48 * 1024 * 1024


def ring_order(size):
    zs = 4 if size % 8 == 0 else 1
    ys = size // zs
    if zs == 1:
        return list(range(size))
    cycle = [(0, 0)]
    for y in range(ys):
        column = range(1, zs) if y % 2 == 0 else range(zs - 1, 0, -1)
        cycle += [(z, y) for z in column]
    cycle += [(0, y) for y in range(ys - 1, 0, -1)]
    return [z * ys + y for z, y in cycle]


def tile_plan(order, early_halves):
    size = len(order)
    half = size // 2
    place = {r: i for i, r in enumerate(order)}
    spare = [0] + [4] * (half - 2) + [2] + [0] * (size - half)
    plans = []
    for rank in range(size):
        arrival, due = {}, {}
        for chunk in range(size):
            behind = (place[rank] - place[chunk]) % size
            distance = min(behind, size - behind)
            for upper in range(2):
                if distance == half:
                    arrival[chunk, upper] = due[chunk, upper] = half + 1
                elif distance == half - 1:
                    arrival[chunk, upper] = half - 1 if upper == int(behind != distance) else half
                    due[chunk, upper] = half if (chunk, upper) in early_halves[rank] else half + 1
                else:
                    arrival[chunk, upper] = distance
                    due[chunk, upper] = size - max(distance, 1)
        ready = {}
        for chunk in range(size):
            both = max(arrival[chunk, 0], arrival[chunk, 1])
            ready[chunk, 1] = both
            ready[chunk, 0] = max(arrival[chunk, 0], arrival[chunk - 1, 1]) if chunk else both
        calls, left = [], set(ready)
        for call in range(size):
            able = sorted((due[t], t) for t in left if ready[t] <= call)
            must = [t for when, t in able if when <= call]
            more = [t for when, t in able if when > call][:max(spare[call] - len(must), 0)]
            calls.append([2 * chunk + upper for chunk, upper in must + more])
            left -= set(must + more)
        assert not left and all(ready[t] <= due[t] for t in ready)
        plans.append(calls)
    return plans


def step_kernel(pieces, rows, heads, *refs):
    total = pieces * rows
    width = heads * HEAD
    it = iter(refs)
    ids, lists = next(it), next(it)
    xs = [next(it) for _ in range(pieces)]
    gain, wq, wkv, cos_tab, sin_tab, key_wide, cache, doc_bias, own_bias = [next(it) for _ in range(9)]
    first = pieces == 1 and rows == 128
    if not first:
        next(it), next(it), next(it)
    qb, kvb, att = next(it), next(it), next(it)
    (x_s, xn_s, w_s, cos_s, sin_s, qo_s, kvo_s, key_s, val_s, qt_s, kvt_s, db_s, ob_s, sc_s, at_s,
     wide_s, own_s, o_s, sem_in, sem_tab, sem_w, sem_k, sem_out, sem_tile, sem_att) = list(it)
    deep = wq.shape[0] // DEPTH_CHUNKS
    blocks = key_wide.shape[0] - 1
    stride = blocks + GROUP

    key_copy = pltpu.make_async_copy(key_wide, key_s, sem_k.at[0])
    val_copy = pltpu.make_async_copy(cache.at[:, pl.ds(HEAD, HEAD)], val_s, sem_k.at[1])
    if pieces:
        x_copies, tab_copies = [], []
        for i in range(pieces):
            span = pl.ds(i * rows, rows)
            place = pl.ds(pl.multiple_of(ids[i] * TILE, TILE), rows)
            x_copies.append(pltpu.make_async_copy(xs[i], x_s.at[span], sem_in.at[i]))
            tab_copies.append(pltpu.make_async_copy(cos_tab.at[place], cos_s.at[span], sem_tab.at[2 * i]))
            tab_copies.append(pltpu.make_async_copy(sin_tab.at[place], sin_s.at[span], sem_tab.at[2 * i + 1]))
        for copy in x_copies:
            copy.start()
        w_copies = []
        for j in range(DEPTH_CHUNKS):
            span = pl.ds(j * deep, deep)
            w_copies.append(pltpu.make_async_copy(wq.at[span], w_s.at[span, pl.ds(0, width)], sem_w.at[2 * j]))
            w_copies.append(
                pltpu.make_async_copy(wkv.at[span], w_s.at[span, pl.ds(width, 2 * HEAD)], sem_w.at[2 * j + 1])
            )
        for copy in w_copies:
            copy.start()
        for copy in tab_copies:
            copy.start()
    count = ids[2]

    def load_cache():
        @pl.when(count > 0)
        def _():
            key_copy.start()
            val_copy.start()

    if not pieces:
        load_cache()
    else:
        gains = gain[...]
        for i in range(pieces):
            x_copies[i].wait()

        def norm_rows(r, carry):
            span = pl.ds(pl.multiple_of(r * 16, 16), 16)
            values = x_s[span, :].astype(jnp.float32)
            mean_square = jnp.mean(values * values, axis=-1, keepdims=True)
            xn_s[span, :] = (values * lax.rsqrt(mean_square + EPS) * gains).astype(jnp.bfloat16)
            return carry

        lax.fori_loop(0, total // 16, norm_rows, 0, unroll=4)
        load_cache()
        for copy in tab_copies:
            copy.wait()
        cosine, sine = cos_s[...], sin_s[...]

        def rotate(v):
            return (v * cosine + pltpu.roll(v, HEAD // 2, 1) * sine).astype(jnp.bfloat16)

        made = None
        for j in range(DEPTH_CHUNKS):
            w_copies[2 * j].wait()
            w_copies[2 * j + 1].wait()
            span = slice(j * deep, (j + 1) * deep)
            more = jnp.dot(xn_s[:, span], w_s[span, :], preferred_element_type=jnp.float32)
            made = more if made is None else made + more
        for h in range(heads):
            qo_s[h] = rotate(made[:, h * HEAD:(h + 1) * HEAD])
        kvo_s[:, :HEAD] = rotate(made[:, width:width + HEAD])
        kvo_s[:, HEAD:] = made[:, width + HEAD:].astype(jnp.bfloat16)
        outs = []
        for i in range(pieces):
            span = pl.ds(i * rows, rows)
            place = pl.ds(pl.multiple_of(ids[i] * TILE, TILE), rows)
            outs.append(pltpu.make_async_copy(qo_s.at[:, span], qb.at[:, place], sem_out.at[2 * i]))
            outs.append(pltpu.make_async_copy(kvo_s.at[span], kvb.at[place], sem_out.at[2 * i + 1]))
        for copy in outs:
            copy.start()
        for copy in outs:
            copy.wait()

    factor = math.log2(math.e) / math.sqrt(HEAD)

    def fetches(i, slot):
        tile = ids[3 + i]
        at = pl.multiple_of(tile * TILE, TILE)
        before = pl.multiple_of(jnp.maximum(tile - 1, 0) * TILE, TILE)
        return [
            pltpu.make_async_copy(qb.at[:, pl.ds(at, TILE)], qt_s.at[slot], sem_tile.at[slot, 0]),
            pltpu.make_async_copy(kvb.at[pl.ds(before, 2 * TILE)], kvt_s.at[slot], sem_tile.at[slot, 1]),
            pltpu.make_async_copy(doc_bias.at[pl.ds(at, TILE)], db_s.at[slot], sem_tile.at[slot, 2]),
            pltpu.make_async_copy(own_bias.at[pl.ds(at, TILE)], ob_s.at[slot], sem_tile.at[slot, 3]),
        ]

    def att_copy(i):
        at = pl.multiple_of(ids[3 + i] * TILE, TILE)
        return pltpu.make_async_copy(at_s, att.at[pl.ds(at, TILE)], sem_att)

    @pl.when(count > 0)
    def _():
        for copy in fetches(0, 0):
            copy.start()
        key_copy.wait()
        val_copy.wait()

    contract_last = (((1,), (1,)), ((), ()))

    def one_tile(i, carry):
        slot = lax.rem(i, 2)

        @pl.when(i + 1 < count)
        def _():
            for copy in fetches(i + 1, 1 - slot):
                copy.start()

        for copy in fetches(i, slot):
            copy.wait()
        tile = ids[3 + i]
        needed = lists[tile * stride]
        for h in range(heads):
            wide_s[h * TILE:(h + 1) * TILE, :HEAD] = qt_s[slot, h]
            wide_s[h * TILE:(h + 1) * TILE, HEAD:] = db_s[slot]
        own = lax.dot_general(
            wide_s[:, :HEAD], kvt_s[slot, :, :HEAD], contract_last, preferred_element_type=jnp.float32
        )
        own = (own.reshape(heads, TILE, HEAD) + ob_s[slot][None]).reshape(heads * TILE, HEAD)
        own_s[...] = own

        def attend(groups):
            listed = [lists[tile * stride + 1 + j] for j in range(groups * GROUP)]
            top = own_s[...]
            for g in range(groups):
                keys = jnp.concatenate([key_s[block] for block in listed[g * GROUP:(g + 1) * GROUP]], axis=1)
                scores = jnp.dot(wide_s[...], keys, preferred_element_type=jnp.float32)
                sc_s[g] = scores
                for c in range(0, GROUP * KEY_BLOCK, HEAD):
                    top = jnp.maximum(top, scores[:, c:c + HEAD])
            top = jnp.max(top, axis=1, keepdims=True) * factor
            weights = jnp.exp2(own_s[...] * factor - top)
            sums = weights
            made = [jnp.dot(weights.astype(jnp.bfloat16), kvt_s[slot, :, HEAD:], preferred_element_type=jnp.float32)]
            made += [None] * (GROUP - 1)
            for j, block in enumerate(listed):
                at = pl.multiple_of(jnp.minimum(block, blocks - 1) * KEY_BLOCK, KEY_BLOCK)
                c = j % GROUP * KEY_BLOCK
                weights = jnp.exp2(sc_s[j // GROUP, :, c:c + KEY_BLOCK] * factor - top)
                sums = sums + (weights[:, :HEAD] + weights[:, HEAD:])
                more = jnp.dot(
                    weights.astype(jnp.bfloat16), val_s[pl.ds(at, KEY_BLOCK), :], preferred_element_type=jnp.float32
                )
                made[j % GROUP] = more if made[j % GROUP] is None else made[j % GROUP] + more
            made = (made[0] + made[1]) + (made[2] + made[3])
            o_s[...] = (made / jnp.sum(sums, axis=1, keepdims=True)).astype(jnp.bfloat16)

        for groups in range(1, blocks // GROUP + 1):

            @pl.when(needed == groups)
            def _(groups=groups):
                attend(groups)

        @pl.when(i > 0)
        def _():
            att_copy(i - 1).wait()

        for h in range(heads):
            at_s[:, h * HEAD:(h + 1) * HEAD] = o_s[h * TILE:(h + 1) * TILE]
        att_copy(i).start()
        return carry

    lax.fori_loop(0, count, one_tile, 0)

    @pl.when(count > 0)
    def _():
        att_copy(count - 1).wait()


def run_step(ids, lists, xs, fixed, state, dims):
    tokens, heads, prefix, depth = dims
    pieces = len(xs)
    rows = xs[0].shape[0] if pieces else TILE
    total = max(pieces * rows, 16)
    width = heads * HEAD
    any_spec = pl.BlockSpec(memory_space=pl.ANY)
    vmem_spec = pl.BlockSpec(memory_space=pltpu.VMEM)
    operands = list(xs) + list(fixed)
    specs = [any_spec] * pieces + [vmem_spec] + [any_spec] * (len(fixed) - 1)
    aliases = {}
    if state is not None:
        aliases = {2 + len(operands) + i: i for i in range(3)}
        operands += list(state)
        specs += [any_spec] * 3
    out_shape = [
        jax.ShapeDtypeStruct((heads, tokens, HEAD), jnp.bfloat16),
        jax.ShapeDtypeStruct((tokens, 2 * HEAD), jnp.bfloat16),
        jax.ShapeDtypeStruct((tokens, width), jnp.bfloat16),
    ]
    small = 16
    w_rows = depth if pieces else small
    scratch = [
        pltpu.VMEM((total, depth), jnp.bfloat16),
        pltpu.VMEM((total, depth), jnp.bfloat16),
        pltpu.VMEM((w_rows, width + 2 * HEAD), jnp.bfloat16),
        pltpu.VMEM((total, HEAD), jnp.float32),
        pltpu.VMEM((total, HEAD), jnp.float32),
        pltpu.VMEM((heads, total, HEAD), jnp.bfloat16),
        pltpu.VMEM((total, 2 * HEAD), jnp.bfloat16),
        pltpu.VMEM((prefix // KEY_BLOCK + 1, 2 * HEAD, KEY_BLOCK), jnp.bfloat16),
        pltpu.VMEM((prefix, HEAD), jnp.bfloat16),
        pltpu.VMEM((2, heads, TILE, HEAD), jnp.bfloat16),
        pltpu.VMEM((2, 2 * TILE, 2 * HEAD), jnp.bfloat16),
        pltpu.VMEM((2, TILE, HEAD), jnp.bfloat16),
        pltpu.VMEM((2, TILE, HEAD), jnp.float32),
        pltpu.VMEM((prefix // KEY_BLOCK // GROUP, heads * TILE, GROUP * KEY_BLOCK), jnp.float32),
        pltpu.VMEM((TILE, width), jnp.bfloat16),
        pltpu.VMEM((heads * TILE, 2 * HEAD), jnp.bfloat16),
        pltpu.VMEM((heads * TILE, HEAD), jnp.float32),
        pltpu.VMEM((heads * TILE, HEAD), jnp.bfloat16),
        pltpu.SemaphoreType.DMA((max(pieces, 1),)),
        pltpu.SemaphoreType.DMA((2 * max(pieces, 1),)),
        pltpu.SemaphoreType.DMA((2 * DEPTH_CHUNKS,)),
        pltpu.SemaphoreType.DMA((2,)),
        pltpu.SemaphoreType.DMA((2 * max(pieces, 1),)),
        pltpu.SemaphoreType.DMA((2, 4)),
        pltpu.SemaphoreType.DMA,
    ]
    return pl.pallas_call(
        functools.partial(step_kernel, pieces, rows, heads),
        grid_spec=pltpu.PrefetchScalarGridSpec(
            num_scalar_prefetch=2,
            grid=(),
            in_specs=specs,
            out_specs=[any_spec] * 3,
            scratch_shapes=scratch,
        ),
        out_shape=out_shape,
        input_output_aliases=aliases,
        compiler_params=pltpu.CompilerParams(vmem_limit_bytes=VMEM_LIMIT),
        cost_estimate=pl.CostEstimate(flops=1 << 20, bytes_accessed=1 << 16, transcendentals=0),
    )(ids, lists, *operands)


def product_kernel(count, ids, att, w_out, *refs):
    outs = refs[:count]
    rows_s, w_s, made_s, sem_rows, sem_w, sem_out = refs[count:]
    columns = w_out.shape[1] // COLUMN_CHUNKS
    row_copies = [
        pltpu.make_async_copy(
            att.at[pl.ds(pl.multiple_of(ids[i] * TILE, TILE), TILE)], rows_s.at[pl.ds(i * TILE, TILE)], sem_rows.at[i]
        )
        for i in range(count)
    ]
    spans = [pl.ds(c * columns, columns) for c in range(COLUMN_CHUNKS)]
    w_copies = [pltpu.make_async_copy(w_out.at[:, span], w_s.at[:, span], sem_w.at[c]) for c, span in enumerate(spans)]
    for copy in row_copies + w_copies:
        copy.start()
    for copy in row_copies:
        copy.wait()
    out_copies = []
    for c, span in enumerate(spans):
        w_copies[c].wait()
        made = jnp.dot(rows_s[...], w_s[:, span], preferred_element_type=jnp.float32)
        made_s[:, span] = made.astype(jnp.bfloat16)
        for i in range(count):
            copy = pltpu.make_async_copy(
                made_s.at[pl.ds(i * TILE, TILE), span], outs[i].at[:, span], sem_out.at[i, c]
            )
            copy.start()
            out_copies.append(copy)
    for copy in out_copies:
        copy.wait()


def product(ids, count, att, w_out):
    width, columns = w_out.shape
    any_spec = pl.BlockSpec(memory_space=pl.ANY)
    return pl.pallas_call(
        functools.partial(product_kernel, count),
        grid_spec=pltpu.PrefetchScalarGridSpec(
            num_scalar_prefetch=1,
            grid=(),
            in_specs=[any_spec] * 2,
            out_specs=[any_spec] * count,
            scratch_shapes=[
                pltpu.VMEM((count * TILE, width), jnp.bfloat16),
                pltpu.VMEM((width, columns), jnp.bfloat16),
                pltpu.VMEM((count * TILE, columns), jnp.bfloat16),
                pltpu.SemaphoreType.DMA((count,)),
                pltpu.SemaphoreType.DMA((COLUMN_CHUNKS,)),
                pltpu.SemaphoreType.DMA((count, COLUMN_CHUNKS)),
            ],
        ),
        out_shape=[jax.ShapeDtypeStruct((TILE, columns), jnp.bfloat16)] * count,
        compiler_params=pltpu.CompilerParams(vmem_limit_bytes=VMEM_LIMIT),
        cost_estimate=pl.CostEstimate(flops=1 << 20, bytes_accessed=1 << 16, transcendentals=0),
    )(ids, att, w_out)


def tables(seg_ids, seg_doc, doc_lens, prefix, cache):
    tokens = seg_ids.shape[0]
    tiles = tokens // TILE
    blocks = prefix // KEY_BLOCK
    docs = doc_lens.shape[0]
    order = jnp.arange(tokens, dtype=jnp.int32)
    start = jnp.sum((seg_ids[None, :] < seg_ids[:, None]).astype(jnp.int32), axis=1, dtype=jnp.int32)
    positions = prefix + order - start
    segments = jnp.arange(seg_doc.shape[0], dtype=jnp.int32)
    tok_doc = jnp.sum(
        jnp.where(seg_ids[:, None] == segments[None, :], seg_doc[None, :], 0), axis=1, dtype=jnp.int32
    )
    doc_list = jnp.arange(docs, dtype=jnp.int32)
    doc_ends = jnp.sum(jnp.where(doc_list[None, :] <= doc_list[:, None], doc_lens[None, :], 0), axis=1)
    doc_starts = doc_ends - doc_lens
    lanes = jnp.arange(HEAD, dtype=jnp.int32)
    half = HEAD // 2
    inverse = ROPE_THETA ** (-(jnp.arange(half, dtype=jnp.float32) * 2.0 / HEAD))
    inverse = jnp.concatenate([inverse, inverse])
    angles = positions.astype(jnp.float32)[:, None] * inverse[None, :]
    cosine = jnp.cos(angles)
    sine = jnp.sin(angles) * jnp.where(lanes < half, -1.0, 1.0)[None, :]
    doc_bias = jnp.where(lanes[None, :] == tok_doc[:, None], 0.0, MASKED).astype(jnp.bfloat16)
    spot = jnp.arange(prefix + KEY_BLOCK, dtype=jnp.int32).reshape(blocks + 1, 1, KEY_BLOCK)
    low = jnp.pad(doc_starts, (0, HEAD - docs), constant_values=prefix).reshape(1, HEAD, 1)
    high = jnp.pad(doc_ends, (0, HEAD - docs), constant_values=prefix + KEY_BLOCK).reshape(1, HEAD, 1)
    one_hot = ((spot >= low) & (spot < high)).astype(jnp.bfloat16)
    by_block = cache[:, :HEAD].reshape(blocks, KEY_BLOCK, HEAD).transpose(0, 2, 1)
    key_wide = jnp.concatenate([jnp.pad(by_block, ((0, 1), (0, 0), (0, 0))), one_hot], axis=1)
    first_key = jnp.maximum(jnp.arange(tiles, dtype=jnp.int32) - 1, 0) * TILE
    spots = first_key[:, None] + lanes[None, :]
    by_tile = seg_ids.reshape(tiles, TILE)
    earlier = jnp.concatenate([by_tile[:1], by_tile[:-1]], axis=0)
    later = jnp.concatenate([by_tile[1:2], by_tile[1:]], axis=0)
    window_seg = jnp.concatenate([earlier, later], axis=1)
    ok = (window_seg[:, None, :] == by_tile[:, :, None]) & (
        spots[:, None, :] <= order.reshape(tiles, TILE)[:, :, None]
    )
    own_bias = jnp.where(ok, 0.0, MASKED).astype(jnp.float32).reshape(tokens, HEAD)
    present = jnp.any(tok_doc.reshape(tiles, TILE)[:, :, None] == doc_list[None, None, :], axis=1)
    edge = jnp.arange(blocks, dtype=jnp.int32) * KEY_BLOCK
    overlap = (doc_starts[:, None] < edge[None, :] + KEY_BLOCK) & (doc_ends[:, None] > edge[None, :])
    flags = jnp.any(present[:, :, None] & overlap[None, :, :], axis=1).astype(jnp.int32)
    block_ids = jnp.arange(blocks, dtype=jnp.int32)
    rank = jnp.sum(jnp.where(block_ids[None, :, None] > block_ids[None, None, :], flags[:, None, :], 0), axis=2)
    listed = jnp.sum(
        jnp.where((rank[:, :, None] == block_ids[None, None, :]) & (flags[:, :, None] > 0), block_ids[None, :, None], 0),
        axis=1,
    )
    count = jnp.sum(flags, axis=1, keepdims=True)
    listed = jnp.where(block_ids[None, :] < count, listed, blocks)
    groups = (count + GROUP - 1) // GROUP
    lists = jnp.pad(jnp.concatenate([groups, listed], axis=1), ((0, 0), (0, GROUP - 1)))
    lists = lists.astype(jnp.int32).reshape(-1)
    return cosine, sine, key_wide, doc_bias, own_bias, lists


def local(
    hidden_in, norm_gain, w_query, keyvalue_weight, w_out, prefix_keyvalue_cache, seg_ids, seg_doc, doc_lens
):
    size = lax.axis_size("tensor")
    tokens = seg_ids.shape[0]
    prefix = prefix_keyvalue_cache.shape[0]
    chunk_rows, depth = hidden_in.shape
    heads = w_query.shape[1] // HEAD
    order = ring_order(size)
    half = size // 2
    rank = lax.axis_index("tensor")

    forward_pairs = [(order[i], order[(i + 1) % size]) for i in range(size)]
    backward_pairs = [(b, a) for a, b in forward_pairs]

    def forward(x):
        return lax.ppermute(x, "tensor", forward_pairs)

    def backward(x):
        return lax.ppermute(x, "tensor", backward_pairs)

    if keyvalue_weight.shape[1] == HEAD:
        swap = [(i, i ^ 1) for i in range(size)]
        even = rank % 2 == 0
        other_weight, other_cache = lax.ppermute((keyvalue_weight, prefix_keyvalue_cache), "tensor", swap)
        keyvalue_weight = jnp.concatenate(
            [jnp.where(even, keyvalue_weight, other_weight), jnp.where(even, other_weight, keyvalue_weight)], axis=1
        )
        prefix_keyvalue_cache = jnp.concatenate(
            [
                jnp.where(even, prefix_keyvalue_cache, other_cache),
                jnp.where(even, other_cache, prefix_keyvalue_cache),
            ],
            axis=1,
        )

    place = {r: i for i, r in enumerate(order)}
    flips = np.zeros((size,), np.int32)
    for r in range(size):
        flips[r] = int(order[(place[r] - 1) % size] == r - 1)
    sends = np.zeros((size, half + 1, 6), np.int32)
    early_halves = []
    for r in range(size):
        for d in range(half + 1):
            ahead, back = order[(place[r] + d) % size], order[(place[r] - d) % size]
            late = [2 * ahead + flips[ahead], 2 * back + 1 - flips[back]]
            sends[r, d] = late + [2 * ahead + 1 - flips[ahead], 2 * back + flips[back], 2 * r, 2 * r + 1]
        early_halves.append({(int(i) // 2, int(i) % 2) for i in sends[r, half - 1, 2:4]})
    tiles = tile_plan(order, early_halves)
    most = max(len(call) for calls in tiles for call in calls)
    plan = np.zeros((size, size, 3 + most), np.int32)
    for r in range(size):
        for call in range(size):
            d = min(call, half - 1) if call <= half else half
            back, ahead = 2 * order[(place[r] - d) % size], 2 * order[(place[r] + d) % size]
            if call == half - 1 or call == half + 1:
                ahead += 1
            elif call == half:
                back += 1
            row = [back, ahead, len(tiles[r][call])] + tiles[r][call]
            plan[r, call, :len(row)] = row
    my_plan = jnp.asarray(plan)[rank]
    my_sends = jnp.asarray(sends)[rank]
    flipped = jnp.asarray(flips)[rank] > 0

    cosine, sine, key_wide, doc_bias, own_bias, lists = tables(
        seg_ids, seg_doc, doc_lens, prefix, prefix_keyvalue_cache
    )
    gain = norm_gain.astype(jnp.float32).reshape(1, depth)
    fixed = (gain, w_query, keyvalue_weight, cosine, sine, key_wide, prefix_keyvalue_cache, doc_bias, own_bias)
    dims = (tokens, heads, prefix, depth)

    def pass_on(pair):
        return forward(pair[0]), backward(pair[1])

    def add(pair, arrived):
        return tuple((a.astype(jnp.float32) + b.astype(jnp.float32)).astype(jnp.bfloat16) for a, b in zip(pair, arrived))

    def step(call, parts, state):
        return tuple(run_step(my_plan[call], lists, parts, fixed, state, dims))

    held = pass_on((hidden_in, hidden_in))
    state = step(0, [hidden_in], None)
    for distance in range(1, half - 1):
        held, state = lax.optimization_barrier((held, state))
        if distance < half - 2:
            following = pass_on(held)
        else:
            following = pass_on((held[0][:TILE], held[1][TILE:])), pass_on((held[0][TILE:], held[1][:TILE]))
        state = step(distance, held, state)
        held = following
    first, second = held
    first, state = lax.optimization_barrier((first, state))
    last = pass_on(first)
    state = step(half - 1, first, state)
    second, state = lax.optimization_barrier((second, state))
    state = step(half, second, state)

    made = tuple(product(my_sends[half - 1, 2:4], 2, state[2], w_out))
    made, last, state = lax.optimization_barrier((made, last, state))
    early = pass_on(made)
    state = step(half + 1, last, state)
    terms = product(jnp.concatenate([my_sends[half, :2], my_sends[half - 1, :2]]), 4, state[2], w_out)
    made, late = tuple(terms[:2]), tuple(terms[2:])
    far = pass_on(made)
    for distance in range(half - 1, 0, -1):
        near = distance - 1
        if near == 0:
            early, made, state = lax.optimization_barrier((early, made, state))
            own = tuple(product(my_sends[1, 4:], 2, state[2], w_out))
            far, own = lax.optimization_barrier((far, own))
        else:
            made, state = lax.optimization_barrier((made, state))
            state = step(size - near, [], state)
            ahead = tuple(product(my_sends[near, 2:4], 2, state[2], w_out))
            early, ahead = lax.optimization_barrier((early, ahead))
            made = add(ahead, early)
            early = pass_on(made)
            made, state = lax.optimization_barrier((made, state))
            following = tuple(product(my_sends[near, :2], 2, state[2], w_out))
            far, following = lax.optimization_barrier((far, following))
        made = add(late, far)
        far = pass_on(made)
        late = following
    wide = [[part.astype(jnp.float32) for part in pair] for pair in (early, far)]
    with_far, with_early = wide[1][0] + wide[0][1], wide[0][0] + wide[1][1]
    halves = [jnp.where(flipped, with_early, with_far), jnp.where(flipped, with_far, with_early)]
    summed = jnp.concatenate([halves[i] + own[i].astype(jnp.float32) for i in range(2)], axis=0)
    return (hidden_in.astype(jnp.float32) + summed).astype(jnp.bfloat16)


def solution(mesh):
    return jax.shard_map(
        local,
        mesh=mesh,
        in_specs=(
            P(("dp", "tensor"), None),
            P(),
            P(None, "tensor"),
            P(None, "tensor"),
            P("tensor", None),
            P(None, "tensor"),
            P("dp"),
            P("dp"),
            P(),
        ),
        out_specs=P(("dp", "tensor"), None),
        check_vma=False,
    )
```

```python
import functools
import math

import jax
import jax.numpy as jnp
import numpy as np
from jax import lax
from jax.experimental import pallas as pl
from jax.experimental.pallas import tpu as pltpu
from jax.sharding import PartitionSpec as P

HEAD = 128
TILE = 64
KEY_BLOCK = 256
GROUP = 4
DEPTH_CHUNKS = 4
COLUMN_CHUNKS = 4
PIECES_MOST = 4
HEADER = PIECES_MOST + 3
MASKED = -1e30
EPS = 1e-05
ROPE_THETA = 500000.0
VMEM_LIMIT = 32 * 1024 * 1024


def ring_order(size):
    zs = 4 if size % 8 == 0 else 1
    ys = size // zs
    if zs == 1:
        return list(range(size))
    cycle = [(0, 0)]
    for y in range(ys):
        column = range(1, zs) if y % 2 == 0 else range(zs - 1, 0, -1)
        cycle += [(z, y) for z in column]
    cycle += [(0, y) for y in range(ys - 1, 0, -1)]
    return [z * ys + y for z, y in cycle]


def tile_plan(order, sends):
    size = len(order)
    half = size // 2
    place = {r: i for i, r in enumerate(order)}
    spare = [0] + [6] * (half - 3) + [1, 2] + [0] * (size - half)
    plans = []
    for rank in range(size):
        arrival, due = {}, {}
        for chunk in range(size):
            behind = (place[rank] - place[chunk]) % size
            distance = min(behind, size - behind)
            for upper in range(2):
                arrival[chunk, upper] = distance
                if distance == half:
                    arrival[chunk, upper] = half + 1
                elif distance == half - 1:
                    arrival[chunk, upper] = half - 1 if upper == int(behind != distance) else half
        for d in range(half + 1):
            for i, row in enumerate(sends[rank, d]):
                if i >= 4:
                    when = size - 1
                elif i >= 2 and 0 < d < half:
                    when = {half - 1: half, half - 2: half + 1}.get(d, size - d - 1)
                elif i < 2 and d > 0:
                    when = half + 1 if d == half else size - max(d - 1, 1)
                else:
                    continue
                due[int(row) // 2, int(row) % 2] = when
        ready = {}
        for chunk in range(size):
            ready[chunk, 1] = max(arrival[chunk, 0], arrival[chunk, 1])
            ready[chunk, 0] = max(arrival[chunk, 0], arrival[chunk - 1, 1]) if chunk else ready[chunk, 1]
        calls, left = [], set(ready)
        for call in range(size):
            able = sorted((due[t], t) for t in left if ready[t] <= call)
            must = [t for when, t in able if when <= call]
            more = [t for when, t in able if when > call][:max(spare[call] - len(must), 0)]
            calls.append([2 * chunk + upper for chunk, upper in must + more])
            left -= set(must + more)
        assert not left and all(ready[t] <= due[t] for t in ready)
        plans.append(calls)
    return plans


def step_kernel(pieces, rows, heads, sending, *refs):
    total = pieces * rows
    width = heads * HEAD
    it = iter(refs)
    ids, lists = next(it), next(it)
    xs = [next(it) for _ in range(pieces)]
    gain, wq, wkv, cos_tab, sin_tab, key_wide, cache, doc_bias, own_bias = [next(it) for _ in range(9)]
    first = pieces == 1 and rows == 128
    if not first:
        next(it), next(it), next(it)
    if sending:
        w_out = next(it)
    qb, kvb, att = next(it), next(it), next(it)
    if sending:
        terms = [next(it), next(it)]
    (x_s, xn_s, w_s, cos_s, sin_s, qo_s, kvo_s, key_s, val_s, qt_s, kvt_s, db_s, ob_s, sc_s, at_s,
     wide_s, own_s, o_s, sem_in, sem_tab, sem_w, sem_k, sem_out, sem_tile, sem_att) = [next(it) for _ in range(25)]
    if sending:
        rows_s, wo_s, made_s, sem_rows, sem_wo, sem_made = list(it)
    deep = wq.shape[0] // DEPTH_CHUNKS
    blocks = key_wide.shape[0] - 1
    stride = blocks + GROUP

    key_copy = pltpu.make_async_copy(key_wide, key_s, sem_k.at[0])
    val_copy = pltpu.make_async_copy(cache.at[:, pl.ds(HEAD, HEAD)], val_s, sem_k.at[1])
    if pieces:
        x_copies, tab_copies = [], []
        for i in range(pieces):
            span = pl.ds(i * rows, rows)
            place = pl.ds(pl.multiple_of(ids[i] * TILE, TILE), rows)
            x_copies.append(pltpu.make_async_copy(xs[i], x_s.at[span], sem_in.at[i]))
            tab_copies.append(pltpu.make_async_copy(cos_tab.at[place], cos_s.at[span], sem_tab.at[2 * i]))
            tab_copies.append(pltpu.make_async_copy(sin_tab.at[place], sin_s.at[span], sem_tab.at[2 * i + 1]))
        for copy in x_copies:
            copy.start()
        w_copies = []
        for j in range(DEPTH_CHUNKS):
            span = pl.ds(j * deep, deep)
            w_copies.append(pltpu.make_async_copy(wq.at[span], w_s.at[span, pl.ds(0, width)], sem_w.at[2 * j]))
            w_copies.append(
                pltpu.make_async_copy(wkv.at[span], w_s.at[span, pl.ds(width, 2 * HEAD)], sem_w.at[2 * j + 1])
            )
        for copy in w_copies:
            copy.start()
        for copy in tab_copies:
            copy.start()
    count = ids[PIECES_MOST]

    def load_cache():
        @pl.when(count > 0)
        def _():
            key_copy.start()
            val_copy.start()

    if not pieces:
        load_cache()
    else:
        gains = gain[...]
        for i in range(pieces):
            x_copies[i].wait()

        def norm_rows(r, carry):
            span = pl.ds(pl.multiple_of(r * 16, 16), 16)
            values = x_s[span, :].astype(jnp.float32)
            mean_square = jnp.mean(values * values, axis=-1, keepdims=True)
            xn_s[span, :] = (values * lax.rsqrt(mean_square + EPS) * gains).astype(jnp.bfloat16)
            return carry

        lax.fori_loop(0, total // 16, norm_rows, 0, unroll=4)
        load_cache()
        for copy in tab_copies:
            copy.wait()
        cosine, sine = cos_s[...], sin_s[...]

        def rotate(v):
            return (v * cosine + pltpu.roll(v, HEAD // 2, 1) * sine).astype(jnp.bfloat16)

        made = None
        for j in range(DEPTH_CHUNKS):
            w_copies[2 * j].wait()
            w_copies[2 * j + 1].wait()
            span = slice(j * deep, (j + 1) * deep)
            more = jnp.dot(xn_s[:, span], w_s[span, :], preferred_element_type=jnp.float32)
            made = more if made is None else made + more
        for h in range(heads):
            qo_s[h] = rotate(made[:, h * HEAD:(h + 1) * HEAD])
        kvo_s[:, :HEAD] = rotate(made[:, width:width + HEAD])
        kvo_s[:, HEAD:] = made[:, width + HEAD:].astype(jnp.bfloat16)
        outs = []
        for i in range(pieces):
            span = pl.ds(i * rows, rows)
            place = pl.ds(pl.multiple_of(ids[i] * TILE, TILE), rows)
            outs.append(pltpu.make_async_copy(qo_s.at[:, span], qb.at[:, place], sem_out.at[2 * i]))
            outs.append(pltpu.make_async_copy(kvo_s.at[span], kvb.at[place], sem_out.at[2 * i + 1]))
        for copy in outs:
            copy.start()
        for copy in outs:
            copy.wait()

    if sending:
        term_copies = weight_copies(w_out, wo_s, sem_wo)
        for copy in term_copies:
            copy.start()
    factor = math.log2(math.e) / math.sqrt(HEAD)

    def fetches(i, slot):
        tile = ids[HEADER + i]
        at = pl.multiple_of(tile * TILE, TILE)
        before = pl.multiple_of(jnp.maximum(tile - 1, 0) * TILE, TILE)
        return [
            pltpu.make_async_copy(qb.at[:, pl.ds(at, TILE)], qt_s.at[slot], sem_tile.at[slot, 0]),
            pltpu.make_async_copy(kvb.at[pl.ds(before, 2 * TILE)], kvt_s.at[slot], sem_tile.at[slot, 1]),
            pltpu.make_async_copy(doc_bias.at[pl.ds(at, TILE)], db_s.at[slot], sem_tile.at[slot, 2]),
            pltpu.make_async_copy(own_bias.at[pl.ds(at, TILE)], ob_s.at[slot], sem_tile.at[slot, 3]),
        ]

    def att_copy(i):
        at = pl.multiple_of(ids[HEADER + i] * TILE, TILE)
        return pltpu.make_async_copy(at_s, att.at[pl.ds(at, TILE)], sem_att)

    @pl.when(count > 0)
    def _():
        for copy in fetches(0, 0):
            copy.start()
        key_copy.wait()
        val_copy.wait()

    contract_last = (((1,), (1,)), ((), ()))

    def one_tile(i, carry):
        slot = lax.rem(i, 2)

        @pl.when(i + 1 < count)
        def _():
            for copy in fetches(i + 1, 1 - slot):
                copy.start()

        for copy in fetches(i, slot):
            copy.wait()
        tile = ids[HEADER + i]
        needed = lists[tile * stride]
        for h in range(heads):
            wide_s[h * TILE:(h + 1) * TILE, :HEAD] = qt_s[slot, h]
            wide_s[h * TILE:(h + 1) * TILE, HEAD:] = db_s[slot]
        own = lax.dot_general(
            wide_s[:, :HEAD], kvt_s[slot, :, :HEAD], contract_last, preferred_element_type=jnp.float32
        )
        own = (own.reshape(heads, TILE, HEAD) + ob_s[slot][None]).reshape(heads * TILE, HEAD)
        own_s[...] = own

        def attend(groups):
            listed = [lists[tile * stride + 1 + j] for j in range(groups * GROUP)]
            top = own_s[...]
            for g in range(groups):
                keys = jnp.concatenate([key_s[block] for block in listed[g * GROUP:(g + 1) * GROUP]], axis=1)
                scores = jnp.dot(wide_s[...], keys, preferred_element_type=jnp.float32)
                sc_s[g] = scores
                for c in range(0, GROUP * KEY_BLOCK, HEAD):
                    top = jnp.maximum(top, scores[:, c:c + HEAD])
            top = jnp.max(top, axis=1, keepdims=True) * factor
            weights = jnp.exp2(own_s[...] * factor - top)
            sums = weights
            made = [jnp.dot(weights.astype(jnp.bfloat16), kvt_s[slot, :, HEAD:], preferred_element_type=jnp.float32)]
            made += [None] * (GROUP - 1)
            for j, block in enumerate(listed):
                at = pl.multiple_of(jnp.minimum(block, blocks - 1) * KEY_BLOCK, KEY_BLOCK)
                c = j % GROUP * KEY_BLOCK
                weights = jnp.exp2(sc_s[j // GROUP, :, c:c + KEY_BLOCK] * factor - top)
                sums = sums + (weights[:, :HEAD] + weights[:, HEAD:])
                more = jnp.dot(
                    weights.astype(jnp.bfloat16), val_s[pl.ds(at, KEY_BLOCK), :], preferred_element_type=jnp.float32
                )
                made[j % GROUP] = more if made[j % GROUP] is None else made[j % GROUP] + more
            made = (made[0] + made[1]) + (made[2] + made[3])
            o_s[...] = (made / jnp.sum(sums, axis=1, keepdims=True)).astype(jnp.bfloat16)

        for groups in range(1, blocks // GROUP + 1):

            @pl.when(needed == groups)
            def _(groups=groups):
                attend(groups)

        @pl.when(i > 0)
        def _():
            att_copy(i - 1).wait()

        for h in range(heads):
            at_s[:, h * HEAD:(h + 1) * HEAD] = o_s[h * TILE:(h + 1) * TILE]
        att_copy(i).start()
        return carry

    lax.fori_loop(0, count, one_tile, 0)

    @pl.when(count > 0)
    def _():
        att_copy(count - 1).wait()

    if sending:
        places = [ids[PIECES_MOST + 1], ids[PIECES_MOST + 2]]
        write_terms(places, att, term_copies, terms, rows_s, wo_s, made_s, sem_rows, sem_made)


def run_step(ids, lists, xs, fixed, state, dims, w_out=None):
    tokens, heads, prefix, depth = dims
    pieces = len(xs)
    rows = xs[0].shape[0] if pieces else TILE
    total = max(pieces * rows, 16)
    width = heads * HEAD
    any_spec = pl.BlockSpec(memory_space=pl.ANY)
    vmem_spec = pl.BlockSpec(memory_space=pltpu.VMEM)
    operands = list(xs) + list(fixed)
    specs = [any_spec] * pieces + [vmem_spec] + [any_spec] * (len(fixed) - 1)
    aliases = {}
    if state is not None:
        aliases = {2 + len(operands) + i: i for i in range(3)}
        operands += list(state)
        specs += [any_spec] * 3
    sending = w_out is not None
    if sending:
        operands.append(w_out)
        specs.append(any_spec)
    out_shape = [
        jax.ShapeDtypeStruct((heads, tokens, HEAD), jnp.bfloat16),
        jax.ShapeDtypeStruct((tokens, 2 * HEAD), jnp.bfloat16),
        jax.ShapeDtypeStruct((tokens, width), jnp.bfloat16),
    ]
    if sending:
        out_shape += [jax.ShapeDtypeStruct((TILE, w_out.shape[1]), jnp.bfloat16)] * 2
    small = 16
    w_rows = depth if pieces else small
    scratch = [
        pltpu.VMEM((total, depth), jnp.bfloat16),
        pltpu.VMEM((total, depth), jnp.bfloat16),
        pltpu.VMEM((w_rows, width + 2 * HEAD), jnp.bfloat16),
        pltpu.VMEM((total, HEAD), jnp.float32),
        pltpu.VMEM((total, HEAD), jnp.float32),
        pltpu.VMEM((heads, total, HEAD), jnp.bfloat16),
        pltpu.VMEM((total, 2 * HEAD), jnp.bfloat16),
        pltpu.VMEM((prefix // KEY_BLOCK + 1, 2 * HEAD, KEY_BLOCK), jnp.bfloat16),
        pltpu.VMEM((prefix, HEAD), jnp.bfloat16),
        pltpu.VMEM((2, heads, TILE, HEAD), jnp.bfloat16),
        pltpu.VMEM((2, 2 * TILE, 2 * HEAD), jnp.bfloat16),
        pltpu.VMEM((2, TILE, HEAD), jnp.bfloat16),
        pltpu.VMEM((2, TILE, HEAD), jnp.float32),
        pltpu.VMEM((prefix // KEY_BLOCK // GROUP, heads * TILE, GROUP * KEY_BLOCK), jnp.float32),
        pltpu.VMEM((TILE, width), jnp.bfloat16),
        pltpu.VMEM((heads * TILE, 2 * HEAD), jnp.bfloat16),
        pltpu.VMEM((heads * TILE, HEAD), jnp.float32),
        pltpu.VMEM((heads * TILE, HEAD), jnp.bfloat16),
        pltpu.SemaphoreType.DMA((max(pieces, 1),)),
        pltpu.SemaphoreType.DMA((2 * max(pieces, 1),)),
        pltpu.SemaphoreType.DMA((2 * DEPTH_CHUNKS,)),
        pltpu.SemaphoreType.DMA((2,)),
        pltpu.SemaphoreType.DMA((2 * max(pieces, 1),)),
        pltpu.SemaphoreType.DMA((2, 4)),
        pltpu.SemaphoreType.DMA,
    ]
    if sending:
        scratch += term_scratch(2, width, w_out.shape[1])
    return pl.pallas_call(
        functools.partial(step_kernel, pieces, rows, heads, sending),
        grid_spec=pltpu.PrefetchScalarGridSpec(
            num_scalar_prefetch=2,
            grid=(),
            in_specs=specs,
            out_specs=[any_spec] * len(out_shape),
            scratch_shapes=scratch,
        ),
        out_shape=out_shape,
        input_output_aliases=aliases,
        compiler_params=pltpu.CompilerParams(vmem_limit_bytes=VMEM_LIMIT),
        cost_estimate=pl.CostEstimate(flops=1 << 20, bytes_accessed=1 << 16, transcendentals=0),
    )(ids, lists, *operands)


def weight_copies(w_out, w_s, sem_w):
    columns = w_out.shape[1] // COLUMN_CHUNKS
    spans = [pl.ds(c * columns, columns) for c in range(COLUMN_CHUNKS)]
    return [pltpu.make_async_copy(w_out.at[:, span], w_s.at[:, span], sem_w.at[c]) for c, span in enumerate(spans)]


def write_terms(places, att, w_copies, outs, rows_s, w_s, made_s, sem_rows, sem_out):
    columns = w_s.shape[1] // COLUMN_CHUNKS
    row_copies = [
        pltpu.make_async_copy(
            att.at[pl.ds(pl.multiple_of(place * TILE, TILE), TILE)], rows_s.at[pl.ds(i * TILE, TILE)], sem_rows.at[i]
        )
        for i, place in enumerate(places)
    ]
    for copy in row_copies:
        copy.start()
    for copy in row_copies:
        copy.wait()
    out_copies = []
    for c in range(COLUMN_CHUNKS):
        span = pl.ds(c * columns, columns)
        w_copies[c].wait()
        made = jnp.dot(rows_s[...], w_s[:, span], preferred_element_type=jnp.float32)
        made_s[:, span] = made.astype(jnp.bfloat16)
        for i in range(len(places)):
            copy = pltpu.make_async_copy(
                made_s.at[pl.ds(i * TILE, TILE), span], outs[i].at[:, span], sem_out.at[i, c]
            )
            copy.start()
            out_copies.append(copy)
    for copy in out_copies:
        copy.wait()


def term_scratch(count, width, columns):
    return [
        pltpu.VMEM((count * TILE, width), jnp.bfloat16),
        pltpu.VMEM((width, columns), jnp.bfloat16),
        pltpu.VMEM((count * TILE, columns), jnp.bfloat16),
        pltpu.SemaphoreType.DMA((count,)),
        pltpu.SemaphoreType.DMA((COLUMN_CHUNKS,)),
        pltpu.SemaphoreType.DMA((count, COLUMN_CHUNKS)),
    ]


def product_kernel(count, ids, att, w_out, *refs):
    rows_s, w_s, made_s, sem_rows, sem_w, sem_out = refs[count:]
    copies = weight_copies(w_out, w_s, sem_w)
    for copy in copies:
        copy.start()
    places = [ids[i] for i in range(count)]
    write_terms(places, att, copies, refs[:count], rows_s, w_s, made_s, sem_rows, sem_out)


def product(ids, count, att, w_out):
    width, columns = w_out.shape
    any_spec = pl.BlockSpec(memory_space=pl.ANY)
    return pl.pallas_call(
        functools.partial(product_kernel, count),
        grid_spec=pltpu.PrefetchScalarGridSpec(
            num_scalar_prefetch=1,
            grid=(),
            in_specs=[any_spec] * 2,
            out_specs=[any_spec] * count,
            scratch_shapes=term_scratch(count, width, columns),
        ),
        out_shape=[jax.ShapeDtypeStruct((TILE, columns), jnp.bfloat16)] * count,
        compiler_params=pltpu.CompilerParams(vmem_limit_bytes=VMEM_LIMIT),
        cost_estimate=pl.CostEstimate(flops=1 << 20, bytes_accessed=1 << 16, transcendentals=0),
    )(ids, att, w_out)


def tables(seg_ids, seg_doc, doc_lens, prefix, cache):
    tokens = seg_ids.shape[0]
    tiles = tokens // TILE
    blocks = prefix // KEY_BLOCK
    docs = doc_lens.shape[0]
    order = jnp.arange(tokens, dtype=jnp.int32)
    start = jnp.sum((seg_ids[None, :] < seg_ids[:, None]).astype(jnp.int32), axis=1, dtype=jnp.int32)
    positions = prefix + order - start
    segments = jnp.arange(seg_doc.shape[0], dtype=jnp.int32)
    tok_doc = jnp.sum(
        jnp.where(seg_ids[:, None] == segments[None, :], seg_doc[None, :], 0), axis=1, dtype=jnp.int32
    )
    doc_list = jnp.arange(docs, dtype=jnp.int32)
    doc_ends = jnp.sum(jnp.where(doc_list[None, :] <= doc_list[:, None], doc_lens[None, :], 0), axis=1)
    doc_starts = doc_ends - doc_lens
    lanes = jnp.arange(HEAD, dtype=jnp.int32)
    half = HEAD // 2
    inverse = ROPE_THETA ** (-(jnp.arange(half, dtype=jnp.float32) * 2.0 / HEAD))
    inverse = jnp.concatenate([inverse, inverse])
    angles = positions.astype(jnp.float32)[:, None] * inverse[None, :]
    cosine = jnp.cos(angles)
    sine = jnp.sin(angles) * jnp.where(lanes < half, -1.0, 1.0)[None, :]
    doc_bias = jnp.where(lanes[None, :] == tok_doc[:, None], 0.0, MASKED).astype(jnp.bfloat16)
    spot = jnp.arange(prefix + KEY_BLOCK, dtype=jnp.int32).reshape(blocks + 1, 1, KEY_BLOCK)
    low = jnp.pad(doc_starts, (0, HEAD - docs), constant_values=prefix).reshape(1, HEAD, 1)
    high = jnp.pad(doc_ends, (0, HEAD - docs), constant_values=prefix + KEY_BLOCK).reshape(1, HEAD, 1)
    one_hot = ((spot >= low) & (spot < high)).astype(jnp.bfloat16)
    by_block = cache[:, :HEAD].reshape(blocks, KEY_BLOCK, HEAD).transpose(0, 2, 1)
    key_wide = jnp.concatenate([jnp.pad(by_block, ((0, 1), (0, 0), (0, 0))), one_hot], axis=1)
    first_key = jnp.maximum(jnp.arange(tiles, dtype=jnp.int32) - 1, 0) * TILE
    spots = first_key[:, None] + lanes[None, :]
    by_tile = seg_ids.reshape(tiles, TILE)
    earlier = jnp.concatenate([by_tile[:1], by_tile[:-1]], axis=0)
    later = jnp.concatenate([by_tile[1:2], by_tile[1:]], axis=0)
    window_seg = jnp.concatenate([earlier, later], axis=1)
    ok = (window_seg[:, None, :] == by_tile[:, :, None]) & (
        spots[:, None, :] <= order.reshape(tiles, TILE)[:, :, None]
    )
    own_bias = jnp.where(ok, 0.0, MASKED).astype(jnp.float32).reshape(tokens, HEAD)
    present = jnp.any(tok_doc.reshape(tiles, TILE)[:, :, None] == doc_list[None, None, :], axis=1)
    edge = jnp.arange(blocks, dtype=jnp.int32) * KEY_BLOCK
    overlap = (doc_starts[:, None] < edge[None, :] + KEY_BLOCK) & (doc_ends[:, None] > edge[None, :])
    flags = jnp.any(present[:, :, None] & overlap[None, :, :], axis=1).astype(jnp.int32)
    block_ids = jnp.arange(blocks, dtype=jnp.int32)
    rank = jnp.sum(jnp.where(block_ids[None, :, None] > block_ids[None, None, :], flags[:, None, :], 0), axis=2)
    listed = jnp.sum(
        jnp.where((rank[:, :, None] == block_ids[None, None, :]) & (flags[:, :, None] > 0), block_ids[None, :, None], 0),
        axis=1,
    )
    count = jnp.sum(flags, axis=1, keepdims=True)
    listed = jnp.where(block_ids[None, :] < count, listed, blocks)
    groups = (count + GROUP - 1) // GROUP
    lists = jnp.pad(jnp.concatenate([groups, listed], axis=1), ((0, 0), (0, GROUP - 1)))
    lists = lists.astype(jnp.int32).reshape(-1)
    return cosine, sine, key_wide, doc_bias, own_bias, lists


def local(
    hidden_in, norm_gain, w_query, keyvalue_weight, w_out, prefix_keyvalue_cache, seg_ids, seg_doc, doc_lens
):
    size = lax.axis_size("tensor")
    tokens = seg_ids.shape[0]
    prefix = prefix_keyvalue_cache.shape[0]
    chunk_rows, depth = hidden_in.shape
    heads = w_query.shape[1] // HEAD
    order = ring_order(size)
    half = size // 2
    rank = lax.axis_index("tensor")

    forward_pairs = [(order[i], order[(i + 1) % size]) for i in range(size)]
    backward_pairs = [(b, a) for a, b in forward_pairs]

    def forward(x):
        return lax.ppermute(x, "tensor", forward_pairs)

    def backward(x):
        return lax.ppermute(x, "tensor", backward_pairs)

    if keyvalue_weight.shape[1] == HEAD:
        swap = [(i, i ^ 1) for i in range(size)]
        even = rank % 2 == 0
        other_weight, other_cache = lax.ppermute((keyvalue_weight, prefix_keyvalue_cache), "tensor", swap)
        keyvalue_weight = jnp.concatenate(
            [jnp.where(even, keyvalue_weight, other_weight), jnp.where(even, other_weight, keyvalue_weight)], axis=1
        )
        prefix_keyvalue_cache = jnp.concatenate(
            [
                jnp.where(even, prefix_keyvalue_cache, other_cache),
                jnp.where(even, other_cache, prefix_keyvalue_cache),
            ],
            axis=1,
        )

    place = {r: i for i, r in enumerate(order)}
    flips = np.zeros((size,), np.int32)
    for r in range(size):
        flips[r] = int(order[(place[r] - 1) % size] == r - 1)
    sends = np.zeros((size, half + 1, 6), np.int32)
    for r in range(size):
        for d in range(half + 1):
            ahead, back = order[(place[r] + d) % size], order[(place[r] - d) % size]
            late = [2 * ahead + flips[ahead], 2 * back + 1 - flips[back]]
            sends[r, d] = late + [2 * ahead + 1 - flips[ahead], 2 * back + flips[back], 2 * r, 2 * r + 1]
    tiles = tile_plan(order, sends)
    most = max(len(call) for calls in tiles for call in calls)
    plan = np.zeros((size, size, HEADER + most), np.int32)
    for r in range(size):
        for call in range(size):
            d = min(call, half - 1) if call <= half else half
            back, ahead = 2 * order[(place[r] - d) % size], 2 * order[(place[r] + d) % size]
            if call == half - 2:
                parts = [back, ahead + 1, back + 1, ahead]
            elif call == half - 1 or call == half + 1:
                parts = [back, ahead + 1, 0, 0]
            elif call == half:
                parts = [back + 1, ahead, 0, 0]
            else:
                parts = [back, ahead, 0, 0]
            terms = sends[r, half, :2] if call == half + 1 else sends[r, half - 1, 2:4]
            row = parts + [len(tiles[r][call])] + [int(i) for i in terms] + tiles[r][call]
            plan[r, call, :len(row)] = row
    my_plan = jnp.asarray(plan)[rank]
    my_sends = jnp.asarray(sends)[rank]
    flipped = jnp.asarray(flips)[rank] > 0

    cosine, sine, key_wide, doc_bias, own_bias, lists = tables(
        seg_ids, seg_doc, doc_lens, prefix, prefix_keyvalue_cache
    )
    gain = norm_gain.astype(jnp.float32).reshape(1, depth)
    fixed = (gain, w_query, keyvalue_weight, cosine, sine, key_wide, prefix_keyvalue_cache, doc_bias, own_bias)
    dims = (tokens, heads, prefix, depth)

    def pass_on(pair):
        return forward(pair[0]), backward(pair[1])

    def add(pair, arrived):
        return tuple((a.astype(jnp.float32) + b.astype(jnp.float32)).astype(jnp.bfloat16) for a, b in zip(pair, arrived))

    def step(call, parts, state):
        return tuple(run_step(my_plan[call], lists, parts, fixed, state, dims))

    def step_and_send(call, parts, state):
        made = tuple(run_step(my_plan[call], lists, parts, fixed, state, dims, w_out))
        return made[:3], made[3:]

    def halves_of(pair):
        return (pair[0][:TILE], pair[1][TILE:]), (pair[0][TILE:], pair[1][:TILE])

    held = pass_on((hidden_in, hidden_in))
    state = step(0, [hidden_in], None)
    for distance in range(1, half - 2):
        held, state = lax.optimization_barrier((held, state))
        if distance < half - 3:
            following = pass_on(held)
        else:
            first, second = (pass_on(part) for part in halves_of(held))
        state = step(distance, held, state)
        if distance < half - 3:
            held = following
    first, state = lax.optimization_barrier((first, state))
    first_on = pass_on(first)
    second, state = lax.optimization_barrier((second, state))
    second_on = pass_on(second)
    state = step(half - 2, first + second, state)
    first, state = lax.optimization_barrier((first_on, state))
    last = pass_on(first)
    state = step(half - 1, first, state)
    second, state = lax.optimization_barrier((second_on, state))
    state, made = step_and_send(half, second, state)
    made, last, state = lax.optimization_barrier((made, last, state))
    early = pass_on(made)
    state, made = step_and_send(half + 1, last, state)
    far = pass_on(made)
    for distance in range(half - 1, 0, -1):
        near = distance - 1
        if near > 0:
            made, state = lax.optimization_barrier((made, state))
            ahead = tuple(product(my_sends[near, 2:4], 2, state[2], w_out))
            early, ahead = lax.optimization_barrier((early, ahead))
            made = add(ahead, early)
            early = pass_on(made)
            made, state = lax.optimization_barrier((made, state))
            state = step(size - near, [], state)
        else:
            early, made, state = lax.optimization_barrier((early, made, state))
        late = product(my_sends[distance], 2 if near > 0 else 6, state[2], w_out)
        own, late = late[4:], tuple(late[:2])
        far, late = lax.optimization_barrier((far, late))
        made = add(late, far)
        far = pass_on(made)
    wide = [[part.astype(jnp.float32) for part in pair] for pair in (early, far)]
    with_far, with_early = wide[1][0] + wide[0][1], wide[0][0] + wide[1][1]
    halves = [jnp.where(flipped, with_early, with_far), jnp.where(flipped, with_far, with_early)]
    summed = jnp.concatenate([halves[i] + own[i].astype(jnp.float32) for i in range(2)], axis=0)
    return (hidden_in.astype(jnp.float32) + summed).astype(jnp.bfloat16)


def solution(mesh):
    return jax.shard_map(
        local,
        mesh=mesh,
        in_specs=(
            P(("dp", "tensor"), None),
            P(),
            P(None, "tensor"),
            P(None, "tensor"),
            P("tensor", None),
            P(None, "tensor"),
            P("dp"),
            P("dp"),
            P(),
        ),
        out_specs=P(("dp", "tensor"), None),
        check_vma=False,
    )
```

```python
import functools
import math

import jax
import jax.numpy as jnp
import numpy as np
from jax import lax
from jax.experimental import pallas as pl
from jax.experimental.pallas import tpu as pltpu
from jax.sharding import PartitionSpec as P

HEAD = 128
TILE = 64
KEY_BLOCK = 256
GROUP = 4
DEPTH_CHUNKS = 4
COLUMN_CHUNKS = 4
PIECES_MOST = 5
HEADER = PIECES_MOST + 3
MASKED = -1e30
EPS = 1e-05
ROPE_THETA = 500000.0
VMEM_LIMIT = 28 * 1024 * 1024
VMEM_LIMIT_FIRST = 44 * 1024 * 1024


def ring_order(size):
    zs = 4 if size % 8 == 0 else 1
    ys = size // zs
    if zs == 1:
        return list(range(size))
    cycle = [(0, 0)]
    for y in range(ys):
        column = range(1, zs) if y % 2 == 0 else range(zs - 1, 0, -1)
        cycle += [(z, y) for z in column]
    cycle += [(0, y) for y in range(ys - 1, 0, -1)]
    return [z * ys + y for z, y in cycle]


def tile_plan(order, sends):
    size = len(order)
    half = size // 2
    place = {r: i for i, r in enumerate(order)}
    spare = [0, 4] + [4] * (half - 4) + [2, 2] + [0] * (size - half)
    plans = []
    for rank in range(size):
        arrival, due = {}, {}
        for chunk in range(size):
            behind = (place[rank] - place[chunk]) % size
            distance = min(behind, size - behind)
            for upper in range(2):
                arrival[chunk, upper] = max(distance, 1)
                if distance == half:
                    arrival[chunk, upper] = half + 1
                elif distance == half - 1:
                    arrival[chunk, upper] = half - 1 if upper == int(behind != distance) else half
        for d in range(half + 1):
            for i, row in enumerate(sends[rank, d]):
                if i >= 4:
                    when = size - 1
                elif i >= 2 and 0 < d < half:
                    when = {half - 1: half, half - 2: half + 1}.get(d, size - d - 1)
                elif i < 2 and d > 0:
                    when = half + 1 if d == half else size - max(d - 1, 1)
                else:
                    continue
                due[int(row) // 2, int(row) % 2] = when
        ready = {}
        for chunk in range(size):
            ready[chunk, 1] = max(arrival[chunk, 0], arrival[chunk, 1])
            ready[chunk, 0] = max(arrival[chunk, 0], arrival[chunk - 1, 1]) if chunk else ready[chunk, 1]
        calls, left = [], set(ready)
        for call in range(size):
            able = sorted((due[t], t) for t in left if ready[t] <= call)
            must = [t for when, t in able if when <= call]
            more = [t for when, t in able if when > call][:max(spare[call] - len(must), 0)]
            calls.append([2 * chunk + upper for chunk, upper in must + more])
            left -= set(must + more)
        assert not left and all(ready[t] <= due[t] for t in ready)
        plans.append(calls)
    return plans


def step_kernel(rows, heads, fresh, sending, *refs):
    pieces = len(rows)
    total = sum(rows)
    spans = [pl.ds(sum(rows[:i]), rows[i]) for i in range(pieces)]
    width = heads * HEAD
    it = iter(refs)
    ids, lists = next(it), next(it)
    xs = [next(it) for _ in range(pieces)]
    gain, wq, wkv, cos_tab, sin_tab, key_wide, cache, doc_bias, own_bias = [next(it) for _ in range(9)]
    if not fresh:
        next(it), next(it), next(it)
    if sending:
        w_out = next(it)
    qb, kvb, att = next(it), next(it), next(it)
    if sending:
        terms = [next(it), next(it)]
    (x_s, xn_s, w_s, cos_s, sin_s, qo_s, kvo_s, key_s, val_s, qt_s, kvt_s, db_s, ob_s, sc_s, at_s,
     wide_s, own_s, o_s, sem_in, sem_tab, sem_w, sem_k, sem_out, sem_tile, sem_att) = [next(it) for _ in range(25)]
    if sending:
        rows_s, wo_s, made_s, sem_rows, sem_wo, sem_made = list(it)
    deep = wq.shape[0] // DEPTH_CHUNKS
    blocks = key_wide.shape[0] - 1
    stride = blocks + GROUP

    key_copy = pltpu.make_async_copy(key_wide, key_s, sem_k.at[0])
    val_copy = pltpu.make_async_copy(cache.at[:, pl.ds(HEAD, HEAD)], val_s, sem_k.at[1])
    if pieces:
        x_copies, tab_copies = [], []
        for i in range(pieces):
            span = spans[i]
            place = pl.ds(pl.multiple_of(ids[i] * TILE, TILE), rows[i])
            x_copies.append(pltpu.make_async_copy(xs[i], x_s.at[span], sem_in.at[i]))
            tab_copies.append(pltpu.make_async_copy(cos_tab.at[place], cos_s.at[span], sem_tab.at[2 * i]))
            tab_copies.append(pltpu.make_async_copy(sin_tab.at[place], sin_s.at[span], sem_tab.at[2 * i + 1]))
        for copy in x_copies:
            copy.start()
        w_copies = []
        for j in range(DEPTH_CHUNKS):
            span = pl.ds(j * deep, deep)
            w_copies.append(pltpu.make_async_copy(wq.at[span], w_s.at[span, pl.ds(0, width)], sem_w.at[2 * j]))
            w_copies.append(
                pltpu.make_async_copy(wkv.at[span], w_s.at[span, pl.ds(width, 2 * HEAD)], sem_w.at[2 * j + 1])
            )
        for copy in w_copies:
            copy.start()
        for copy in tab_copies:
            copy.start()
    count = ids[PIECES_MOST]

    def load_cache():
        @pl.when(count > 0)
        def _():
            key_copy.start()
            val_copy.start()

    if not pieces:
        load_cache()
    else:
        gains = gain[...]
        for i in range(pieces):
            x_copies[i].wait()

        def norm_rows(r, carry):
            span = pl.ds(pl.multiple_of(r * 16, 16), 16)
            values = x_s[span, :].astype(jnp.float32)
            mean_square = jnp.mean(values * values, axis=-1, keepdims=True)
            xn_s[span, :] = (values * lax.rsqrt(mean_square + EPS) * gains).astype(jnp.bfloat16)
            return carry

        lax.fori_loop(0, total // 16, norm_rows, 0, unroll=4)
        load_cache()
        for copy in tab_copies:
            copy.wait()
        cosine, sine = cos_s[...], sin_s[...]

        def rotate(v):
            return (v * cosine + pltpu.roll(v, HEAD // 2, 1) * sine).astype(jnp.bfloat16)

        made = None
        for j in range(DEPTH_CHUNKS):
            w_copies[2 * j].wait()
            w_copies[2 * j + 1].wait()
            span = slice(j * deep, (j + 1) * deep)
            more = jnp.dot(xn_s[:, span], w_s[span, :], preferred_element_type=jnp.float32)
            made = more if made is None else made + more
        for h in range(heads):
            qo_s[h] = rotate(made[:, h * HEAD:(h + 1) * HEAD])
        kvo_s[:, :HEAD] = rotate(made[:, width:width + HEAD])
        kvo_s[:, HEAD:] = made[:, width + HEAD:].astype(jnp.bfloat16)
        outs = []
        for i in range(pieces):
            span = spans[i]
            place = pl.ds(pl.multiple_of(ids[i] * TILE, TILE), rows[i])
            outs.append(pltpu.make_async_copy(qo_s.at[:, span], qb.at[:, place], sem_out.at[2 * i]))
            outs.append(pltpu.make_async_copy(kvo_s.at[span], kvb.at[place], sem_out.at[2 * i + 1]))
        for copy in outs:
            copy.start()
        for copy in outs:
            copy.wait()

    if sending:
        term_copies = weight_copies(w_out, wo_s, sem_wo)
        for copy in term_copies:
            copy.start()
    factor = math.log2(math.e) / math.sqrt(HEAD)

    def fetches(i, slot):
        tile = ids[HEADER + i]
        at = pl.multiple_of(tile * TILE, TILE)
        before = pl.multiple_of(jnp.maximum(tile - 1, 0) * TILE, TILE)
        return [
            pltpu.make_async_copy(qb.at[:, pl.ds(at, TILE)], qt_s.at[slot], sem_tile.at[slot, 0]),
            pltpu.make_async_copy(kvb.at[pl.ds(before, 2 * TILE)], kvt_s.at[slot], sem_tile.at[slot, 1]),
            pltpu.make_async_copy(doc_bias.at[pl.ds(at, TILE)], db_s.at[slot], sem_tile.at[slot, 2]),
            pltpu.make_async_copy(own_bias.at[pl.ds(at, TILE)], ob_s.at[slot], sem_tile.at[slot, 3]),
        ]

    def att_copy(i):
        at = pl.multiple_of(ids[HEADER + i] * TILE, TILE)
        return pltpu.make_async_copy(at_s, att.at[pl.ds(at, TILE)], sem_att)

    @pl.when(count > 0)
    def _():
        for copy in fetches(0, 0):
            copy.start()
        key_copy.wait()
        val_copy.wait()

    contract_last = (((1,), (1,)), ((), ()))

    def one_tile(i, carry):
        slot = lax.rem(i, 2)

        @pl.when(i + 1 < count)
        def _():
            for copy in fetches(i + 1, 1 - slot):
                copy.start()

        for copy in fetches(i, slot):
            copy.wait()
        tile = ids[HEADER + i]
        needed = lists[tile * stride]
        for h in range(heads):
            wide_s[h * TILE:(h + 1) * TILE, :HEAD] = qt_s[slot, h]
            wide_s[h * TILE:(h + 1) * TILE, HEAD:] = db_s[slot]
        own = lax.dot_general(
            wide_s[:, :HEAD], kvt_s[slot, :, :HEAD], contract_last, preferred_element_type=jnp.float32
        )
        own = (own.reshape(heads, TILE, HEAD) + ob_s[slot][None]).reshape(heads * TILE, HEAD)
        own_s[...] = own

        def attend(groups):
            listed = [lists[tile * stride + 1 + j] for j in range(groups * GROUP)]
            top = own_s[...]
            for g in range(groups):
                keys = jnp.concatenate([key_s[block] for block in listed[g * GROUP:(g + 1) * GROUP]], axis=1)
                scores = jnp.dot(wide_s[...], keys, preferred_element_type=jnp.float32)
                sc_s[g] = scores
                for c in range(0, GROUP * KEY_BLOCK, HEAD):
                    top = jnp.maximum(top, scores[:, c:c + HEAD])
            top = jnp.max(top, axis=1, keepdims=True) * factor
            weights = jnp.exp2(own_s[...] * factor - top)
            sums = weights
            made = [jnp.dot(weights.astype(jnp.bfloat16), kvt_s[slot, :, HEAD:], preferred_element_type=jnp.float32)]
            made += [None] * (GROUP - 1)
            for j, block in enumerate(listed):
                at = pl.multiple_of(jnp.minimum(block, blocks - 1) * KEY_BLOCK, KEY_BLOCK)
                c = j % GROUP * KEY_BLOCK
                weights = jnp.exp2(sc_s[j // GROUP, :, c:c + KEY_BLOCK] * factor - top)
                sums = sums + (weights[:, :HEAD] + weights[:, HEAD:])
                more = jnp.dot(
                    weights.astype(jnp.bfloat16), val_s[pl.ds(at, KEY_BLOCK), :], preferred_element_type=jnp.float32
                )
                made[j % GROUP] = more if made[j % GROUP] is None else made[j % GROUP] + more
            made = (made[0] + made[1]) + (made[2] + made[3])
            o_s[...] = (made / jnp.sum(sums, axis=1, keepdims=True)).astype(jnp.bfloat16)

        for groups in range(1, blocks // GROUP + 1):

            @pl.when(needed == groups)
            def _(groups=groups):
                attend(groups)

        @pl.when(i > 0)
        def _():
            att_copy(i - 1).wait()

        for h in range(heads):
            at_s[:, h * HEAD:(h + 1) * HEAD] = o_s[h * TILE:(h + 1) * TILE]
        att_copy(i).start()
        return carry

    lax.fori_loop(0, count, one_tile, 0)

    @pl.when(count > 0)
    def _():
        att_copy(count - 1).wait()

    if sending:
        places = [ids[PIECES_MOST + 1], ids[PIECES_MOST + 2]]
        write_terms(places, att, term_copies, terms, rows_s, wo_s, made_s, sem_rows, sem_made)


def run_step(ids, lists, xs, fixed, state, dims, w_out=None):
    tokens, heads, prefix, depth = dims
    pieces = len(xs)
    rows = [x.shape[0] for x in xs]
    total = max(sum(rows), 16)
    width = heads * HEAD
    any_spec = pl.BlockSpec(memory_space=pl.ANY)
    vmem_spec = pl.BlockSpec(memory_space=pltpu.VMEM)
    operands = list(xs) + list(fixed)
    specs = [any_spec] * pieces + [vmem_spec] + [any_spec] * (len(fixed) - 1)
    aliases = {}
    if state is not None:
        aliases = {2 + len(operands) + i: i for i in range(3)}
        operands += list(state)
        specs += [any_spec] * 3
    sending = w_out is not None
    if sending:
        operands.append(w_out)
        specs.append(any_spec)
    out_shape = [
        jax.ShapeDtypeStruct((heads, tokens, HEAD), jnp.bfloat16),
        jax.ShapeDtypeStruct((tokens, 2 * HEAD), jnp.bfloat16),
        jax.ShapeDtypeStruct((tokens, width), jnp.bfloat16),
    ]
    if sending:
        out_shape += [jax.ShapeDtypeStruct((TILE, w_out.shape[1]), jnp.bfloat16)] * 2
    small = 16
    w_rows = depth if pieces else small
    scratch = [
        pltpu.VMEM((total, depth), jnp.bfloat16),
        pltpu.VMEM((total, depth), jnp.bfloat16),
        pltpu.VMEM((w_rows, width + 2 * HEAD), jnp.bfloat16),
        pltpu.VMEM((total, HEAD), jnp.float32),
        pltpu.VMEM((total, HEAD), jnp.float32),
        pltpu.VMEM((heads, total, HEAD), jnp.bfloat16),
        pltpu.VMEM((total, 2 * HEAD), jnp.bfloat16),
        pltpu.VMEM((prefix // KEY_BLOCK + 1, 2 * HEAD, KEY_BLOCK), jnp.bfloat16),
        pltpu.VMEM((prefix, HEAD), jnp.bfloat16),
        pltpu.VMEM((2, heads, TILE, HEAD), jnp.bfloat16),
        pltpu.VMEM((2, 2 * TILE, 2 * HEAD), jnp.bfloat16),
        pltpu.VMEM((2, TILE, HEAD), jnp.bfloat16),
        pltpu.VMEM((2, TILE, HEAD), jnp.float32),
        pltpu.VMEM((prefix // KEY_BLOCK // GROUP, heads * TILE, GROUP * KEY_BLOCK), jnp.float32),
        pltpu.VMEM((TILE, width), jnp.bfloat16),
        pltpu.VMEM((heads * TILE, 2 * HEAD), jnp.bfloat16),
        pltpu.VMEM((heads * TILE, HEAD), jnp.float32),
        pltpu.VMEM((heads * TILE, HEAD), jnp.bfloat16),
        pltpu.SemaphoreType.DMA((max(pieces, 1),)),
        pltpu.SemaphoreType.DMA((2 * max(pieces, 1),)),
        pltpu.SemaphoreType.DMA((2 * DEPTH_CHUNKS,)),
        pltpu.SemaphoreType.DMA((2,)),
        pltpu.SemaphoreType.DMA((2 * max(pieces, 1),)),
        pltpu.SemaphoreType.DMA((2, 4)),
        pltpu.SemaphoreType.DMA,
    ]
    if sending:
        scratch += term_scratch(2, width, w_out.shape[1])
    return pl.pallas_call(
        functools.partial(step_kernel, rows, heads, state is None, sending),
        grid_spec=pltpu.PrefetchScalarGridSpec(
            num_scalar_prefetch=2,
            grid=(),
            in_specs=specs,
            out_specs=[any_spec] * len(out_shape),
            scratch_shapes=scratch,
        ),
        out_shape=out_shape,
        input_output_aliases=aliases,
        compiler_params=pltpu.CompilerParams(vmem_limit_bytes=VMEM_LIMIT_FIRST if state is None else VMEM_LIMIT),
        cost_estimate=pl.CostEstimate(flops=1 << 20, bytes_accessed=1 << 16, transcendentals=0),
    )(ids, lists, *operands)


def weight_copies(w_out, w_s, sem_w):
    columns = w_out.shape[1] // COLUMN_CHUNKS
    spans = [pl.ds(c * columns, columns) for c in range(COLUMN_CHUNKS)]
    return [pltpu.make_async_copy(w_out.at[:, span], w_s.at[:, span], sem_w.at[c]) for c, span in enumerate(spans)]


def write_terms(places, att, w_copies, outs, rows_s, w_s, made_s, sem_rows, sem_out):
    columns = w_s.shape[1] // COLUMN_CHUNKS
    row_copies = [
        pltpu.make_async_copy(
            att.at[pl.ds(pl.multiple_of(place * TILE, TILE), TILE)], rows_s.at[pl.ds(i * TILE, TILE)], sem_rows.at[i]
        )
        for i, place in enumerate(places)
    ]
    for copy in row_copies:
        copy.start()
    for copy in row_copies:
        copy.wait()
    out_copies = []
    for c in range(COLUMN_CHUNKS):
        span = pl.ds(c * columns, columns)
        w_copies[c].wait()
        made = jnp.dot(rows_s[...], w_s[:, span], preferred_element_type=jnp.float32)
        made_s[:, span] = made.astype(jnp.bfloat16)
        for i in range(len(places)):
            copy = pltpu.make_async_copy(
                made_s.at[pl.ds(i * TILE, TILE), span], outs[i].at[:, span], sem_out.at[i, c]
            )
            copy.start()
            out_copies.append(copy)
    for copy in out_copies:
        copy.wait()


def term_scratch(count, width, columns):
    return [
        pltpu.VMEM((count * TILE, width), jnp.bfloat16),
        pltpu.VMEM((width, columns), jnp.bfloat16),
        pltpu.VMEM((count * TILE, columns), jnp.bfloat16),
        pltpu.SemaphoreType.DMA((count,)),
        pltpu.SemaphoreType.DMA((COLUMN_CHUNKS,)),
        pltpu.SemaphoreType.DMA((count, COLUMN_CHUNKS)),
    ]


def product_kernel(count, ids, att, w_out, *refs):
    rows_s, w_s, made_s, sem_rows, sem_w, sem_out = refs[count:]
    copies = weight_copies(w_out, w_s, sem_w)
    for copy in copies:
        copy.start()
    places = [ids[i] for i in range(count)]
    write_terms(places, att, copies, refs[:count], rows_s, w_s, made_s, sem_rows, sem_out)


def product(ids, count, att, w_out):
    width, columns = w_out.shape
    any_spec = pl.BlockSpec(memory_space=pl.ANY)
    return pl.pallas_call(
        functools.partial(product_kernel, count),
        grid_spec=pltpu.PrefetchScalarGridSpec(
            num_scalar_prefetch=1,
            grid=(),
            in_specs=[any_spec] * 2,
            out_specs=[any_spec] * count,
            scratch_shapes=term_scratch(count, width, columns),
        ),
        out_shape=[jax.ShapeDtypeStruct((TILE, columns), jnp.bfloat16)] * count,
        compiler_params=pltpu.CompilerParams(vmem_limit_bytes=VMEM_LIMIT),
        cost_estimate=pl.CostEstimate(flops=1 << 20, bytes_accessed=1 << 16, transcendentals=0),
    )(ids, att, w_out)


def tables(seg_ids, seg_doc, doc_lens, prefix, cache):
    tokens = seg_ids.shape[0]
    tiles = tokens // TILE
    blocks = prefix // KEY_BLOCK
    docs = doc_lens.shape[0]
    order = jnp.arange(tokens, dtype=jnp.int32)
    start = jnp.sum((seg_ids[None, :] < seg_ids[:, None]).astype(jnp.int32), axis=1, dtype=jnp.int32)
    positions = prefix + order - start
    segments = jnp.arange(seg_doc.shape[0], dtype=jnp.int32)
    tok_doc = jnp.sum(
        jnp.where(seg_ids[:, None] == segments[None, :], seg_doc[None, :], 0), axis=1, dtype=jnp.int32
    )
    doc_list = jnp.arange(docs, dtype=jnp.int32)
    doc_ends = jnp.sum(jnp.where(doc_list[None, :] <= doc_list[:, None], doc_lens[None, :], 0), axis=1)
    doc_starts = doc_ends - doc_lens
    lanes = jnp.arange(HEAD, dtype=jnp.int32)
    half = HEAD // 2
    inverse = ROPE_THETA ** (-(jnp.arange(half, dtype=jnp.float32) * 2.0 / HEAD))
    inverse = jnp.concatenate([inverse, inverse])
    angles = positions.astype(jnp.float32)[:, None] * inverse[None, :]
    cosine = jnp.cos(angles)
    sine = jnp.sin(angles) * jnp.where(lanes < half, -1.0, 1.0)[None, :]
    doc_bias = jnp.where(lanes[None, :] == tok_doc[:, None], 0.0, MASKED).astype(jnp.bfloat16)
    spot = jnp.arange(prefix + KEY_BLOCK, dtype=jnp.int32).reshape(blocks + 1, 1, KEY_BLOCK)
    low = jnp.pad(doc_starts, (0, HEAD - docs), constant_values=prefix).reshape(1, HEAD, 1)
    high = jnp.pad(doc_ends, (0, HEAD - docs), constant_values=prefix + KEY_BLOCK).reshape(1, HEAD, 1)
    one_hot = ((spot >= low) & (spot < high)).astype(jnp.bfloat16)
    by_block = cache[:, :HEAD].reshape(blocks, KEY_BLOCK, HEAD).transpose(0, 2, 1)
    key_wide = jnp.concatenate([jnp.pad(by_block, ((0, 1), (0, 0), (0, 0))), one_hot], axis=1)
    first_key = jnp.maximum(jnp.arange(tiles, dtype=jnp.int32) - 1, 0) * TILE
    spots = first_key[:, None] + lanes[None, :]
    by_tile = seg_ids.reshape(tiles, TILE)
    earlier = jnp.concatenate([by_tile[:1], by_tile[:-1]], axis=0)
    later = jnp.concatenate([by_tile[1:2], by_tile[1:]], axis=0)
    window_seg = jnp.concatenate([earlier, later], axis=1)
    ok = (window_seg[:, None, :] == by_tile[:, :, None]) & (
        spots[:, None, :] <= order.reshape(tiles, TILE)[:, :, None]
    )
    own_bias = jnp.where(ok, 0.0, MASKED).astype(jnp.float32).reshape(tokens, HEAD)
    present = jnp.any(tok_doc.reshape(tiles, TILE)[:, :, None] == doc_list[None, None, :], axis=1)
    edge = jnp.arange(blocks, dtype=jnp.int32) * KEY_BLOCK
    overlap = (doc_starts[:, None] < edge[None, :] + KEY_BLOCK) & (doc_ends[:, None] > edge[None, :])
    flags = jnp.any(present[:, :, None] & overlap[None, :, :], axis=1).astype(jnp.int32)
    block_ids = jnp.arange(blocks, dtype=jnp.int32)
    rank = jnp.sum(jnp.where(block_ids[None, :, None] > block_ids[None, None, :], flags[:, None, :], 0), axis=2)
    listed = jnp.sum(
        jnp.where((rank[:, :, None] == block_ids[None, None, :]) & (flags[:, :, None] > 0), block_ids[None, :, None], 0),
        axis=1,
    )
    count = jnp.sum(flags, axis=1, keepdims=True)
    listed = jnp.where(block_ids[None, :] < count, listed, blocks)
    groups = (count + GROUP - 1) // GROUP
    lists = jnp.pad(jnp.concatenate([groups, listed], axis=1), ((0, 0), (0, GROUP - 1)))
    lists = lists.astype(jnp.int32).reshape(-1)
    return cosine, sine, key_wide, doc_bias, own_bias, lists


def local(
    hidden_in, norm_gain, w_query, keyvalue_weight, w_out, prefix_keyvalue_cache, seg_ids, seg_doc, doc_lens
):
    size = lax.axis_size("tensor")
    tokens = seg_ids.shape[0]
    prefix = prefix_keyvalue_cache.shape[0]
    chunk_rows, depth = hidden_in.shape
    heads = w_query.shape[1] // HEAD
    order = ring_order(size)
    half = size // 2
    rank = lax.axis_index("tensor")

    forward_pairs = [(order[i], order[(i + 1) % size]) for i in range(size)]
    backward_pairs = [(b, a) for a, b in forward_pairs]

    def forward(x):
        return lax.ppermute(x, "tensor", forward_pairs)

    def backward(x):
        return lax.ppermute(x, "tensor", backward_pairs)

    if keyvalue_weight.shape[1] == HEAD:
        swap = [(i, i ^ 1) for i in range(size)]
        even = rank % 2 == 0
        other_weight, other_cache = lax.ppermute((keyvalue_weight, prefix_keyvalue_cache), "tensor", swap)
        keyvalue_weight = jnp.concatenate(
            [jnp.where(even, keyvalue_weight, other_weight), jnp.where(even, other_weight, keyvalue_weight)], axis=1
        )
        prefix_keyvalue_cache = jnp.concatenate(
            [
                jnp.where(even, prefix_keyvalue_cache, other_cache),
                jnp.where(even, other_cache, prefix_keyvalue_cache),
            ],
            axis=1,
        )

    place = {r: i for i, r in enumerate(order)}
    flips = np.zeros((size,), np.int32)
    for r in range(size):
        flips[r] = int(order[(place[r] - 1) % size] == r - 1)
    sends = np.zeros((size, half + 1, 6), np.int32)
    for r in range(size):
        for d in range(half + 1):
            ahead, back = order[(place[r] + d) % size], order[(place[r] - d) % size]
            late = [2 * ahead + flips[ahead], 2 * back + 1 - flips[back]]
            sends[r, d] = late + [2 * ahead + 1 - flips[ahead], 2 * back + flips[back], 2 * r, 2 * r + 1]
    tiles = tile_plan(order, sends)
    most = max(len(call) for calls in tiles for call in calls)
    plan = np.zeros((size, size, HEADER + most), np.int32)
    for r in range(size):
        for call in range(size):
            d = min(call, half - 1) if call <= half else half
            back, ahead = 2 * order[(place[r] - d) % size], 2 * order[(place[r] + d) % size]
            parts = [back, ahead + 1, back + 1, ahead, 0]
            if call == 1:
                parts = [2 * r] + parts[:4]
            elif call == half:
                parts = [back + 1, ahead, 0, 0, 0]
            terms = sends[r, half, :2] if call == half + 1 else sends[r, half - 1, 2:4]
            row = parts + [len(tiles[r][call])] + [int(i) for i in terms] + tiles[r][call]
            plan[r, call, :len(row)] = row
    my_plan = jnp.asarray(plan)[rank]
    my_sends = jnp.asarray(sends)[rank]
    flipped = jnp.asarray(flips)[rank] > 0

    cosine, sine, key_wide, doc_bias, own_bias, lists = tables(
        seg_ids, seg_doc, doc_lens, prefix, prefix_keyvalue_cache
    )
    gain = norm_gain.astype(jnp.float32).reshape(1, depth)
    fixed = (gain, w_query, keyvalue_weight, cosine, sine, key_wide, prefix_keyvalue_cache, doc_bias, own_bias)
    dims = (tokens, heads, prefix, depth)

    def pass_on(pair):
        return forward(pair[0]), backward(pair[1])

    def add(pair, arrived):
        return tuple((a.astype(jnp.float32) + b.astype(jnp.float32)).astype(jnp.bfloat16) for a, b in zip(pair, arrived))

    def step(call, parts, state):
        return tuple(run_step(my_plan[call], lists, parts, fixed, state, dims))

    def step_and_send(call, parts, state):
        made = tuple(run_step(my_plan[call], lists, parts, fixed, state, dims, w_out))
        return made[:3], made[3:]

    first = pass_on((hidden_in[:TILE], hidden_in[TILE:]))
    second = pass_on((hidden_in[TILE:], hidden_in[:TILE]))
    state = None
    for distance in range(1, half - 1):
        first, state = lax.optimization_barrier((first, state))
        first_on = pass_on(first)
        second, state = lax.optimization_barrier((second, state))
        second_on = pass_on(second)
        state = step(distance, ((hidden_in,) if distance == 1 else ()) + first + second, state)
        first, second = first_on, second_on
    first, state = lax.optimization_barrier((first, state))
    last = pass_on(first)
    state = step(half - 1, first, state)
    second, state = lax.optimization_barrier((second, state))
    state, made = step_and_send(half, second, state)
    made, last, state = lax.optimization_barrier((made, last, state))
    early = pass_on(made)
    state, made = step_and_send(half + 1, last, state)
    far = pass_on(made)
    for distance in range(half - 1, 0, -1):
        near = distance - 1
        if near > 0:
            made, state = lax.optimization_barrier((made, state))
            ahead = tuple(product(my_sends[near, 2:4], 2, state[2], w_out))
            early, ahead = lax.optimization_barrier((early, ahead))
            made = add(ahead, early)
            early = pass_on(made)
            made, state = lax.optimization_barrier((made, state))
            state = step(size - near, [], state)
        else:
            early, made, state = lax.optimization_barrier((early, made, state))
        late = product(my_sends[distance], 2 if near > 0 else 6, state[2], w_out)
        own, late = late[4:], tuple(late[:2])
        far, late = lax.optimization_barrier((far, late))
        made = add(late, far)
        far = pass_on(made)
    wide = [[part.astype(jnp.float32) for part in pair] for pair in (early, far)]
    with_far, with_early = wide[1][0] + wide[0][1], wide[0][0] + wide[1][1]
    halves = [jnp.where(flipped, with_early, with_far), jnp.where(flipped, with_far, with_early)]
    summed = jnp.concatenate([halves[i] + own[i].astype(jnp.float32) for i in range(2)], axis=0)
    return (hidden_in.astype(jnp.float32) + summed).astype(jnp.bfloat16)


def solution(mesh):
    return jax.shard_map(
        local,
        mesh=mesh,
        in_specs=(
            P(("dp", "tensor"), None),
            P(),
            P(None, "tensor"),
            P(None, "tensor"),
            P("tensor", None),
            P(None, "tensor"),
            P("dp"),
            P("dp"),
            P(),
        ),
        out_specs=P(("dp", "tensor"), None),
        check_vma=False,
    )
```

```python
import functools
import math

import jax
import jax.numpy as jnp
import numpy as np
from jax import lax
from jax.experimental import pallas as pl
from jax.experimental.pallas import tpu as pltpu
from jax.sharding import PartitionSpec as P

HEAD = 128
TILE = 64
KEY_BLOCK = 256
GROUP = 4
DEPTH_CHUNKS = 4
COLUMN_CHUNKS = 4
PIECES_MOST = 4
HEADER = PIECES_MOST + 3
MASKED = -1e30
EPS = 1e-05
ROPE_THETA = 500000.0
VMEM_LIMIT = 32 * 1024 * 1024


def ring_order(size):
    zs = 4 if size % 8 == 0 else 1
    ys = size // zs
    if zs == 1:
        return list(range(size))
    cycle = [(0, 0)]
    for y in range(ys):
        column = range(1, zs) if y % 2 == 0 else range(zs - 1, 0, -1)
        cycle += [(z, y) for z in column]
    cycle += [(0, y) for y in range(ys - 1, 0, -1)]
    return [z * ys + y for z, y in cycle]


def tile_plan(order, sends):
    size = len(order)
    half = size // 2
    place = {r: i for i, r in enumerate(order)}
    spare = [0] + [6] * (half - 3) + [1, 2] + [0] * (size - half)
    plans = []
    for rank in range(size):
        arrival, due = {}, {}
        for chunk in range(size):
            behind = (place[rank] - place[chunk]) % size
            distance = min(behind, size - behind)
            for upper in range(2):
                arrival[chunk, upper] = distance
                if distance == half:
                    arrival[chunk, upper] = half + 1
                elif distance == half - 1:
                    arrival[chunk, upper] = half - 1 if upper == int(behind != distance) else half
        for d in range(half + 1):
            for i, row in enumerate(sends[rank, d]):
                if i >= 4:
                    when = size - 1
                elif i >= 2 and 0 < d < half:
                    when = {half - 1: half, half - 2: half + 1}.get(d, size - d - 1)
                elif i < 2 and d > 0:
                    when = half + 1 if d == half else size - max(d - 1, 1)
                else:
                    continue
                due[int(row) // 2, int(row) % 2] = when
        ready = {}
        for chunk in range(size):
            ready[chunk, 1] = max(arrival[chunk, 0], arrival[chunk, 1])
            ready[chunk, 0] = max(arrival[chunk, 0], arrival[chunk - 1, 1]) if chunk else ready[chunk, 1]
        calls, left = [], set(ready)
        for call in range(size):
            able = sorted((due[t], t) for t in left if ready[t] <= call)
            must = [t for when, t in able if when <= call]
            more = [t for when, t in able if when > call][:max(spare[call] - len(must), 0)]
            calls.append([2 * chunk + upper for chunk, upper in must + more])
            left -= set(must + more)
        assert not left and all(ready[t] <= due[t] for t in ready)
        plans.append(calls)
    return plans


def step_kernel(pieces, rows, heads, sending, *refs):
    total = pieces * rows
    width = heads * HEAD
    it = iter(refs)
    ids, lists = next(it), next(it)
    xs = [next(it) for _ in range(pieces)]
    gain, wq, wkv, cos_tab, sin_tab, key_wide, cache, doc_bias, own_bias = [next(it) for _ in range(9)]
    first = pieces == 1 and rows == 128
    if not first:
        next(it), next(it), next(it)
    if sending:
        w_out = next(it)
    qb, kvb, att = next(it), next(it), next(it)
    if sending:
        terms = [next(it), next(it)]
    (x_s, xn_s, w_s, cos_s, sin_s, qo_s, kvo_s, key_s, val_s, qt_s, kvt_s, db_s, ob_s, sc_s, at_s,
     wide_s, own_s, o_s, sem_in, sem_tab, sem_w, sem_k, sem_out, sem_tile, sem_att) = [next(it) for _ in range(25)]
    if sending:
        rows_s, wo_s, made_s, sem_rows, sem_wo, sem_made = list(it)
    deep = wq.shape[0] // DEPTH_CHUNKS
    blocks = key_wide.shape[0] - 1
    stride = blocks + GROUP

    key_copy = pltpu.make_async_copy(key_wide, key_s, sem_k.at[0])
    val_copy = pltpu.make_async_copy(cache.at[:, pl.ds(HEAD, HEAD)], val_s, sem_k.at[1])
    if pieces:
        x_copies, tab_copies = [], []
        for i in range(pieces):
            span = pl.ds(i * rows, rows)
            place = pl.ds(pl.multiple_of(ids[i] * TILE, TILE), rows)
            x_copies.append(pltpu.make_async_copy(xs[i], x_s.at[span], sem_in.at[i]))
            tab_copies.append(pltpu.make_async_copy(cos_tab.at[place], cos_s.at[span], sem_tab.at[2 * i]))
            tab_copies.append(pltpu.make_async_copy(sin_tab.at[place], sin_s.at[span], sem_tab.at[2 * i + 1]))
        for copy in x_copies:
            copy.start()
        w_copies = []
        for j in range(DEPTH_CHUNKS):
            span = pl.ds(j * deep, deep)
            w_copies.append(pltpu.make_async_copy(wq.at[span], w_s.at[span, pl.ds(0, width)], sem_w.at[2 * j]))
            w_copies.append(
                pltpu.make_async_copy(wkv.at[span], w_s.at[span, pl.ds(width, 2 * HEAD)], sem_w.at[2 * j + 1])
            )
        for copy in w_copies:
            copy.start()
        for copy in tab_copies:
            copy.start()
    count = ids[PIECES_MOST]

    def load_cache():
        @pl.when(count > 0)
        def _():
            key_copy.start()
            val_copy.start()

    if not pieces:
        load_cache()
    else:
        gains = gain[...]
        for i in range(pieces):
            x_copies[i].wait()

        def norm_rows(r, carry):
            span = pl.ds(pl.multiple_of(r * 16, 16), 16)
            values = x_s[span, :].astype(jnp.float32)
            mean_square = jnp.mean(values * values, axis=-1, keepdims=True)
            xn_s[span, :] = (values * lax.rsqrt(mean_square + EPS) * gains).astype(jnp.bfloat16)
            return carry

        lax.fori_loop(0, total // 16, norm_rows, 0, unroll=4)
        load_cache()
        for copy in tab_copies:
            copy.wait()
        cosine, sine = cos_s[...], sin_s[...]

        def rotate(v):
            return (v * cosine + pltpu.roll(v, HEAD // 2, 1) * sine).astype(jnp.bfloat16)

        made = None
        for j in range(DEPTH_CHUNKS):
            w_copies[2 * j].wait()
            w_copies[2 * j + 1].wait()
            span = slice(j * deep, (j + 1) * deep)
            more = jnp.dot(xn_s[:, span], w_s[span, :], preferred_element_type=jnp.float32)
            made = more if made is None else made + more
        for h in range(heads):
            qo_s[h] = rotate(made[:, h * HEAD:(h + 1) * HEAD])
        kvo_s[:, :HEAD] = rotate(made[:, width:width + HEAD])
        kvo_s[:, HEAD:] = made[:, width + HEAD:].astype(jnp.bfloat16)
        outs = []
        for i in range(pieces):
            span = pl.ds(i * rows, rows)
            place = pl.ds(pl.multiple_of(ids[i] * TILE, TILE), rows)
            outs.append(pltpu.make_async_copy(qo_s.at[:, span], qb.at[:, place], sem_out.at[2 * i]))
            outs.append(pltpu.make_async_copy(kvo_s.at[span], kvb.at[place], sem_out.at[2 * i + 1]))
        for copy in outs:
            copy.start()
        for copy in outs:
            copy.wait()

    if sending:
        term_copies = weight_copies(w_out, wo_s, sem_wo)
        for copy in term_copies:
            copy.start()
    factor = math.log2(math.e) / math.sqrt(HEAD)

    def fetches(i, slot):
        tile = ids[HEADER + i]
        at = pl.multiple_of(tile * TILE, TILE)
        before = pl.multiple_of(jnp.maximum(tile - 1, 0) * TILE, TILE)
        return [
            pltpu.make_async_copy(qb.at[:, pl.ds(at, TILE)], qt_s.at[slot], sem_tile.at[slot, 0]),
            pltpu.make_async_copy(kvb.at[pl.ds(before, 2 * TILE)], kvt_s.at[slot], sem_tile.at[slot, 1]),
            pltpu.make_async_copy(doc_bias.at[pl.ds(at, TILE)], db_s.at[slot], sem_tile.at[slot, 2]),
            pltpu.make_async_copy(own_bias.at[pl.ds(at, TILE)], ob_s.at[slot], sem_tile.at[slot, 3]),
        ]

    def att_copy(i):
        at = pl.multiple_of(ids[HEADER + i] * TILE, TILE)
        return pltpu.make_async_copy(at_s, att.at[pl.ds(at, TILE)], sem_att)

    @pl.when(count > 0)
    def _():
        for copy in fetches(0, 0):
            copy.start()
        key_copy.wait()
        val_copy.wait()

    contract_last = (((1,), (1,)), ((), ()))

    def one_tile(i, carry):
        slot = lax.rem(i, 2)

        @pl.when(i + 1 < count)
        def _():
            for copy in fetches(i + 1, 1 - slot):
                copy.start()

        for copy in fetches(i, slot):
            copy.wait()
        tile = ids[HEADER + i]
        needed = lists[tile * stride]
        for h in range(heads):
            wide_s[h * TILE:(h + 1) * TILE, :HEAD] = qt_s[slot, h]
            wide_s[h * TILE:(h + 1) * TILE, HEAD:] = db_s[slot]
        own = lax.dot_general(
            wide_s[:, :HEAD], kvt_s[slot, :, :HEAD], contract_last, preferred_element_type=jnp.float32
        )
        own = (own.reshape(heads, TILE, HEAD) + ob_s[slot][None]).reshape(heads * TILE, HEAD)
        own_s[...] = own

        def attend(groups):
            listed = [lists[tile * stride + 1 + j] for j in range(groups * GROUP)]
            top = own_s[...]
            for g in range(groups):
                keys = jnp.concatenate([key_s[block] for block in listed[g * GROUP:(g + 1) * GROUP]], axis=1)
                scores = jnp.dot(wide_s[...], keys, preferred_element_type=jnp.float32)
                sc_s[g] = scores
                for c in range(0, GROUP * KEY_BLOCK, HEAD):
                    top = jnp.maximum(top, scores[:, c:c + HEAD])
            top = jnp.max(top, axis=1, keepdims=True) * factor
            weights = jnp.exp2(own_s[...] * factor - top)
            sums = weights
            made = [jnp.dot(weights.astype(jnp.bfloat16), kvt_s[slot, :, HEAD:], preferred_element_type=jnp.float32)]
            made += [None] * (GROUP - 1)
            for j, block in enumerate(listed):
                at = pl.multiple_of(jnp.minimum(block, blocks - 1) * KEY_BLOCK, KEY_BLOCK)
                c = j % GROUP * KEY_BLOCK
                weights = jnp.exp2(sc_s[j // GROUP, :, c:c + KEY_BLOCK] * factor - top)
                sums = sums + (weights[:, :HEAD] + weights[:, HEAD:])
                more = jnp.dot(
                    weights.astype(jnp.bfloat16), val_s[pl.ds(at, KEY_BLOCK), :], preferred_element_type=jnp.float32
                )
                made[j % GROUP] = more if made[j % GROUP] is None else made[j % GROUP] + more
            made = (made[0] + made[1]) + (made[2] + made[3])
            o_s[...] = (made / jnp.sum(sums, axis=1, keepdims=True)).astype(jnp.bfloat16)

        for groups in range(1, blocks // GROUP + 1):

            @pl.when(needed == groups)
            def _(groups=groups):
                attend(groups)

        @pl.when(i > 0)
        def _():
            att_copy(i - 1).wait()

        for h in range(heads):
            at_s[:, h * HEAD:(h + 1) * HEAD] = o_s[h * TILE:(h + 1) * TILE]
        att_copy(i).start()
        return carry

    lax.fori_loop(0, count, one_tile, 0)

    @pl.when(count > 0)
    def _():
        att_copy(count - 1).wait()

    if sending:
        places = [ids[PIECES_MOST + 1], ids[PIECES_MOST + 2]]
        write_terms(places, att, term_copies, terms, rows_s, wo_s, made_s, sem_rows, sem_made)


def run_step(ids, lists, xs, fixed, state, dims, w_out=None):
    tokens, heads, prefix, depth = dims
    pieces = len(xs)
    rows = xs[0].shape[0] if pieces else TILE
    total = max(pieces * rows, 16)
    width = heads * HEAD
    any_spec = pl.BlockSpec(memory_space=pl.ANY)
    vmem_spec = pl.BlockSpec(memory_space=pltpu.VMEM)
    operands = list(xs) + list(fixed)
    specs = [any_spec] * pieces + [vmem_spec] + [any_spec] * (len(fixed) - 1)
    aliases = {}
    if state is not None:
        aliases = {2 + len(operands) + i: i for i in range(3)}
        operands += list(state)
        specs += [any_spec] * 3
    sending = w_out is not None
    if sending:
        operands.append(w_out)
        specs.append(any_spec)
    out_shape = [
        jax.ShapeDtypeStruct((heads, tokens, HEAD), jnp.bfloat16),
        jax.ShapeDtypeStruct((tokens, 2 * HEAD), jnp.bfloat16),
        jax.ShapeDtypeStruct((tokens, width), jnp.bfloat16),
    ]
    if sending:
        out_shape += [jax.ShapeDtypeStruct((TILE, w_out.shape[1]), jnp.bfloat16)] * 2
    small = 16
    w_rows = depth if pieces else small
    scratch = [
        pltpu.VMEM((total, depth), jnp.bfloat16),
        pltpu.VMEM((total, depth), jnp.bfloat16),
        pltpu.VMEM((w_rows, width + 2 * HEAD), jnp.bfloat16),
        pltpu.VMEM((total, HEAD), jnp.float32),
        pltpu.VMEM((total, HEAD), jnp.float32),
        pltpu.VMEM((heads, total, HEAD), jnp.bfloat16),
        pltpu.VMEM((total, 2 * HEAD), jnp.bfloat16),
        pltpu.VMEM((prefix // KEY_BLOCK + 1, 2 * HEAD, KEY_BLOCK), jnp.bfloat16),
        pltpu.VMEM((prefix, HEAD), jnp.bfloat16),
        pltpu.VMEM((2, heads, TILE, HEAD), jnp.bfloat16),
        pltpu.VMEM((2, 2 * TILE, 2 * HEAD), jnp.bfloat16),
        pltpu.VMEM((2, TILE, HEAD), jnp.bfloat16),
        pltpu.VMEM((2, TILE, HEAD), jnp.float32),
        pltpu.VMEM((prefix // KEY_BLOCK // GROUP, heads * TILE, GROUP * KEY_BLOCK), jnp.float32),
        pltpu.VMEM((TILE, width), jnp.bfloat16),
        pltpu.VMEM((heads * TILE, 2 * HEAD), jnp.bfloat16),
        pltpu.VMEM((heads * TILE, HEAD), jnp.float32),
        pltpu.VMEM((heads * TILE, HEAD), jnp.bfloat16),
        pltpu.SemaphoreType.DMA((max(pieces, 1),)),
        pltpu.SemaphoreType.DMA((2 * max(pieces, 1),)),
        pltpu.SemaphoreType.DMA((2 * DEPTH_CHUNKS,)),
        pltpu.SemaphoreType.DMA((2,)),
        pltpu.SemaphoreType.DMA((2 * max(pieces, 1),)),
        pltpu.SemaphoreType.DMA((2, 4)),
        pltpu.SemaphoreType.DMA,
    ]
    if sending:
        scratch += term_scratch(2, width, w_out.shape[1])
    return pl.pallas_call(
        functools.partial(step_kernel, pieces, rows, heads, sending),
        grid_spec=pltpu.PrefetchScalarGridSpec(
            num_scalar_prefetch=2,
            grid=(),
            in_specs=specs,
            out_specs=[any_spec] * len(out_shape),
            scratch_shapes=scratch,
        ),
        out_shape=out_shape,
        input_output_aliases=aliases,
        compiler_params=pltpu.CompilerParams(vmem_limit_bytes=VMEM_LIMIT),
        cost_estimate=pl.CostEstimate(flops=1 << 20, bytes_accessed=1 << 16, transcendentals=0),
    )(ids, lists, *operands)


def weight_copies(w_out, w_s, sem_w):
    columns = w_out.shape[1] // COLUMN_CHUNKS
    spans = [pl.ds(c * columns, columns) for c in range(COLUMN_CHUNKS)]
    return [pltpu.make_async_copy(w_out.at[:, span], w_s.at[:, span], sem_w.at[c]) for c, span in enumerate(spans)]


def write_terms(places, att, w_copies, outs, rows_s, w_s, made_s, sem_rows, sem_out):
    columns = w_s.shape[1] // COLUMN_CHUNKS
    row_copies = [
        pltpu.make_async_copy(
            att.at[pl.ds(pl.multiple_of(place * TILE, TILE), TILE)], rows_s.at[pl.ds(i * TILE, TILE)], sem_rows.at[i]
        )
        for i, place in enumerate(places)
    ]
    for copy in row_copies:
        copy.start()
    for copy in row_copies:
        copy.wait()
    out_copies = []
    for c in range(COLUMN_CHUNKS):
        span = pl.ds(c * columns, columns)
        w_copies[c].wait()
        made = jnp.dot(rows_s[...], w_s[:, span], preferred_element_type=jnp.float32)
        made_s[:, span] = made.astype(jnp.bfloat16)
        for i in range(len(places)):
            copy = pltpu.make_async_copy(
                made_s.at[pl.ds(i * TILE, TILE), span], outs[i].at[:, span], sem_out.at[i, c]
            )
            copy.start()
            out_copies.append(copy)
    for copy in out_copies:
        copy.wait()


def term_scratch(count, width, columns):
    return [
        pltpu.VMEM((count * TILE, width), jnp.bfloat16),
        pltpu.VMEM((width, columns), jnp.bfloat16),
        pltpu.VMEM((count * TILE, columns), jnp.bfloat16),
        pltpu.SemaphoreType.DMA((count,)),
        pltpu.SemaphoreType.DMA((COLUMN_CHUNKS,)),
        pltpu.SemaphoreType.DMA((count, COLUMN_CHUNKS)),
    ]


def product_kernel(count, ids, att, w_out, *refs):
    rows_s, w_s, made_s, sem_rows, sem_w, sem_out = refs[count:]
    copies = weight_copies(w_out, w_s, sem_w)
    for copy in copies:
        copy.start()
    places = [ids[i] for i in range(count)]
    write_terms(places, att, copies, refs[:count], rows_s, w_s, made_s, sem_rows, sem_out)


def product(ids, count, att, w_out):
    width, columns = w_out.shape
    any_spec = pl.BlockSpec(memory_space=pl.ANY)
    return pl.pallas_call(
        functools.partial(product_kernel, count),
        grid_spec=pltpu.PrefetchScalarGridSpec(
            num_scalar_prefetch=1,
            grid=(),
            in_specs=[any_spec] * 2,
            out_specs=[any_spec] * count,
            scratch_shapes=term_scratch(count, width, columns),
        ),
        out_shape=[jax.ShapeDtypeStruct((TILE, columns), jnp.bfloat16)] * count,
        compiler_params=pltpu.CompilerParams(vmem_limit_bytes=VMEM_LIMIT),
        cost_estimate=pl.CostEstimate(flops=1 << 20, bytes_accessed=1 << 16, transcendentals=0),
    )(ids, att, w_out)


def tables(seg_ids, seg_doc, doc_lens, prefix, cache):
    tokens = seg_ids.shape[0]
    tiles = tokens // TILE
    blocks = prefix // KEY_BLOCK
    docs = doc_lens.shape[0]
    order = jnp.arange(tokens, dtype=jnp.int32)
    start = jnp.sum((seg_ids[None, :] < seg_ids[:, None]).astype(jnp.int32), axis=1, dtype=jnp.int32)
    positions = prefix + order - start
    segments = jnp.arange(seg_doc.shape[0], dtype=jnp.int32)
    tok_doc = jnp.sum(
        jnp.where(seg_ids[:, None] == segments[None, :], seg_doc[None, :], 0), axis=1, dtype=jnp.int32
    )
    doc_list = jnp.arange(docs, dtype=jnp.int32)
    doc_ends = jnp.sum(jnp.where(doc_list[None, :] <= doc_list[:, None], doc_lens[None, :], 0), axis=1)
    doc_starts = doc_ends - doc_lens
    lanes = jnp.arange(HEAD, dtype=jnp.int32)
    half = HEAD // 2
    inverse = ROPE_THETA ** (-(jnp.arange(half, dtype=jnp.float32) * 2.0 / HEAD))
    inverse = jnp.concatenate([inverse, inverse])
    angles = positions.astype(jnp.float32)[:, None] * inverse[None, :]
    cosine = jnp.cos(angles)
    sine = jnp.sin(angles) * jnp.where(lanes < half, -1.0, 1.0)[None, :]
    doc_bias = jnp.where(lanes[None, :] == tok_doc[:, None], 0.0, MASKED).astype(jnp.bfloat16)
    spot = jnp.arange(prefix + KEY_BLOCK, dtype=jnp.int32).reshape(blocks + 1, 1, KEY_BLOCK)
    low = jnp.pad(doc_starts, (0, HEAD - docs), constant_values=prefix).reshape(1, HEAD, 1)
    high = jnp.pad(doc_ends, (0, HEAD - docs), constant_values=prefix + KEY_BLOCK).reshape(1, HEAD, 1)
    one_hot = ((spot >= low) & (spot < high)).astype(jnp.bfloat16)
    by_block = cache[:, :HEAD].reshape(blocks, KEY_BLOCK, HEAD).transpose(0, 2, 1)
    key_wide = jnp.concatenate([jnp.pad(by_block, ((0, 1), (0, 0), (0, 0))), one_hot], axis=1)
    first_key = jnp.maximum(jnp.arange(tiles, dtype=jnp.int32) - 1, 0) * TILE
    spots = first_key[:, None] + lanes[None, :]
    by_tile = seg_ids.reshape(tiles, TILE)
    earlier = jnp.concatenate([by_tile[:1], by_tile[:-1]], axis=0)
    later = jnp.concatenate([by_tile[1:2], by_tile[1:]], axis=0)
    window_seg = jnp.concatenate([earlier, later], axis=1)
    ok = (window_seg[:, None, :] == by_tile[:, :, None]) & (
        spots[:, None, :] <= order.reshape(tiles, TILE)[:, :, None]
    )
    own_bias = jnp.where(ok, 0.0, MASKED).astype(jnp.float32).reshape(tokens, HEAD)
    present = jnp.any(tok_doc.reshape(tiles, TILE)[:, :, None] == doc_list[None, None, :], axis=1)
    edge = jnp.arange(blocks, dtype=jnp.int32) * KEY_BLOCK
    overlap = (doc_starts[:, None] < edge[None, :] + KEY_BLOCK) & (doc_ends[:, None] > edge[None, :])
    flags = jnp.any(present[:, :, None] & overlap[None, :, :], axis=1).astype(jnp.int32)
    block_ids = jnp.arange(blocks, dtype=jnp.int32)
    rank = jnp.sum(jnp.where(block_ids[None, :, None] > block_ids[None, None, :], flags[:, None, :], 0), axis=2)
    listed = jnp.sum(
        jnp.where((rank[:, :, None] == block_ids[None, None, :]) & (flags[:, :, None] > 0), block_ids[None, :, None], 0),
        axis=1,
    )
    count = jnp.sum(flags, axis=1, keepdims=True)
    listed = jnp.where(block_ids[None, :] < count, listed, blocks)
    groups = (count + GROUP - 1) // GROUP
    lists = jnp.pad(jnp.concatenate([groups, listed], axis=1), ((0, 0), (0, GROUP - 1)))
    lists = lists.astype(jnp.int32).reshape(-1)
    return cosine, sine, key_wide, doc_bias, own_bias, lists


def local(
    hidden_in, norm_gain, w_query, keyvalue_weight, w_out, prefix_keyvalue_cache, seg_ids, seg_doc, doc_lens
):
    size = lax.axis_size("tensor")
    tokens = seg_ids.shape[0]
    prefix = prefix_keyvalue_cache.shape[0]
    chunk_rows, depth = hidden_in.shape
    heads = w_query.shape[1] // HEAD
    order = ring_order(size)
    half = size // 2
    rank = lax.axis_index("tensor")

    forward_pairs = [(order[i], order[(i + 1) % size]) for i in range(size)]
    backward_pairs = [(b, a) for a, b in forward_pairs]

    def forward(x):
        return lax.ppermute(x, "tensor", forward_pairs)

    def backward(x):
        return lax.ppermute(x, "tensor", backward_pairs)

    if keyvalue_weight.shape[1] == HEAD:
        swap = [(i, i ^ 1) for i in range(size)]
        even = rank % 2 == 0
        other_weight, other_cache = lax.ppermute((keyvalue_weight, prefix_keyvalue_cache), "tensor", swap)
        keyvalue_weight = jnp.concatenate(
            [jnp.where(even, keyvalue_weight, other_weight), jnp.where(even, other_weight, keyvalue_weight)], axis=1
        )
        prefix_keyvalue_cache = jnp.concatenate(
            [
                jnp.where(even, prefix_keyvalue_cache, other_cache),
                jnp.where(even, other_cache, prefix_keyvalue_cache),
            ],
            axis=1,
        )

    place = {r: i for i, r in enumerate(order)}
    flips = np.zeros((size,), np.int32)
    for r in range(size):
        flips[r] = int(order[(place[r] - 1) % size] == r - 1)
    sends = np.zeros((size, half + 1, 6), np.int32)
    for r in range(size):
        for d in range(half + 1):
            ahead, back = order[(place[r] + d) % size], order[(place[r] - d) % size]
            late = [2 * ahead + flips[ahead], 2 * back + 1 - flips[back]]
            sends[r, d] = late + [2 * ahead + 1 - flips[ahead], 2 * back + flips[back], 2 * r, 2 * r + 1]
    tiles = tile_plan(order, sends)
    most = max(len(call) for calls in tiles for call in calls)
    plan = np.zeros((size, size, HEADER + most), np.int32)
    for r in range(size):
        for call in range(size):
            d = min(call, half - 1) if call <= half else half
            back, ahead = 2 * order[(place[r] - d) % size], 2 * order[(place[r] + d) % size]
            if call == half - 1 or call == half + 1:
                parts = [back, ahead + 1, 0, 0]
            elif call == half:
                parts = [back + 1, ahead, 0, 0]
            else:
                parts = [back, ahead, 0, 0]
            terms = sends[r, half, :2] if call == half + 1 else sends[r, half - 1, 2:4]
            row = parts + [len(tiles[r][call])] + [int(i) for i in terms] + tiles[r][call]
            plan[r, call, :len(row)] = row
    my_plan = jnp.asarray(plan)[rank]
    my_sends = jnp.asarray(sends)[rank]
    flipped = jnp.asarray(flips)[rank] > 0

    cosine, sine, key_wide, doc_bias, own_bias, lists = tables(
        seg_ids, seg_doc, doc_lens, prefix, prefix_keyvalue_cache
    )
    gain = norm_gain.astype(jnp.float32).reshape(1, depth)
    fixed = (gain, w_query, keyvalue_weight, cosine, sine, key_wide, prefix_keyvalue_cache, doc_bias, own_bias)
    dims = (tokens, heads, prefix, depth)

    def pass_on(pair):
        return forward(pair[0]), backward(pair[1])

    def add(pair, arrived):
        return tuple((a.astype(jnp.float32) + b.astype(jnp.float32)).astype(jnp.bfloat16) for a, b in zip(pair, arrived))

    def step(call, parts, state):
        return tuple(run_step(my_plan[call], lists, parts, fixed, state, dims))

    def step_and_send(call, parts, state):
        made = tuple(run_step(my_plan[call], lists, parts, fixed, state, dims, w_out))
        return made[:3], made[3:]

    def halves_of(pair):
        return (pair[0][:TILE], pair[1][TILE:]), (pair[0][TILE:], pair[1][:TILE])

    held = pass_on((hidden_in, hidden_in))
    state = step(0, [hidden_in], None)
    for distance in range(1, half - 2):
        held, state = lax.optimization_barrier((held, state))
        following = pass_on(held)
        state = step(distance, held, state)
        held = following
    held, state = lax.optimization_barrier((held, state))
    first, rest = halves_of(held)
    first = pass_on(first)
    state = step(half - 2, held, state)
    rest, state = lax.optimization_barrier((rest, state))
    second = pass_on(rest)
    first, state = lax.optimization_barrier((first, state))
    last = pass_on(first)
    state = step(half - 1, first, state)
    second, state = lax.optimization_barrier((second, state))
    state, made = step_and_send(half, second, state)
    made, last, state = lax.optimization_barrier((made, last, state))
    early = pass_on(made)
    state, made = step_and_send(half + 1, last, state)
    far = pass_on(made)
    for distance in range(half - 1, 0, -1):
        near = distance - 1
        if near > 0:
            made, state = lax.optimization_barrier((made, state))
            ahead = tuple(product(my_sends[near, 2:4], 2, state[2], w_out))
            early, ahead = lax.optimization_barrier((early, ahead))
            made = add(ahead, early)
            early = pass_on(made)
            made, state = lax.optimization_barrier((made, state))
            state = step(size - near, [], state)
        else:
            early, made, state = lax.optimization_barrier((early, made, state))
        late = product(my_sends[distance], 2 if near > 0 else 6, state[2], w_out)
        own, late = late[4:], tuple(late[:2])
        far, late = lax.optimization_barrier((far, late))
        made = add(late, far)
        far = pass_on(made)
    wide = [part.astype(jnp.float32) for part in early]
    own = [part.astype(jnp.float32) for part in own]
    base = (
        hidden_in[:TILE].astype(jnp.float32) + own[0] + jnp.where(flipped, wide[0], wide[1]),
        hidden_in[TILE:].astype(jnp.float32) + own[1] + jnp.where(flipped, wide[1], wide[0]),
    )
    base, far = lax.optimization_barrier((base, far))
    far = [part.astype(jnp.float32) for part in far]
    lower = base[0] + jnp.where(flipped, far[1], far[0])
    upper = base[1] + jnp.where(flipped, far[0], far[1])
    return jnp.concatenate([lower, upper], axis=0).astype(jnp.bfloat16)


def solution(mesh):
    return jax.shard_map(
        local,
        mesh=mesh,
        in_specs=(
            P(("dp", "tensor"), None),
            P(),
            P(None, "tensor"),
            P(None, "tensor"),
            P("tensor", None),
            P(None, "tensor"),
            P("dp"),
            P("dp"),
            P(),
        ),
        out_specs=P(("dp", "tensor"), None),
        check_vma=False,
    )
```

```python
import functools
import math

import jax
import jax.numpy as jnp
import numpy as np
from jax import lax
from jax.experimental import pallas as pl
from jax.experimental.pallas import tpu as pltpu
from jax.sharding import PartitionSpec as P

HEAD = 128
TILE = 64
KEY_BLOCK = 256
GROUP = 4
DEPTH_CHUNKS = 4
COLUMN_CHUNKS = 4
PIECES_MOST = 4
HEADER = PIECES_MOST + 3
MASKED = -1e30
EPS = 1e-05
ROPE_THETA = 500000.0
VMEM_LIMIT = 32 * 1024 * 1024


def ring_order(size):
    zs = 4 if size % 8 == 0 else 1
    ys = size // zs
    if zs == 1:
        return list(range(size))
    cycle = [(0, 0)]
    for y in range(ys):
        column = range(1, zs) if y % 2 == 0 else range(zs - 1, 0, -1)
        cycle += [(z, y) for z in column]
    cycle += [(0, y) for y in range(ys - 1, 0, -1)]
    return [z * ys + y for z, y in cycle]


def tile_plan(order, sends):
    size = len(order)
    half = size // 2
    place = {r: i for i, r in enumerate(order)}
    spare = [0] + [6] * (half - 3) + [1, 2] + [0] * (size - half)
    plans = []
    for rank in range(size):
        arrival, due = {}, {}
        for chunk in range(size):
            behind = (place[rank] - place[chunk]) % size
            distance = min(behind, size - behind)
            for upper in range(2):
                arrival[chunk, upper] = distance
                if distance == half:
                    arrival[chunk, upper] = half + 1
                elif distance == half - 1:
                    arrival[chunk, upper] = half - 1 if upper == int(behind != distance) else half
        for d in range(half + 1):
            for i, row in enumerate(sends[rank, d]):
                if i >= 4:
                    when = size - 1
                elif i >= 2 and 0 < d < half:
                    when = {half - 1: half, half - 2: half + 1}.get(d, size - d - 1)
                elif i < 2 and d > 0:
                    when = half + 1 if d == half else size - max(d - 1, 1)
                else:
                    continue
                due[int(row) // 2, int(row) % 2] = when
        ready = {}
        for chunk in range(size):
            ready[chunk, 1] = max(arrival[chunk, 0], arrival[chunk, 1])
            ready[chunk, 0] = max(arrival[chunk, 0], arrival[chunk - 1, 1]) if chunk else ready[chunk, 1]
        calls, left = [], set(ready)
        for call in range(size):
            able = sorted((due[t], t) for t in left if ready[t] <= call)
            must = [t for when, t in able if when <= call]
            more = [t for when, t in able if when > call][:max(spare[call] - len(must), 0)]
            calls.append([2 * chunk + upper for chunk, upper in must + more])
            left -= set(must + more)
        assert not left and all(ready[t] <= due[t] for t in ready)
        plans.append(calls)
    return plans


def step_kernel(pieces, rows, heads, sending, *refs):
    total = pieces * rows
    width = heads * HEAD
    it = iter(refs)
    ids, lists = next(it), next(it)
    xs = [next(it) for _ in range(pieces)]
    gain, wq, wkv, cos_tab, sin_tab, key_wide, cache, doc_bias, own_bias = [next(it) for _ in range(9)]
    first = pieces == 1 and rows == 128
    if not first:
        next(it), next(it), next(it)
    if sending:
        w_out = next(it)
    qb, kvb, att = next(it), next(it), next(it)
    if sending:
        terms = [next(it), next(it)]
    (x_s, xn_s, w_s, cos_s, sin_s, qo_s, kvo_s, key_s, val_s, qt_s, kvt_s, db_s, ob_s, sc_s, at_s,
     wide_s, own_s, o_s, m_s, l_s, f_s, sem_in, sem_tab, sem_w, sem_k, sem_out, sem_tile, sem_att) = [next(it) for _ in range(28)]
    if sending:
        rows_s, wo_s, made_s, sem_rows, sem_wo, sem_made = list(it)
    deep = wq.shape[0] // DEPTH_CHUNKS
    blocks = key_wide.shape[0] - 1
    stride = blocks + GROUP

    key_copy = pltpu.make_async_copy(key_wide, key_s, sem_k.at[0])
    val_copy = pltpu.make_async_copy(cache.at[:, pl.ds(HEAD, HEAD)], val_s, sem_k.at[1])
    if pieces:
        x_copies, tab_copies = [], []
        for i in range(pieces):
            span = pl.ds(i * rows, rows)
            place = pl.ds(pl.multiple_of(ids[i] * TILE, TILE), rows)
            x_copies.append(pltpu.make_async_copy(xs[i], x_s.at[span], sem_in.at[i]))
            tab_copies.append(pltpu.make_async_copy(cos_tab.at[place], cos_s.at[span], sem_tab.at[2 * i]))
            tab_copies.append(pltpu.make_async_copy(sin_tab.at[place], sin_s.at[span], sem_tab.at[2 * i + 1]))
        for copy in x_copies:
            copy.start()
        w_copies = []
        for j in range(DEPTH_CHUNKS):
            span = pl.ds(j * deep, deep)
            w_copies.append(pltpu.make_async_copy(wq.at[span], w_s.at[span, pl.ds(0, width)], sem_w.at[2 * j]))
            w_copies.append(
                pltpu.make_async_copy(wkv.at[span], w_s.at[span, pl.ds(width, 2 * HEAD)], sem_w.at[2 * j + 1])
            )
        for copy in w_copies:
            copy.start()
        for copy in tab_copies:
            copy.start()
    count = ids[PIECES_MOST]

    def load_cache():
        @pl.when(count > 0)
        def _():
            key_copy.start()
            val_copy.start()

    if not pieces:
        load_cache()
    else:
        gains = gain[...]
        for i in range(pieces):
            x_copies[i].wait()

        def norm_rows(r, carry):
            span = pl.ds(pl.multiple_of(r * 16, 16), 16)
            values = x_s[span, :].astype(jnp.float32)
            mean_square = jnp.mean(values * values, axis=-1, keepdims=True)
            xn_s[span, :] = (values * lax.rsqrt(mean_square + EPS) * gains).astype(jnp.bfloat16)
            return carry

        lax.fori_loop(0, total // 16, norm_rows, 0, unroll=4)
        load_cache()
        for copy in tab_copies:
            copy.wait()
        cosine, sine = cos_s[...], sin_s[...]

        def rotate(v):
            return (v * cosine + pltpu.roll(v, HEAD // 2, 1) * sine).astype(jnp.bfloat16)

        made = None
        for j in range(DEPTH_CHUNKS):
            w_copies[2 * j].wait()
            w_copies[2 * j + 1].wait()
            span = slice(j * deep, (j + 1) * deep)
            more = jnp.dot(xn_s[:, span], w_s[span, :], preferred_element_type=jnp.float32)
            made = more if made is None else made + more
        for h in range(heads):
            qo_s[h] = rotate(made[:, h * HEAD:(h + 1) * HEAD])
        kvo_s[:, :HEAD] = rotate(made[:, width:width + HEAD])
        kvo_s[:, HEAD:] = made[:, width + HEAD:].astype(jnp.bfloat16)
        outs = []
        for i in range(pieces):
            span = pl.ds(i * rows, rows)
            place = pl.ds(pl.multiple_of(ids[i] * TILE, TILE), rows)
            outs.append(pltpu.make_async_copy(qo_s.at[:, span], qb.at[:, place], sem_out.at[2 * i]))
            outs.append(pltpu.make_async_copy(kvo_s.at[span], kvb.at[place], sem_out.at[2 * i + 1]))
        for copy in outs:
            copy.start()
        for copy in outs:
            copy.wait()

    if sending:
        term_copies = weight_copies(w_out, wo_s, sem_wo)
        for copy in term_copies:
            copy.start()
    factor = math.log2(math.e) / math.sqrt(HEAD)

    def fetches(i, slot):
        tile = ids[HEADER + i]
        at = pl.multiple_of(tile * TILE, TILE)
        before = pl.multiple_of(jnp.maximum(tile - 1, 0) * TILE, TILE)
        return [
            pltpu.make_async_copy(qb.at[:, pl.ds(at, TILE)], qt_s.at[slot], sem_tile.at[slot, 0]),
            pltpu.make_async_copy(kvb.at[pl.ds(before, 2 * TILE)], kvt_s.at[slot], sem_tile.at[slot, 1]),
            pltpu.make_async_copy(doc_bias.at[pl.ds(at, TILE)], db_s.at[slot], sem_tile.at[slot, 2]),
            pltpu.make_async_copy(own_bias.at[pl.ds(at, TILE)], ob_s.at[slot], sem_tile.at[slot, 3]),
        ]

    def att_copy(i):
        at = pl.multiple_of(ids[HEADER + i] * TILE, TILE)
        return pltpu.make_async_copy(at_s, att.at[pl.ds(at, TILE)], sem_att)

    @pl.when(count > 0)
    def _():
        for copy in fetches(0, 0):
            copy.start()
        key_copy.wait()
        val_copy.wait()

    contract_last = (((1,), (1,)), ((), ()))

    def one_tile(i, carry):
        slot = lax.rem(i, 2)

        @pl.when(i + 1 < count)
        def _():
            for copy in fetches(i + 1, 1 - slot):
                copy.start()

        for copy in fetches(i, slot):
            copy.wait()
        tile = ids[HEADER + i]
        needed = lists[tile * stride]
        for h in range(heads):
            wide_s[h * TILE:(h + 1) * TILE, :HEAD] = qt_s[slot, h]
            wide_s[h * TILE:(h + 1) * TILE, HEAD:] = db_s[slot]
        own = lax.dot_general(
            wide_s[:, :HEAD], kvt_s[slot, :, :HEAD], contract_last, preferred_element_type=jnp.float32
        )
        own = (own.reshape(heads, TILE, HEAD) + ob_s[slot][None]).reshape(heads * TILE, HEAD)
        own_s[...] = own

        first_block = tile * stride + 1

        def score_group(g, c):
            listed = [lists[first_block + g * GROUP + u] for u in range(GROUP)]
            keys = jnp.concatenate([key_s[block] for block in listed], axis=1)
            scores = jnp.dot(wide_s[...], keys, preferred_element_type=jnp.float32)
            sc_s[g] = scores
            top = m_s[...]
            for c in range(0, GROUP * KEY_BLOCK, HEAD):
                top = jnp.maximum(top, scores[:, c:c + HEAD])
            m_s[...] = top
            return c

        m_s[...] = own
        lax.fori_loop(0, needed, score_group, 0)
        top = jnp.max(m_s[...], axis=1, keepdims=True) * factor
        weights = jnp.exp2(own_s[...] * factor - top)
        l_s[...] = weights
        f_s[...] = jnp.dot(weights.astype(jnp.bfloat16), kvt_s[slot, :, HEAD:], preferred_element_type=jnp.float32)

        def value_group(g, c):
            sums, made = l_s[...], []
            for u in range(GROUP):
                block = lists[first_block + g * GROUP + u]
                at = pl.multiple_of(jnp.minimum(block, blocks - 1) * KEY_BLOCK, KEY_BLOCK)
                weights = jnp.exp2(sc_s[g, :, u * KEY_BLOCK:(u + 1) * KEY_BLOCK] * factor - top)
                sums = sums + (weights[:, :HEAD] + weights[:, HEAD:])
                made.append(
                    jnp.dot(
                        weights.astype(jnp.bfloat16), val_s[pl.ds(at, KEY_BLOCK), :], preferred_element_type=jnp.float32
                    )
                )
            l_s[...] = sums
            f_s[...] += (made[0] + made[1]) + (made[2] + made[3])
            return c

        lax.fori_loop(0, needed, value_group, 0)
        o_s[...] = (f_s[...] / jnp.sum(l_s[...], axis=1, keepdims=True)).astype(jnp.bfloat16)

        @pl.when(i > 0)
        def _():
            att_copy(i - 1).wait()

        for h in range(heads):
            at_s[:, h * HEAD:(h + 1) * HEAD] = o_s[h * TILE:(h + 1) * TILE]
        att_copy(i).start()
        return carry

    lax.fori_loop(0, count, one_tile, 0)

    @pl.when(count > 0)
    def _():
        att_copy(count - 1).wait()

    if sending:
        places = [ids[PIECES_MOST + 1], ids[PIECES_MOST + 2]]
        write_terms(places, att, term_copies, terms, rows_s, wo_s, made_s, sem_rows, sem_made)


def run_step(ids, lists, xs, fixed, state, dims, w_out=None):
    tokens, heads, prefix, depth = dims
    pieces = len(xs)
    rows = xs[0].shape[0] if pieces else TILE
    total = max(pieces * rows, 16)
    width = heads * HEAD
    any_spec = pl.BlockSpec(memory_space=pl.ANY)
    vmem_spec = pl.BlockSpec(memory_space=pltpu.VMEM)
    operands = list(xs) + list(fixed)
    specs = [any_spec] * pieces + [vmem_spec] + [any_spec] * (len(fixed) - 1)
    aliases = {}
    if state is not None:
        aliases = {2 + len(operands) + i: i for i in range(3)}
        operands += list(state)
        specs += [any_spec] * 3
    sending = w_out is not None
    if sending:
        operands.append(w_out)
        specs.append(any_spec)
    out_shape = [
        jax.ShapeDtypeStruct((heads, tokens, HEAD), jnp.bfloat16),
        jax.ShapeDtypeStruct((tokens, 2 * HEAD), jnp.bfloat16),
        jax.ShapeDtypeStruct((tokens, width), jnp.bfloat16),
    ]
    if sending:
        out_shape += [jax.ShapeDtypeStruct((TILE, w_out.shape[1]), jnp.bfloat16)] * 2
    small = 16
    w_rows = depth if pieces else small
    scratch = [
        pltpu.VMEM((total, depth), jnp.bfloat16),
        pltpu.VMEM((total, depth), jnp.bfloat16),
        pltpu.VMEM((w_rows, width + 2 * HEAD), jnp.bfloat16),
        pltpu.VMEM((total, HEAD), jnp.float32),
        pltpu.VMEM((total, HEAD), jnp.float32),
        pltpu.VMEM((heads, total, HEAD), jnp.bfloat16),
        pltpu.VMEM((total, 2 * HEAD), jnp.bfloat16),
        pltpu.VMEM((prefix // KEY_BLOCK + 1, 2 * HEAD, KEY_BLOCK), jnp.bfloat16),
        pltpu.VMEM((prefix, HEAD), jnp.bfloat16),
        pltpu.VMEM((2, heads, TILE, HEAD), jnp.bfloat16),
        pltpu.VMEM((2, 2 * TILE, 2 * HEAD), jnp.bfloat16),
        pltpu.VMEM((2, TILE, HEAD), jnp.bfloat16),
        pltpu.VMEM((2, TILE, HEAD), jnp.float32),
        pltpu.VMEM((prefix // KEY_BLOCK // GROUP, heads * TILE, GROUP * KEY_BLOCK), jnp.float32),
        pltpu.VMEM((TILE, width), jnp.bfloat16),
        pltpu.VMEM((heads * TILE, 2 * HEAD), jnp.bfloat16),
        pltpu.VMEM((heads * TILE, HEAD), jnp.float32),
        pltpu.VMEM((heads * TILE, HEAD), jnp.bfloat16),
        pltpu.VMEM((heads * TILE, HEAD), jnp.float32),
        pltpu.VMEM((heads * TILE, HEAD), jnp.float32),
        pltpu.VMEM((heads * TILE, HEAD), jnp.float32),
        pltpu.SemaphoreType.DMA((max(pieces, 1),)),
        pltpu.SemaphoreType.DMA((2 * max(pieces, 1),)),
        pltpu.SemaphoreType.DMA((2 * DEPTH_CHUNKS,)),
        pltpu.SemaphoreType.DMA((2,)),
        pltpu.SemaphoreType.DMA((2 * max(pieces, 1),)),
        pltpu.SemaphoreType.DMA((2, 4)),
        pltpu.SemaphoreType.DMA,
    ]
    if sending:
        scratch += term_scratch(2, width, w_out.shape[1])
    return pl.pallas_call(
        functools.partial(step_kernel, pieces, rows, heads, sending),
        grid_spec=pltpu.PrefetchScalarGridSpec(
            num_scalar_prefetch=2,
            grid=(),
            in_specs=specs,
            out_specs=[any_spec] * len(out_shape),
            scratch_shapes=scratch,
        ),
        out_shape=out_shape,
        input_output_aliases=aliases,
        compiler_params=pltpu.CompilerParams(vmem_limit_bytes=VMEM_LIMIT),
        cost_estimate=pl.CostEstimate(flops=1 << 20, bytes_accessed=1 << 16, transcendentals=0),
    )(ids, lists, *operands)


def weight_copies(w_out, w_s, sem_w):
    columns = w_out.shape[1] // COLUMN_CHUNKS
    spans = [pl.ds(c * columns, columns) for c in range(COLUMN_CHUNKS)]
    return [pltpu.make_async_copy(w_out.at[:, span], w_s.at[:, span], sem_w.at[c]) for c, span in enumerate(spans)]


def write_terms(places, att, w_copies, outs, rows_s, w_s, made_s, sem_rows, sem_out):
    columns = w_s.shape[1] // COLUMN_CHUNKS
    row_copies = [
        pltpu.make_async_copy(
            att.at[pl.ds(pl.multiple_of(place * TILE, TILE), TILE)], rows_s.at[pl.ds(i * TILE, TILE)], sem_rows.at[i]
        )
        for i, place in enumerate(places)
    ]
    for copy in row_copies:
        copy.start()
    for copy in row_copies:
        copy.wait()
    out_copies = []
    for c in range(COLUMN_CHUNKS):
        span = pl.ds(c * columns, columns)
        w_copies[c].wait()
        made = jnp.dot(rows_s[...], w_s[:, span], preferred_element_type=jnp.float32)
        made_s[:, span] = made.astype(jnp.bfloat16)
        for i in range(len(places)):
            copy = pltpu.make_async_copy(
                made_s.at[pl.ds(i * TILE, TILE), span], outs[i].at[:, span], sem_out.at[i, c]
            )
            copy.start()
            out_copies.append(copy)
    for copy in out_copies:
        copy.wait()


def term_scratch(count, width, columns):
    return [
        pltpu.VMEM((count * TILE, width), jnp.bfloat16),
        pltpu.VMEM((width, columns), jnp.bfloat16),
        pltpu.VMEM((count * TILE, columns), jnp.bfloat16),
        pltpu.SemaphoreType.DMA((count,)),
        pltpu.SemaphoreType.DMA((COLUMN_CHUNKS,)),
        pltpu.SemaphoreType.DMA((count, COLUMN_CHUNKS)),
    ]


def product_kernel(count, ids, att, w_out, *refs):
    rows_s, w_s, made_s, sem_rows, sem_w, sem_out = refs[count:]
    copies = weight_copies(w_out, w_s, sem_w)
    for copy in copies:
        copy.start()
    places = [ids[i] for i in range(count)]
    write_terms(places, att, copies, refs[:count], rows_s, w_s, made_s, sem_rows, sem_out)


def product(ids, count, att, w_out):
    width, columns = w_out.shape
    any_spec = pl.BlockSpec(memory_space=pl.ANY)
    return pl.pallas_call(
        functools.partial(product_kernel, count),
        grid_spec=pltpu.PrefetchScalarGridSpec(
            num_scalar_prefetch=1,
            grid=(),
            in_specs=[any_spec] * 2,
            out_specs=[any_spec] * count,
            scratch_shapes=term_scratch(count, width, columns),
        ),
        out_shape=[jax.ShapeDtypeStruct((TILE, columns), jnp.bfloat16)] * count,
        compiler_params=pltpu.CompilerParams(vmem_limit_bytes=VMEM_LIMIT),
        cost_estimate=pl.CostEstimate(flops=1 << 20, bytes_accessed=1 << 16, transcendentals=0),
    )(ids, att, w_out)


def tables(seg_ids, seg_doc, doc_lens, prefix, cache):
    tokens = seg_ids.shape[0]
    tiles = tokens // TILE
    blocks = prefix // KEY_BLOCK
    docs = doc_lens.shape[0]
    order = jnp.arange(tokens, dtype=jnp.int32)
    start = jnp.sum((seg_ids[None, :] < seg_ids[:, None]).astype(jnp.int32), axis=1, dtype=jnp.int32)
    positions = prefix + order - start
    segments = jnp.arange(seg_doc.shape[0], dtype=jnp.int32)
    tok_doc = jnp.sum(
        jnp.where(seg_ids[:, None] == segments[None, :], seg_doc[None, :], 0), axis=1, dtype=jnp.int32
    )
    doc_list = jnp.arange(docs, dtype=jnp.int32)
    doc_ends = jnp.sum(jnp.where(doc_list[None, :] <= doc_list[:, None], doc_lens[None, :], 0), axis=1)
    doc_starts = doc_ends - doc_lens
    lanes = jnp.arange(HEAD, dtype=jnp.int32)
    half = HEAD // 2
    inverse = ROPE_THETA ** (-(jnp.arange(half, dtype=jnp.float32) * 2.0 / HEAD))
    inverse = jnp.concatenate([inverse, inverse])
    angles = positions.astype(jnp.float32)[:, None] * inverse[None, :]
    cosine = jnp.cos(angles)
    sine = jnp.sin(angles) * jnp.where(lanes < half, -1.0, 1.0)[None, :]
    doc_bias = jnp.where(lanes[None, :] == tok_doc[:, None], 0.0, MASKED).astype(jnp.bfloat16)
    spot = jnp.arange(prefix + KEY_BLOCK, dtype=jnp.int32).reshape(blocks + 1, 1, KEY_BLOCK)
    low = jnp.pad(doc_starts, (0, HEAD - docs), constant_values=prefix).reshape(1, HEAD, 1)
    high = jnp.pad(doc_ends, (0, HEAD - docs), constant_values=prefix + KEY_BLOCK).reshape(1, HEAD, 1)
    one_hot = ((spot >= low) & (spot < high)).astype(jnp.bfloat16)
    by_block = cache[:, :HEAD].reshape(blocks, KEY_BLOCK, HEAD).transpose(0, 2, 1)
    key_wide = jnp.concatenate([jnp.pad(by_block, ((0, 1), (0, 0), (0, 0))), one_hot], axis=1)
    first_key = jnp.maximum(jnp.arange(tiles, dtype=jnp.int32) - 1, 0) * TILE
    spots = first_key[:, None] + lanes[None, :]
    by_tile = seg_ids.reshape(tiles, TILE)
    earlier = jnp.concatenate([by_tile[:1], by_tile[:-1]], axis=0)
    later = jnp.concatenate([by_tile[1:2], by_tile[1:]], axis=0)
    window_seg = jnp.concatenate([earlier, later], axis=1)
    ok = (window_seg[:, None, :] == by_tile[:, :, None]) & (
        spots[:, None, :] <= order.reshape(tiles, TILE)[:, :, None]
    )
    own_bias = jnp.where(ok, 0.0, MASKED).astype(jnp.float32).reshape(tokens, HEAD)
    present = jnp.any(tok_doc.reshape(tiles, TILE)[:, :, None] == doc_list[None, None, :], axis=1)
    edge = jnp.arange(blocks, dtype=jnp.int32) * KEY_BLOCK
    overlap = (doc_starts[:, None] < edge[None, :] + KEY_BLOCK) & (doc_ends[:, None] > edge[None, :])
    flags = jnp.any(present[:, :, None] & overlap[None, :, :], axis=1).astype(jnp.int32)
    block_ids = jnp.arange(blocks, dtype=jnp.int32)
    rank = jnp.sum(jnp.where(block_ids[None, :, None] > block_ids[None, None, :], flags[:, None, :], 0), axis=2)
    listed = jnp.sum(
        jnp.where((rank[:, :, None] == block_ids[None, None, :]) & (flags[:, :, None] > 0), block_ids[None, :, None], 0),
        axis=1,
    )
    count = jnp.sum(flags, axis=1, keepdims=True)
    listed = jnp.where(block_ids[None, :] < count, listed, blocks)
    groups = (count + GROUP - 1) // GROUP
    lists = jnp.pad(jnp.concatenate([groups, listed], axis=1), ((0, 0), (0, GROUP - 1)))
    lists = lists.astype(jnp.int32).reshape(-1)
    return cosine, sine, key_wide, doc_bias, own_bias, lists


def local(
    hidden_in, norm_gain, w_query, keyvalue_weight, w_out, prefix_keyvalue_cache, seg_ids, seg_doc, doc_lens
):
    size = lax.axis_size("tensor")
    tokens = seg_ids.shape[0]
    prefix = prefix_keyvalue_cache.shape[0]
    chunk_rows, depth = hidden_in.shape
    heads = w_query.shape[1] // HEAD
    order = ring_order(size)
    half = size // 2
    rank = lax.axis_index("tensor")

    forward_pairs = [(order[i], order[(i + 1) % size]) for i in range(size)]
    backward_pairs = [(b, a) for a, b in forward_pairs]

    def forward(x):
        return lax.ppermute(x, "tensor", forward_pairs)

    def backward(x):
        return lax.ppermute(x, "tensor", backward_pairs)

    if keyvalue_weight.shape[1] == HEAD:
        swap = [(i, i ^ 1) for i in range(size)]
        even = rank % 2 == 0
        other_weight, other_cache = lax.ppermute((keyvalue_weight, prefix_keyvalue_cache), "tensor", swap)
        keyvalue_weight = jnp.concatenate(
            [jnp.where(even, keyvalue_weight, other_weight), jnp.where(even, other_weight, keyvalue_weight)], axis=1
        )
        prefix_keyvalue_cache = jnp.concatenate(
            [
                jnp.where(even, prefix_keyvalue_cache, other_cache),
                jnp.where(even, other_cache, prefix_keyvalue_cache),
            ],
            axis=1,
        )

    place = {r: i for i, r in enumerate(order)}
    flips = np.zeros((size,), np.int32)
    for r in range(size):
        flips[r] = int(order[(place[r] - 1) % size] == r - 1)
    sends = np.zeros((size, half + 1, 6), np.int32)
    for r in range(size):
        for d in range(half + 1):
            ahead, back = order[(place[r] + d) % size], order[(place[r] - d) % size]
            late = [2 * ahead + flips[ahead], 2 * back + 1 - flips[back]]
            sends[r, d] = late + [2 * ahead + 1 - flips[ahead], 2 * back + flips[back], 2 * r, 2 * r + 1]
    tiles = tile_plan(order, sends)
    most = max(len(call) for calls in tiles for call in calls)
    plan = np.zeros((size, size, HEADER + most), np.int32)
    for r in range(size):
        for call in range(size):
            d = min(call, half - 1) if call <= half else half
            back, ahead = 2 * order[(place[r] - d) % size], 2 * order[(place[r] + d) % size]
            if call == half - 1 or call == half + 1:
                parts = [back, ahead + 1, 0, 0]
            elif call == half:
                parts = [back + 1, ahead, 0, 0]
            else:
                parts = [back, ahead, 0, 0]
            terms = sends[r, half, :2] if call == half + 1 else sends[r, half - 1, 2:4]
            row = parts + [len(tiles[r][call])] + [int(i) for i in terms] + tiles[r][call]
            plan[r, call, :len(row)] = row
    my_plan = jnp.asarray(plan)[rank]
    my_sends = jnp.asarray(sends)[rank]
    flipped = jnp.asarray(flips)[rank] > 0

    cosine, sine, key_wide, doc_bias, own_bias, lists = tables(
        seg_ids, seg_doc, doc_lens, prefix, prefix_keyvalue_cache
    )
    gain = norm_gain.astype(jnp.float32).reshape(1, depth)
    fixed = (gain, w_query, keyvalue_weight, cosine, sine, key_wide, prefix_keyvalue_cache, doc_bias, own_bias)
    dims = (tokens, heads, prefix, depth)

    def pass_on(pair):
        return forward(pair[0]), backward(pair[1])

    def add(pair, arrived):
        return tuple((a.astype(jnp.float32) + b.astype(jnp.float32)).astype(jnp.bfloat16) for a, b in zip(pair, arrived))

    def step(call, parts, state):
        return tuple(run_step(my_plan[call], lists, parts, fixed, state, dims))

    def step_and_send(call, parts, state):
        made = tuple(run_step(my_plan[call], lists, parts, fixed, state, dims, w_out))
        return made[:3], made[3:]

    def halves_of(pair):
        return (pair[0][:TILE], pair[1][TILE:]), (pair[0][TILE:], pair[1][:TILE])

    held = pass_on((hidden_in, hidden_in))
    state = step(0, [hidden_in], None)
    for distance in range(1, half - 2):
        held, state = lax.optimization_barrier((held, state))
        following = pass_on(held)
        state = step(distance, held, state)
        held = following
    held, state = lax.optimization_barrier((held, state))
    first, rest = halves_of(held)
    first = pass_on(first)
    state = step(half - 2, held, state)
    rest, state = lax.optimization_barrier((rest, state))
    second = pass_on(rest)
    first, state = lax.optimization_barrier((first, state))
    last = pass_on(first)
    state = step(half - 1, first, state)
    second, state = lax.optimization_barrier((second, state))
    state, made = step_and_send(half, second, state)
    made, last, state = lax.optimization_barrier((made, last, state))
    early = pass_on(made)
    state, made = step_and_send(half + 1, last, state)
    far = pass_on(made)
    for distance in range(half - 1, 0, -1):
        near = distance - 1
        if near > 0:
            made, state = lax.optimization_barrier((made, state))
            ahead = tuple(product(my_sends[near, 2:4], 2, state[2], w_out))
            early, ahead = lax.optimization_barrier((early, ahead))
            made = add(ahead, early)
            early = pass_on(made)
            made, state = lax.optimization_barrier((made, state))
            state = step(size - near, [], state)
        else:
            early, made, state = lax.optimization_barrier((early, made, state))
        late = product(my_sends[distance], 2 if near > 0 else 6, state[2], w_out)
        own, late = late[4:], tuple(late[:2])
        far, late = lax.optimization_barrier((far, late))
        made = add(late, far)
        far = pass_on(made)
    wide = [part.astype(jnp.float32) for part in early]
    own = [part.astype(jnp.float32) for part in own]
    base = (
        hidden_in[:TILE].astype(jnp.float32) + own[0] + jnp.where(flipped, wide[0], wide[1]),
        hidden_in[TILE:].astype(jnp.float32) + own[1] + jnp.where(flipped, wide[1], wide[0]),
    )
    base, far = lax.optimization_barrier((base, far))
    far = [part.astype(jnp.float32) for part in far]
    lower = base[0] + jnp.where(flipped, far[1], far[0])
    upper = base[1] + jnp.where(flipped, far[0], far[1])
    return jnp.concatenate([lower, upper], axis=0).astype(jnp.bfloat16)


def solution(mesh):
    return jax.shard_map(
        local,
        mesh=mesh,
        in_specs=(
            P(("dp", "tensor"), None),
            P(),
            P(None, "tensor"),
            P(None, "tensor"),
            P("tensor", None),
            P(None, "tensor"),
            P("dp"),
            P("dp"),
            P(),
        ),
        out_specs=P(("dp", "tensor"), None),
        check_vma=False,
    )
```

```python
import functools
import math

import jax
import jax.numpy as jnp
import numpy as np
from jax import lax
from jax.experimental import pallas as pl
from jax.experimental.pallas import tpu as pltpu
from jax.sharding import PartitionSpec as P

HEAD = 128
TILE = 64
KEY_BLOCK = 256
GROUP = 4
DEPTH_CHUNKS = 4
COLUMN_CHUNKS = 4
PIECES_MOST = 4
HEADER = PIECES_MOST + 3
MASKED = -1e30
EPS = 1e-05
ROPE_THETA = 500000.0
VMEM_LIMIT = 32 * 1024 * 1024


def ring_order(size):
    zs = 4 if size % 8 == 0 else 1
    ys = size // zs
    if zs == 1:
        return list(range(size))
    cycle = [(0, 0)]
    for y in range(ys):
        column = range(1, zs) if y % 2 == 0 else range(zs - 1, 0, -1)
        cycle += [(z, y) for z in column]
    cycle += [(0, y) for y in range(ys - 1, 0, -1)]
    return [z * ys + y for z, y in cycle]


def tile_plan(order, sends):
    size = len(order)
    half = size // 2
    place = {r: i for i, r in enumerate(order)}
    spare = [0] + [6] * (half - 3) + [1, 2] + [0] * (size - half)
    plans = []
    for rank in range(size):
        arrival, due = {}, {}
        for chunk in range(size):
            behind = (place[rank] - place[chunk]) % size
            distance = min(behind, size - behind)
            for upper in range(2):
                arrival[chunk, upper] = distance
                if distance == half:
                    arrival[chunk, upper] = half + 1
                elif distance == half - 1:
                    arrival[chunk, upper] = half - 1 if upper == int(behind != distance) else half
        for d in range(half + 1):
            for i, row in enumerate(sends[rank, d]):
                if i >= 4:
                    when = size - 1
                elif i >= 2 and 0 < d < half:
                    when = {half - 1: half, half - 2: half + 1}.get(d, size - d - 1)
                elif i < 2 and d > 0:
                    when = half + 1 if d == half else size - max(d - 1, 1)
                else:
                    continue
                due[int(row) // 2, int(row) % 2] = when
        ready = {}
        for chunk in range(size):
            ready[chunk, 1] = max(arrival[chunk, 0], arrival[chunk, 1])
            ready[chunk, 0] = max(arrival[chunk, 0], arrival[chunk - 1, 1]) if chunk else ready[chunk, 1]
        calls, left = [], set(ready)
        for call in range(size):
            able = sorted((due[t], t) for t in left if ready[t] <= call)
            must = [t for when, t in able if when <= call]
            more = [t for when, t in able if when > call][:max(spare[call] - len(must), 0)]
            calls.append([2 * chunk + upper for chunk, upper in must + more])
            left -= set(must + more)
        assert not left and all(ready[t] <= due[t] for t in ready)
        plans.append(calls)
    return plans


def step_kernel(pieces, rows, heads, sending, *refs):
    total = pieces * rows
    width = heads * HEAD
    it = iter(refs)
    ids, lists = next(it), next(it)
    xs = [next(it) for _ in range(pieces)]
    gain, wq, wkv, cos_tab, sin_tab, key_wide, cache, doc_bias, own_bias = [next(it) for _ in range(9)]
    first = pieces == 1 and rows == 128
    if not first:
        next(it), next(it), next(it)
    if sending:
        w_out = next(it)
    qb, kvb, att = next(it), next(it), next(it)
    if sending:
        terms = [next(it), next(it)]
    (x_s, xn_s, w_s, cos_s, sin_s, qo_s, kvo_s, key_s, val_s, qt_s, kvt_s, db_s, ob_s, sc_s, at_s,
     wide_s, own_s, o_s, sem_in, sem_tab, sem_w, sem_k, sem_out, sem_tile, sem_att) = [next(it) for _ in range(25)]
    if sending:
        rows_s, wo_s, made_s, sem_rows, sem_wo, sem_made = list(it)
    deep = wq.shape[0] // DEPTH_CHUNKS
    blocks = key_wide.shape[0] - 1
    stride = blocks + GROUP

    key_copy = pltpu.make_async_copy(key_wide, key_s, sem_k.at[0])
    val_copy = pltpu.make_async_copy(cache.at[:, pl.ds(HEAD, HEAD)], val_s, sem_k.at[1])
    if pieces:
        x_copies, tab_copies = [], []
        for i in range(pieces):
            span = pl.ds(i * rows, rows)
            place = pl.ds(pl.multiple_of(ids[i] * TILE, TILE), rows)
            x_copies.append(pltpu.make_async_copy(xs[i], x_s.at[span], sem_in.at[i]))
            tab_copies.append(pltpu.make_async_copy(cos_tab.at[place], cos_s.at[span], sem_tab.at[2 * i]))
            tab_copies.append(pltpu.make_async_copy(sin_tab.at[place], sin_s.at[span], sem_tab.at[2 * i + 1]))
        for copy in x_copies:
            copy.start()
        w_copies = []
        for j in range(DEPTH_CHUNKS):
            span = pl.ds(j * deep, deep)
            w_copies.append(pltpu.make_async_copy(wq.at[span], w_s.at[span, pl.ds(0, width)], sem_w.at[2 * j]))
            w_copies.append(
                pltpu.make_async_copy(wkv.at[span], w_s.at[span, pl.ds(width, 2 * HEAD)], sem_w.at[2 * j + 1])
            )
        for copy in w_copies:
            copy.start()
        for copy in tab_copies:
            copy.start()
    count = ids[PIECES_MOST]

    def load_cache():
        @pl.when(count > 0)
        def _():
            key_copy.start()
            val_copy.start()

    if not pieces:
        load_cache()
    else:
        gains = gain[...]
        for i in range(pieces):
            x_copies[i].wait()

        def norm_rows(r, carry):
            span = pl.ds(pl.multiple_of(r * 16, 16), 16)
            values = x_s[span, :].astype(jnp.float32)
            mean_square = jnp.mean(values * values, axis=-1, keepdims=True)
            xn_s[span, :] = (values * lax.rsqrt(mean_square + EPS) * gains).astype(jnp.bfloat16)
            return carry

        lax.fori_loop(0, total // 16, norm_rows, 0, unroll=4)
        load_cache()
        for copy in tab_copies:
            copy.wait()
        cosine, sine = cos_s[...], sin_s[...]

        def rotate(v):
            return (v * cosine + pltpu.roll(v, HEAD // 2, 1) * sine).astype(jnp.bfloat16)

        made = None
        for j in range(DEPTH_CHUNKS):
            w_copies[2 * j].wait()
            w_copies[2 * j + 1].wait()
            span = slice(j * deep, (j + 1) * deep)
            more = jnp.dot(xn_s[:, span], w_s[span, :], preferred_element_type=jnp.float32)
            made = more if made is None else made + more
        for h in range(heads):
            qo_s[h] = rotate(made[:, h * HEAD:(h + 1) * HEAD])
        kvo_s[:, :HEAD] = rotate(made[:, width:width + HEAD])
        kvo_s[:, HEAD:] = made[:, width + HEAD:].astype(jnp.bfloat16)
        outs = []
        for i in range(pieces):
            span = pl.ds(i * rows, rows)
            place = pl.ds(pl.multiple_of(ids[i] * TILE, TILE), rows)
            outs.append(pltpu.make_async_copy(qo_s.at[:, span], qb.at[:, place], sem_out.at[2 * i]))
            outs.append(pltpu.make_async_copy(kvo_s.at[span], kvb.at[place], sem_out.at[2 * i + 1]))
        for copy in outs:
            copy.start()
        for copy in outs:
            copy.wait()

    if sending:
        term_copies = weight_copies(w_out, wo_s, sem_wo)
        for copy in term_copies:
            copy.start()
    factor = math.log2(math.e) / math.sqrt(HEAD)

    def fetches(i, slot):
        tile = ids[HEADER + i]
        at = pl.multiple_of(tile * TILE, TILE)
        before = pl.multiple_of(jnp.maximum(tile - 1, 0) * TILE, TILE)
        return [
            pltpu.make_async_copy(qb.at[:, pl.ds(at, TILE)], qt_s.at[slot], sem_tile.at[slot, 0]),
            pltpu.make_async_copy(kvb.at[pl.ds(before, 2 * TILE)], kvt_s.at[slot], sem_tile.at[slot, 1]),
            pltpu.make_async_copy(doc_bias.at[pl.ds(at, TILE)], db_s.at[slot], sem_tile.at[slot, 2]),
            pltpu.make_async_copy(own_bias.at[pl.ds(at, TILE)], ob_s.at[slot], sem_tile.at[slot, 3]),
        ]

    def att_copy(i):
        at = pl.multiple_of(ids[HEADER + i] * TILE, TILE)
        return pltpu.make_async_copy(at_s, att.at[pl.ds(at, TILE)], sem_att)

    @pl.when(count > 0)
    def _():
        for copy in fetches(0, 0):
            copy.start()
        key_copy.wait()
        val_copy.wait()

    contract_last = (((1,), (1,)), ((), ()))

    def one_tile(i, carry):
        slot = lax.rem(i, 2)

        @pl.when(i + 1 < count)
        def _():
            for copy in fetches(i + 1, 1 - slot):
                copy.start()

        for copy in fetches(i, slot):
            copy.wait()
        tile = ids[HEADER + i]
        needed = lists[tile * stride]
        for h in range(heads):
            wide_s[h * TILE:(h + 1) * TILE, :HEAD] = qt_s[slot, h]
            wide_s[h * TILE:(h + 1) * TILE, HEAD:] = db_s[slot]
        own = lax.dot_general(
            wide_s[:, :HEAD], kvt_s[slot, :, :HEAD], contract_last, preferred_element_type=jnp.float32
        )
        own = (own.reshape(heads, TILE, HEAD) + ob_s[slot][None]).reshape(heads * TILE, HEAD)
        own_s[...] = own

        def attend(groups):
            listed = [lists[tile * stride + 1 + j] for j in range(groups * GROUP)]
            top = own_s[...]
            for g in range(groups):
                keys = jnp.concatenate([key_s[block] for block in listed[g * GROUP:(g + 1) * GROUP]], axis=1)
                scores = jnp.dot(wide_s[...], keys, preferred_element_type=jnp.float32)
                sc_s[g] = scores
                for c in range(0, GROUP * KEY_BLOCK, HEAD):
                    top = jnp.maximum(top, scores[:, c:c + HEAD])
            top = jnp.max(top, axis=1, keepdims=True) * factor
            weights = jnp.exp2(own_s[...] * factor - top)
            sums = weights
            made = [jnp.dot(weights.astype(jnp.bfloat16), kvt_s[slot, :, HEAD:], preferred_element_type=jnp.float32)]
            made += [None] * (GROUP - 1)
            for j, block in enumerate(listed):
                at = pl.multiple_of(jnp.minimum(block, blocks - 1) * KEY_BLOCK, KEY_BLOCK)
                c = j % GROUP * KEY_BLOCK
                weights = jnp.exp2(sc_s[j // GROUP, :, c:c + KEY_BLOCK] * factor - top)
                sums = sums + (weights[:, :HEAD] + weights[:, HEAD:])
                more = jnp.dot(
                    weights.astype(jnp.bfloat16), val_s[pl.ds(at, KEY_BLOCK), :], preferred_element_type=jnp.float32
                )
                made[j % GROUP] = more if made[j % GROUP] is None else made[j % GROUP] + more
            made = (made[0] + made[1]) + (made[2] + made[3])
            o_s[...] = (made / jnp.sum(sums, axis=1, keepdims=True)).astype(jnp.bfloat16)

        for groups in range(1, blocks // GROUP + 1):

            @pl.when(needed == groups)
            def _(groups=groups):
                attend(groups)

        @pl.when(i > 0)
        def _():
            att_copy(i - 1).wait()

        for h in range(heads):
            at_s[:, h * HEAD:(h + 1) * HEAD] = o_s[h * TILE:(h + 1) * TILE]
        att_copy(i).start()
        return carry

    lax.fori_loop(0, count, one_tile, 0)

    @pl.when(count > 0)
    def _():
        att_copy(count - 1).wait()

    if sending:
        places = [ids[PIECES_MOST + 1], ids[PIECES_MOST + 2]]
        write_terms(places, att, term_copies, terms, rows_s, wo_s, made_s, sem_rows, sem_made)


def run_step(ids, lists, xs, fixed, state, dims, w_out=None):
    tokens, heads, prefix, depth = dims
    pieces = len(xs)
    rows = xs[0].shape[0] if pieces else TILE
    total = max(pieces * rows, 16)
    width = heads * HEAD
    any_spec = pl.BlockSpec(memory_space=pl.ANY)
    vmem_spec = pl.BlockSpec(memory_space=pltpu.VMEM)
    operands = list(xs) + list(fixed)
    specs = [any_spec] * pieces + [vmem_spec] + [any_spec] * (len(fixed) - 1)
    aliases = {}
    if state is not None:
        aliases = {2 + len(operands) + i: i for i in range(3)}
        operands += list(state)
        specs += [any_spec] * 3
    sending = w_out is not None
    if sending:
        operands.append(w_out)
        specs.append(any_spec)
    out_shape = [
        jax.ShapeDtypeStruct((heads, tokens, HEAD), jnp.bfloat16),
        jax.ShapeDtypeStruct((tokens, 2 * HEAD), jnp.bfloat16),
        jax.ShapeDtypeStruct((tokens, width), jnp.bfloat16),
    ]
    if sending:
        out_shape += [jax.ShapeDtypeStruct((TILE, w_out.shape[1]), jnp.bfloat16)] * 2
    small = 16
    w_rows = depth if pieces else small
    scratch = [
        pltpu.VMEM((total, depth), jnp.bfloat16),
        pltpu.VMEM((total, depth), jnp.bfloat16),
        pltpu.VMEM((w_rows, width + 2 * HEAD), jnp.bfloat16),
        pltpu.VMEM((total, HEAD), jnp.float32),
        pltpu.VMEM((total, HEAD), jnp.float32),
        pltpu.VMEM((heads, total, HEAD), jnp.bfloat16),
        pltpu.VMEM((total, 2 * HEAD), jnp.bfloat16),
        pltpu.VMEM((prefix // KEY_BLOCK + 1, 2 * HEAD, KEY_BLOCK), jnp.bfloat16),
        pltpu.VMEM((prefix, HEAD), jnp.bfloat16),
        pltpu.VMEM((2, heads, TILE, HEAD), jnp.bfloat16),
        pltpu.VMEM((2, 2 * TILE, 2 * HEAD), jnp.bfloat16),
        pltpu.VMEM((2, TILE, HEAD), jnp.bfloat16),
        pltpu.VMEM((2, TILE, HEAD), jnp.float32),
        pltpu.VMEM((prefix // KEY_BLOCK // GROUP, heads * TILE, GROUP * KEY_BLOCK), jnp.float32),
        pltpu.VMEM((TILE, width), jnp.bfloat16),
        pltpu.VMEM((heads * TILE, 2 * HEAD), jnp.bfloat16),
        pltpu.VMEM((heads * TILE, HEAD), jnp.float32),
        pltpu.VMEM((heads * TILE, HEAD), jnp.bfloat16),
        pltpu.SemaphoreType.DMA((max(pieces, 1),)),
        pltpu.SemaphoreType.DMA((2 * max(pieces, 1),)),
        pltpu.SemaphoreType.DMA((2 * DEPTH_CHUNKS,)),
        pltpu.SemaphoreType.DMA((2,)),
        pltpu.SemaphoreType.DMA((2 * max(pieces, 1),)),
        pltpu.SemaphoreType.DMA((2, 4)),
        pltpu.SemaphoreType.DMA,
    ]
    if sending:
        scratch += term_scratch(2, width, w_out.shape[1])
    return pl.pallas_call(
        functools.partial(step_kernel, pieces, rows, heads, sending),
        grid_spec=pltpu.PrefetchScalarGridSpec(
            num_scalar_prefetch=2,
            grid=(),
            in_specs=specs,
            out_specs=[any_spec] * len(out_shape),
            scratch_shapes=scratch,
        ),
        out_shape=out_shape,
        input_output_aliases=aliases,
        compiler_params=pltpu.CompilerParams(vmem_limit_bytes=VMEM_LIMIT),
        cost_estimate=pl.CostEstimate(flops=1 << 20, bytes_accessed=1 << 16, transcendentals=0),
    )(ids, lists, *operands)


def weight_copies(w_out, w_s, sem_w):
    columns = w_out.shape[1] // COLUMN_CHUNKS
    spans = [pl.ds(c * columns, columns) for c in range(COLUMN_CHUNKS)]
    return [pltpu.make_async_copy(w_out.at[:, span], w_s.at[:, span], sem_w.at[c]) for c, span in enumerate(spans)]


def write_terms(places, att, w_copies, outs, rows_s, w_s, made_s, sem_rows, sem_out):
    columns = w_s.shape[1] // COLUMN_CHUNKS
    row_copies = [
        pltpu.make_async_copy(
            att.at[pl.ds(pl.multiple_of(place * TILE, TILE), TILE)], rows_s.at[pl.ds(i * TILE, TILE)], sem_rows.at[i]
        )
        for i, place in enumerate(places)
    ]
    for copy in row_copies:
        copy.start()
    for copy in row_copies:
        copy.wait()
    out_copies = []
    for c in range(COLUMN_CHUNKS):
        span = pl.ds(c * columns, columns)
        w_copies[c].wait()
        made = jnp.dot(rows_s[...], w_s[:, span], preferred_element_type=jnp.float32)
        made_s[:, span] = made.astype(jnp.bfloat16)
        for i in range(len(places)):
            copy = pltpu.make_async_copy(
                made_s.at[pl.ds(i * TILE, TILE), span], outs[i].at[:, span], sem_out.at[i, c]
            )
            copy.start()
            out_copies.append(copy)
    for copy in out_copies:
        copy.wait()


def term_scratch(count, width, columns):
    return [
        pltpu.VMEM((count * TILE, width), jnp.bfloat16),
        pltpu.VMEM((width, columns), jnp.bfloat16),
        pltpu.VMEM((count * TILE, columns), jnp.bfloat16),
        pltpu.SemaphoreType.DMA((count,)),
        pltpu.SemaphoreType.DMA((COLUMN_CHUNKS,)),
        pltpu.SemaphoreType.DMA((count, COLUMN_CHUNKS)),
    ]


def product_kernel(count, ids, att, w_out, *refs):
    rows_s, w_s, made_s, sem_rows, sem_w, sem_out = refs[count:]
    copies = weight_copies(w_out, w_s, sem_w)
    for copy in copies:
        copy.start()
    places = [ids[i] for i in range(count)]
    write_terms(places, att, copies, refs[:count], rows_s, w_s, made_s, sem_rows, sem_out)


def product(ids, count, att, w_out):
    width, columns = w_out.shape
    any_spec = pl.BlockSpec(memory_space=pl.ANY)
    return pl.pallas_call(
        functools.partial(product_kernel, count),
        grid_spec=pltpu.PrefetchScalarGridSpec(
            num_scalar_prefetch=1,
            grid=(),
            in_specs=[any_spec] * 2,
            out_specs=[any_spec] * count,
            scratch_shapes=term_scratch(count, width, columns),
        ),
        out_shape=[jax.ShapeDtypeStruct((TILE, columns), jnp.bfloat16)] * count,
        compiler_params=pltpu.CompilerParams(vmem_limit_bytes=VMEM_LIMIT),
        cost_estimate=pl.CostEstimate(flops=1 << 20, bytes_accessed=1 << 16, transcendentals=0),
    )(ids, att, w_out)


def tables(seg_ids, seg_doc, doc_lens, prefix, cache):
    tokens = seg_ids.shape[0]
    tiles = tokens // TILE
    blocks = prefix // KEY_BLOCK
    docs = doc_lens.shape[0]
    order = jnp.arange(tokens, dtype=jnp.int32)
    start = jnp.sum((seg_ids[None, :] < seg_ids[:, None]).astype(jnp.int32), axis=1, dtype=jnp.int32)
    positions = prefix + order - start
    segments = jnp.arange(seg_doc.shape[0], dtype=jnp.int32)
    tok_doc = jnp.sum(
        jnp.where(seg_ids[:, None] == segments[None, :], seg_doc[None, :], 0), axis=1, dtype=jnp.int32
    )
    doc_list = jnp.arange(docs, dtype=jnp.int32)
    doc_ends = jnp.sum(jnp.where(doc_list[None, :] <= doc_list[:, None], doc_lens[None, :], 0), axis=1)
    doc_starts = doc_ends - doc_lens
    lanes = jnp.arange(HEAD, dtype=jnp.int32)
    half = HEAD // 2
    inverse = ROPE_THETA ** (-(jnp.arange(half, dtype=jnp.float32) * 2.0 / HEAD))
    inverse = jnp.concatenate([inverse, inverse])
    angles = positions.astype(jnp.float32)[:, None] * inverse[None, :]
    cosine = jnp.cos(angles)
    sine = jnp.sin(angles) * jnp.where(lanes < half, -1.0, 1.0)[None, :]
    doc_bias = jnp.where(lanes[None, :] == tok_doc[:, None], 0.0, MASKED).astype(jnp.bfloat16)
    spot = jnp.arange(prefix + KEY_BLOCK, dtype=jnp.int32).reshape(blocks + 1, 1, KEY_BLOCK)
    low = jnp.pad(doc_starts, (0, HEAD - docs), constant_values=prefix).reshape(1, HEAD, 1)
    high = jnp.pad(doc_ends, (0, HEAD - docs), constant_values=prefix + KEY_BLOCK).reshape(1, HEAD, 1)
    one_hot = ((spot >= low) & (spot < high)).astype(jnp.bfloat16)
    by_block = cache[:, :HEAD].reshape(blocks, KEY_BLOCK, HEAD).transpose(0, 2, 1)
    key_wide = jnp.concatenate([jnp.pad(by_block, ((0, 1), (0, 0), (0, 0))), one_hot], axis=1)
    first_key = jnp.maximum(jnp.arange(tiles, dtype=jnp.int32) - 1, 0) * TILE
    spots = first_key[:, None] + lanes[None, :]
    by_tile = seg_ids.reshape(tiles, TILE)
    earlier = jnp.concatenate([by_tile[:1], by_tile[:-1]], axis=0)
    later = jnp.concatenate([by_tile[1:2], by_tile[1:]], axis=0)
    window_seg = jnp.concatenate([earlier, later], axis=1)
    ok = (window_seg[:, None, :] == by_tile[:, :, None]) & (
        spots[:, None, :] <= order.reshape(tiles, TILE)[:, :, None]
    )
    own_bias = jnp.where(ok, 0.0, MASKED).astype(jnp.float32).reshape(tokens, HEAD)
    present = jnp.any(tok_doc.reshape(tiles, TILE)[:, :, None] == doc_list[None, None, :], axis=1)
    edge = jnp.arange(blocks, dtype=jnp.int32) * KEY_BLOCK
    overlap = (doc_starts[:, None] < edge[None, :] + KEY_BLOCK) & (doc_ends[:, None] > edge[None, :])
    flags = jnp.any(present[:, :, None] & overlap[None, :, :], axis=1).astype(jnp.int32)
    block_ids = jnp.arange(blocks, dtype=jnp.int32)
    rank = jnp.sum(jnp.where(block_ids[None, :, None] > block_ids[None, None, :], flags[:, None, :], 0), axis=2)
    listed = jnp.sum(
        jnp.where((rank[:, :, None] == block_ids[None, None, :]) & (flags[:, :, None] > 0), block_ids[None, :, None], 0),
        axis=1,
    )
    count = jnp.sum(flags, axis=1, keepdims=True)
    listed = jnp.where(block_ids[None, :] < count, listed, blocks)
    groups = (count + GROUP - 1) // GROUP
    lists = jnp.pad(jnp.concatenate([groups, listed], axis=1), ((0, 0), (0, GROUP - 1)))
    lists = lists.astype(jnp.int32).reshape(-1)
    return cosine, sine, key_wide, doc_bias, own_bias, lists


def local(
    hidden_in, norm_gain, w_query, keyvalue_weight, w_out, prefix_keyvalue_cache, seg_ids, seg_doc, doc_lens
):
    size = lax.axis_size("tensor")
    tokens = seg_ids.shape[0]
    prefix = prefix_keyvalue_cache.shape[0]
    chunk_rows, depth = hidden_in.shape
    heads = w_query.shape[1] // HEAD
    order = ring_order(size)
    half = size // 2
    rank = lax.axis_index("tensor")

    forward_pairs = [(order[i], order[(i + 1) % size]) for i in range(size)]
    backward_pairs = [(b, a) for a, b in forward_pairs]

    def forward(x):
        return lax.ppermute(x, "tensor", forward_pairs)

    def backward(x):
        return lax.ppermute(x, "tensor", backward_pairs)

    if keyvalue_weight.shape[1] == HEAD:
        swap = [(i, i ^ 1) for i in range(size)]
        even = rank % 2 == 0
        other_weight, other_cache = lax.ppermute((keyvalue_weight, prefix_keyvalue_cache), "tensor", swap)
        keyvalue_weight = jnp.concatenate(
            [jnp.where(even, keyvalue_weight, other_weight), jnp.where(even, other_weight, keyvalue_weight)], axis=1
        )
        prefix_keyvalue_cache = jnp.concatenate(
            [
                jnp.where(even, prefix_keyvalue_cache, other_cache),
                jnp.where(even, other_cache, prefix_keyvalue_cache),
            ],
            axis=1,
        )

    place = {r: i for i, r in enumerate(order)}
    flips = np.zeros((size,), np.int32)
    for r in range(size):
        flips[r] = int(order[(place[r] - 1) % size] == r - 1)
    sends = np.zeros((size, half + 1, 6), np.int32)
    for r in range(size):
        for d in range(half + 1):
            ahead, back = order[(place[r] + d) % size], order[(place[r] - d) % size]
            late = [2 * ahead + flips[ahead], 2 * back + 1 - flips[back]]
            sends[r, d] = late + [2 * ahead + 1 - flips[ahead], 2 * back + flips[back], 2 * r, 2 * r + 1]
    tiles = tile_plan(order, sends)
    most = max(len(call) for calls in tiles for call in calls)
    plan = np.zeros((size, size, HEADER + most), np.int32)
    for r in range(size):
        for call in range(size):
            d = min(call, half - 1) if call <= half else half
            back, ahead = 2 * order[(place[r] - d) % size], 2 * order[(place[r] + d) % size]
            if call == half - 1 or call == half + 1:
                parts = [back, ahead + 1, 0, 0]
            elif call == half:
                parts = [back + 1, ahead, 0, 0]
            else:
                parts = [back, ahead, 0, 0]
            terms = sends[r, half, :2] if call == half + 1 else sends[r, half - 1, 2:4]
            row = parts + [len(tiles[r][call])] + [int(i) for i in terms] + tiles[r][call]
            plan[r, call, :len(row)] = row
    my_plan = jnp.asarray(plan)[rank]
    my_sends = jnp.asarray(sends)[rank]
    late_ids = {d: my_sends[d, :2] for d in range(2, half)}
    late_ids[1] = jnp.concatenate([my_sends[1, :2], my_sends[1, 4:]])
    early_ids = {d: my_sends[d, 2:4] for d in range(1, half - 1)}
    flipped = jnp.asarray(flips)[rank] > 0

    cosine, sine, key_wide, doc_bias, own_bias, lists = tables(
        seg_ids, seg_doc, doc_lens, prefix, prefix_keyvalue_cache
    )
    gain = norm_gain.astype(jnp.float32).reshape(1, depth)
    fixed = (gain, w_query, keyvalue_weight, cosine, sine, key_wide, prefix_keyvalue_cache, doc_bias, own_bias)
    dims = (tokens, heads, prefix, depth)

    def pass_on(pair):
        return forward(pair[0]), backward(pair[1])

    def add(pair, arrived):
        return tuple((a.astype(jnp.float32) + b.astype(jnp.float32)).astype(jnp.bfloat16) for a, b in zip(pair, arrived))

    def step(call, parts, state):
        return tuple(run_step(my_plan[call], lists, parts, fixed, state, dims))

    def step_and_send(call, parts, state):
        made = tuple(run_step(my_plan[call], lists, parts, fixed, state, dims, w_out))
        return made[:3], made[3:]

    def halves_of(pair):
        return (pair[0][:TILE], pair[1][TILE:]), (pair[0][TILE:], pair[1][:TILE])

    held = pass_on((hidden_in, hidden_in))
    state = step(0, [hidden_in], None)
    state, late_ids, early_ids, flipped = lax.optimization_barrier((state, late_ids, early_ids, flipped))
    for distance in range(1, half - 2):
        held, state = lax.optimization_barrier((held, state))
        following = pass_on(held)
        state = step(distance, held, state)
        held = following
    held, state = lax.optimization_barrier((held, state))
    first, rest = halves_of(held)
    first = pass_on(first)
    state = step(half - 2, held, state)
    rest, state = lax.optimization_barrier((rest, state))
    second = pass_on(rest)
    first, state = lax.optimization_barrier((first, state))
    last = pass_on(first)
    state = step(half - 1, first, state)
    second, state = lax.optimization_barrier((second, state))
    state, made = step_and_send(half, second, state)
    made, last, state = lax.optimization_barrier((made, last, state))
    early = pass_on(made)
    state, made = step_and_send(half + 1, last, state)
    far = pass_on(made)
    for distance in range(half - 1, 0, -1):
        near = distance - 1
        if near > 0:
            made, state = lax.optimization_barrier((made, state))
            ahead = tuple(product(early_ids[near], 2, state[2], w_out))
            early, ahead = lax.optimization_barrier((early, ahead))
            made = add(ahead, early)
            early = pass_on(made)
            made, state = lax.optimization_barrier((made, state))
            state = step(size - near, [], state)
        else:
            early, made, state = lax.optimization_barrier((early, made, state))
        late = product(late_ids[distance], 2 if near > 0 else 4, state[2], w_out)
        own, late = late[2:], tuple(late[:2])
        far, late = lax.optimization_barrier((far, late))
        made = add(late, far)
        far = pass_on(made)
    wide = [part.astype(jnp.float32) for part in early]
    own = [part.astype(jnp.float32) for part in own]
    base = (
        hidden_in[:TILE].astype(jnp.float32) + own[0] + jnp.where(flipped, wide[0], wide[1]),
        hidden_in[TILE:].astype(jnp.float32) + own[1] + jnp.where(flipped, wide[1], wide[0]),
    )
    base, far = lax.optimization_barrier((base, far))
    far = [part.astype(jnp.float32) for part in far]
    lower = base[0] + jnp.where(flipped, far[1], far[0])
    upper = base[1] + jnp.where(flipped, far[0], far[1])
    return jnp.concatenate([lower, upper], axis=0).astype(jnp.bfloat16)


def solution(mesh):
    return jax.shard_map(
        local,
        mesh=mesh,
        in_specs=(
            P(("dp", "tensor"), None),
            P(),
            P(None, "tensor"),
            P(None, "tensor"),
            P("tensor", None),
            P(None, "tensor"),
            P("dp"),
            P("dp"),
            P(),
        ),
        out_specs=P(("dp", "tensor"), None),
        check_vma=False,
    )
```

```python
import functools
import math

import jax
import jax.numpy as jnp
import numpy as np
from jax import lax
from jax.experimental import pallas as pl
from jax.experimental.pallas import tpu as pltpu
from jax.sharding import PartitionSpec as P

HEAD = 128
TILE = 64
KEY_BLOCK = 256
GROUP = 4
DEPTH_CHUNKS = 4
COLUMN_CHUNKS = 4
PIECES_MOST = 4
HEADER = PIECES_MOST + 3
MASKED = -1e30
EPS = 1e-05
ROPE_THETA = 500000.0
VMEM_LIMIT = 32 * 1024 * 1024


def ring_order(size):
    zs = 4 if size % 8 == 0 else 1
    ys = size // zs
    if zs == 1:
        return list(range(size))
    cycle = [(0, 0)]
    for y in range(ys):
        column = range(1, zs) if y % 2 == 0 else range(zs - 1, 0, -1)
        cycle += [(z, y) for z in column]
    cycle += [(0, y) for y in range(ys - 1, 0, -1)]
    return [z * ys + y for z, y in cycle]


def tile_plan(order, sends):
    size = len(order)
    half = size // 2
    place = {r: i for i, r in enumerate(order)}
    spare = [0] + [6] * (half - 3) + [1, 2] + [0] * (size - half)
    plans = []
    for rank in range(size):
        arrival, due = {}, {}
        for chunk in range(size):
            behind = (place[rank] - place[chunk]) % size
            distance = min(behind, size - behind)
            for upper in range(2):
                arrival[chunk, upper] = distance
                if distance == half:
                    arrival[chunk, upper] = half + 1
                elif distance == half - 1:
                    arrival[chunk, upper] = half - 1 if upper == int(behind != distance) else half
        for d in range(half + 1):
            for i, row in enumerate(sends[rank, d]):
                if i >= 4:
                    when = size - 1
                elif i >= 2 and 0 < d < half:
                    when = {half - 1: half, half - 2: half + 1}.get(d, size - d - 1)
                elif i < 2 and d > 0:
                    when = half + 1 if d == half else size - max(d - 1, 1)
                else:
                    continue
                due[int(row) // 2, int(row) % 2] = when
        ready = {}
        for chunk in range(size):
            ready[chunk, 1] = max(arrival[chunk, 0], arrival[chunk, 1])
            ready[chunk, 0] = max(arrival[chunk, 0], arrival[chunk - 1, 1]) if chunk else ready[chunk, 1]
        calls, left = [], set(ready)
        for call in range(size):
            able = sorted((due[t], t) for t in left if ready[t] <= call)
            must = [t for when, t in able if when <= call]
            more = [t for when, t in able if when > call][:max(spare[call] - len(must), 0)]
            calls.append([2 * chunk + upper for chunk, upper in must + more])
            left -= set(must + more)
        assert not left and all(ready[t] <= due[t] for t in ready)
        plans.append(calls)
    return plans


def step_kernel(pieces, rows, heads, sending, *refs):
    total = pieces * rows
    width = heads * HEAD
    it = iter(refs)
    ids, lists = next(it), next(it)
    xs = [next(it) for _ in range(pieces)]
    gain, wq, wkv, cos_tab, sin_tab, key_wide, cache, doc_bias, own_bias = [next(it) for _ in range(9)]
    first = pieces == 1 and rows == 128
    if not first:
        next(it), next(it), next(it)
    if sending:
        w_out = next(it)
    qb, kvb, att = next(it), next(it), next(it)
    if sending:
        terms = [next(it), next(it)]
    (x_s, xn_s, w_s, cos_s, sin_s, qo_s, kvo_s, key_s, val_s, qt_s, kvt_s, db_s, ob_s, sc_s, at_s,
     wide_s, own_s, o_s, sem_in, sem_tab, sem_w, sem_k, sem_out, sem_tile, sem_att) = [next(it) for _ in range(25)]
    if sending:
        rows_s, wo_s, made_s, sem_rows, sem_wo, sem_made = list(it)
    deep = wq.shape[0] // DEPTH_CHUNKS
    blocks = key_wide.shape[0] - 1
    stride = blocks + GROUP

    if not first:
        key_copy = pltpu.make_async_copy(key_wide, key_s, sem_k.at[0])
        val_copy = pltpu.make_async_copy(cache.at[:, pl.ds(HEAD, HEAD)], val_s, sem_k.at[1])
    if pieces:
        x_copies, tab_copies = [], []
        for i in range(pieces):
            span = pl.ds(i * rows, rows)
            place = pl.ds(pl.multiple_of(ids[i] * TILE, TILE), rows)
            x_copies.append(pltpu.make_async_copy(xs[i], x_s.at[span], sem_in.at[i]))
            tab_copies.append(pltpu.make_async_copy(cos_tab.at[place], cos_s.at[span], sem_tab.at[2 * i]))
            tab_copies.append(pltpu.make_async_copy(sin_tab.at[place], sin_s.at[span], sem_tab.at[2 * i + 1]))
        for copy in x_copies:
            copy.start()
        w_copies = []
        for j in range(DEPTH_CHUNKS):
            span = pl.ds(j * deep, deep)
            w_copies.append(pltpu.make_async_copy(wq.at[span], w_s.at[span, pl.ds(0, width)], sem_w.at[2 * j]))
            w_copies.append(
                pltpu.make_async_copy(wkv.at[span], w_s.at[span, pl.ds(width, 2 * HEAD)], sem_w.at[2 * j + 1])
            )
        for copy in w_copies:
            copy.start()
        for copy in tab_copies:
            copy.start()
    count = ids[PIECES_MOST]

    def load_cache():
        @pl.when(count > 0)
        def _():
            key_copy.start()
            val_copy.start()

    if not pieces:
        load_cache()
    else:
        gains = gain[...]
        for i in range(pieces):
            x_copies[i].wait()

        def norm_rows(r, carry):
            span = pl.ds(pl.multiple_of(r * 16, 16), 16)
            values = x_s[span, :].astype(jnp.float32)
            mean_square = jnp.mean(values * values, axis=-1, keepdims=True)
            xn_s[span, :] = (values * lax.rsqrt(mean_square + EPS) * gains).astype(jnp.bfloat16)
            return carry

        lax.fori_loop(0, total // 16, norm_rows, 0, unroll=4)
        if not first:
            load_cache()
        for copy in tab_copies:
            copy.wait()
        cosine, sine = cos_s[...], sin_s[...]

        def rotate(v):
            return (v * cosine + pltpu.roll(v, HEAD // 2, 1) * sine).astype(jnp.bfloat16)

        made = None
        for j in range(DEPTH_CHUNKS):
            w_copies[2 * j].wait()
            w_copies[2 * j + 1].wait()
            span = slice(j * deep, (j + 1) * deep)
            more = jnp.dot(xn_s[:, span], w_s[span, :], preferred_element_type=jnp.float32)
            made = more if made is None else made + more
        for h in range(heads):
            qo_s[h] = rotate(made[:, h * HEAD:(h + 1) * HEAD])
        kvo_s[:, :HEAD] = rotate(made[:, width:width + HEAD])
        kvo_s[:, HEAD:] = made[:, width + HEAD:].astype(jnp.bfloat16)
        outs = []
        for i in range(pieces):
            span = pl.ds(i * rows, rows)
            place = pl.ds(pl.multiple_of(ids[i] * TILE, TILE), rows)
            outs.append(pltpu.make_async_copy(qo_s.at[:, span], qb.at[:, place], sem_out.at[2 * i]))
            outs.append(pltpu.make_async_copy(kvo_s.at[span], kvb.at[place], sem_out.at[2 * i + 1]))
        for copy in outs:
            copy.start()
        for copy in outs:
            copy.wait()

    if first:
        return
    if sending:
        term_copies = weight_copies(w_out, wo_s, sem_wo)
        for copy in term_copies:
            copy.start()
    factor = math.log2(math.e) / math.sqrt(HEAD)

    def fetches(i, slot):
        tile = ids[HEADER + i]
        at = pl.multiple_of(tile * TILE, TILE)
        before = pl.multiple_of(jnp.maximum(tile - 1, 0) * TILE, TILE)
        return [
            pltpu.make_async_copy(qb.at[:, pl.ds(at, TILE)], qt_s.at[slot], sem_tile.at[slot, 0]),
            pltpu.make_async_copy(kvb.at[pl.ds(before, 2 * TILE)], kvt_s.at[slot], sem_tile.at[slot, 1]),
            pltpu.make_async_copy(doc_bias.at[pl.ds(at, TILE)], db_s.at[slot], sem_tile.at[slot, 2]),
            pltpu.make_async_copy(own_bias.at[pl.ds(at, TILE)], ob_s.at[slot], sem_tile.at[slot, 3]),
        ]

    def att_copy(i):
        at = pl.multiple_of(ids[HEADER + i] * TILE, TILE)
        return pltpu.make_async_copy(at_s, att.at[pl.ds(at, TILE)], sem_att)

    @pl.when(count > 0)
    def _():
        for copy in fetches(0, 0):
            copy.start()
        key_copy.wait()
        val_copy.wait()

    contract_last = (((1,), (1,)), ((), ()))

    def one_tile(i, carry):
        slot = lax.rem(i, 2)

        @pl.when(i + 1 < count)
        def _():
            for copy in fetches(i + 1, 1 - slot):
                copy.start()

        for copy in fetches(i, slot):
            copy.wait()
        tile = ids[HEADER + i]
        needed = lists[tile * stride]
        for h in range(heads):
            wide_s[h * TILE:(h + 1) * TILE, :HEAD] = qt_s[slot, h]
            wide_s[h * TILE:(h + 1) * TILE, HEAD:] = db_s[slot]
        own = lax.dot_general(
            wide_s[:, :HEAD], kvt_s[slot, :, :HEAD], contract_last, preferred_element_type=jnp.float32
        )
        own = (own.reshape(heads, TILE, HEAD) + ob_s[slot][None]).reshape(heads * TILE, HEAD)
        own_s[...] = own

        def attend(groups):
            listed = [lists[tile * stride + 1 + j] for j in range(groups * GROUP)]
            top = own_s[...]
            for g in range(groups):
                keys = jnp.concatenate([key_s[block] for block in listed[g * GROUP:(g + 1) * GROUP]], axis=1)
                scores = jnp.dot(wide_s[...], keys, preferred_element_type=jnp.float32)
                sc_s[g] = scores
                for c in range(0, GROUP * KEY_BLOCK, HEAD):
                    top = jnp.maximum(top, scores[:, c:c + HEAD])
            top = jnp.max(top, axis=1, keepdims=True) * factor
            weights = jnp.exp2(own_s[...] * factor - top)
            sums = weights
            made = [jnp.dot(weights.astype(jnp.bfloat16), kvt_s[slot, :, HEAD:], preferred_element_type=jnp.float32)]
            made += [None] * (GROUP - 1)
            for j, block in enumerate(listed):
                at = pl.multiple_of(jnp.minimum(block, blocks - 1) * KEY_BLOCK, KEY_BLOCK)
                c = j % GROUP * KEY_BLOCK
                weights = jnp.exp2(sc_s[j // GROUP, :, c:c + KEY_BLOCK] * factor - top)
                sums = sums + (weights[:, :HEAD] + weights[:, HEAD:])
                more = jnp.dot(
                    weights.astype(jnp.bfloat16), val_s[pl.ds(at, KEY_BLOCK), :], preferred_element_type=jnp.float32
                )
                made[j % GROUP] = more if made[j % GROUP] is None else made[j % GROUP] + more
            made = (made[0] + made[1]) + (made[2] + made[3])
            o_s[...] = (made / jnp.sum(sums, axis=1, keepdims=True)).astype(jnp.bfloat16)

        for groups in range(1, blocks // GROUP + 1):

            @pl.when(needed == groups)
            def _(groups=groups):
                attend(groups)

        @pl.when(i > 0)
        def _():
            att_copy(i - 1).wait()

        for h in range(heads):
            at_s[:, h * HEAD:(h + 1) * HEAD] = o_s[h * TILE:(h + 1) * TILE]
        att_copy(i).start()
        return carry

    lax.fori_loop(0, count, one_tile, 0)

    @pl.when(count > 0)
    def _():
        att_copy(count - 1).wait()

    if sending:
        places = [ids[PIECES_MOST + 1], ids[PIECES_MOST + 2]]
        write_terms(places, att, term_copies, terms, rows_s, wo_s, made_s, sem_rows, sem_made)


def run_step(ids, lists, xs, fixed, state, dims, w_out=None):
    tokens, heads, prefix, depth = dims
    pieces = len(xs)
    rows = xs[0].shape[0] if pieces else TILE
    total = max(pieces * rows, 16)
    width = heads * HEAD
    any_spec = pl.BlockSpec(memory_space=pl.ANY)
    vmem_spec = pl.BlockSpec(memory_space=pltpu.VMEM)
    operands = list(xs) + list(fixed)
    specs = [any_spec] * pieces + [vmem_spec] + [any_spec] * (len(fixed) - 1)
    aliases = {}
    if state is not None:
        aliases = {2 + len(operands) + i: i for i in range(3)}
        operands += list(state)
        specs += [any_spec] * 3
    sending = w_out is not None
    if sending:
        operands.append(w_out)
        specs.append(any_spec)
    out_shape = [
        jax.ShapeDtypeStruct((heads, tokens, HEAD), jnp.bfloat16),
        jax.ShapeDtypeStruct((tokens, 2 * HEAD), jnp.bfloat16),
        jax.ShapeDtypeStruct((tokens, width), jnp.bfloat16),
    ]
    if sending:
        out_shape += [jax.ShapeDtypeStruct((TILE, w_out.shape[1]), jnp.bfloat16)] * 2
    small = 16
    w_rows = depth if pieces else small
    scratch = [
        pltpu.VMEM((total, depth), jnp.bfloat16),
        pltpu.VMEM((total, depth), jnp.bfloat16),
        pltpu.VMEM((w_rows, width + 2 * HEAD), jnp.bfloat16),
        pltpu.VMEM((total, HEAD), jnp.float32),
        pltpu.VMEM((total, HEAD), jnp.float32),
        pltpu.VMEM((heads, total, HEAD), jnp.bfloat16),
        pltpu.VMEM((total, 2 * HEAD), jnp.bfloat16),
        pltpu.VMEM((prefix // KEY_BLOCK + 1, 2 * HEAD, KEY_BLOCK), jnp.bfloat16),
        pltpu.VMEM((prefix, HEAD), jnp.bfloat16),
        pltpu.VMEM((2, heads, TILE, HEAD), jnp.bfloat16),
        pltpu.VMEM((2, 2 * TILE, 2 * HEAD), jnp.bfloat16),
        pltpu.VMEM((2, TILE, HEAD), jnp.bfloat16),
        pltpu.VMEM((2, TILE, HEAD), jnp.float32),
        pltpu.VMEM((prefix // KEY_BLOCK // GROUP, heads * TILE, GROUP * KEY_BLOCK), jnp.float32),
        pltpu.VMEM((TILE, width), jnp.bfloat16),
        pltpu.VMEM((heads * TILE, 2 * HEAD), jnp.bfloat16),
        pltpu.VMEM((heads * TILE, HEAD), jnp.float32),
        pltpu.VMEM((heads * TILE, HEAD), jnp.bfloat16),
        pltpu.SemaphoreType.DMA((max(pieces, 1),)),
        pltpu.SemaphoreType.DMA((2 * max(pieces, 1),)),
        pltpu.SemaphoreType.DMA((2 * DEPTH_CHUNKS,)),
        pltpu.SemaphoreType.DMA((2,)),
        pltpu.SemaphoreType.DMA((2 * max(pieces, 1),)),
        pltpu.SemaphoreType.DMA((2, 4)),
        pltpu.SemaphoreType.DMA,
    ]
    if sending:
        scratch += term_scratch(2, width, w_out.shape[1])
    return pl.pallas_call(
        functools.partial(step_kernel, pieces, rows, heads, sending),
        grid_spec=pltpu.PrefetchScalarGridSpec(
            num_scalar_prefetch=2,
            grid=(),
            in_specs=specs,
            out_specs=[any_spec] * len(out_shape),
            scratch_shapes=scratch,
        ),
        out_shape=out_shape,
        input_output_aliases=aliases,
        compiler_params=pltpu.CompilerParams(vmem_limit_bytes=VMEM_LIMIT),
        cost_estimate=pl.CostEstimate(flops=1 << 20, bytes_accessed=1 << 16, transcendentals=0),
    )(ids, lists, *operands)


def weight_copies(w_out, w_s, sem_w):
    columns = w_out.shape[1] // COLUMN_CHUNKS
    spans = [pl.ds(c * columns, columns) for c in range(COLUMN_CHUNKS)]
    return [pltpu.make_async_copy(w_out.at[:, span], w_s.at[:, span], sem_w.at[c]) for c, span in enumerate(spans)]


def write_terms(places, att, w_copies, outs, rows_s, w_s, made_s, sem_rows, sem_out):
    columns = w_s.shape[1] // COLUMN_CHUNKS
    row_copies = [
        pltpu.make_async_copy(
            att.at[pl.ds(pl.multiple_of(place * TILE, TILE), TILE)], rows_s.at[pl.ds(i * TILE, TILE)], sem_rows.at[i]
        )
        for i, place in enumerate(places)
    ]
    for copy in row_copies:
        copy.start()
    for copy in row_copies:
        copy.wait()
    out_copies = []
    for c in range(COLUMN_CHUNKS):
        span = pl.ds(c * columns, columns)
        w_copies[c].wait()
        made = jnp.dot(rows_s[...], w_s[:, span], preferred_element_type=jnp.float32)
        made_s[:, span] = made.astype(jnp.bfloat16)
        for i in range(len(places)):
            copy = pltpu.make_async_copy(
                made_s.at[pl.ds(i * TILE, TILE), span], outs[i].at[:, span], sem_out.at[i, c]
            )
            copy.start()
            out_copies.append(copy)
    for copy in out_copies:
        copy.wait()


def term_scratch(count, width, columns):
    return [
        pltpu.VMEM((count * TILE, width), jnp.bfloat16),
        pltpu.VMEM((width, columns), jnp.bfloat16),
        pltpu.VMEM((count * TILE, columns), jnp.bfloat16),
        pltpu.SemaphoreType.DMA((count,)),
        pltpu.SemaphoreType.DMA((COLUMN_CHUNKS,)),
        pltpu.SemaphoreType.DMA((count, COLUMN_CHUNKS)),
    ]


def product_kernel(count, ids, att, w_out, *refs):
    rows_s, w_s, made_s, sem_rows, sem_w, sem_out = refs[count:]
    copies = weight_copies(w_out, w_s, sem_w)
    for copy in copies:
        copy.start()
    places = [ids[i] for i in range(count)]
    write_terms(places, att, copies, refs[:count], rows_s, w_s, made_s, sem_rows, sem_out)


def product(ids, count, att, w_out):
    width, columns = w_out.shape
    any_spec = pl.BlockSpec(memory_space=pl.ANY)
    return pl.pallas_call(
        functools.partial(product_kernel, count),
        grid_spec=pltpu.PrefetchScalarGridSpec(
            num_scalar_prefetch=1,
            grid=(),
            in_specs=[any_spec] * 2,
            out_specs=[any_spec] * count,
            scratch_shapes=term_scratch(count, width, columns),
        ),
        out_shape=[jax.ShapeDtypeStruct((TILE, columns), jnp.bfloat16)] * count,
        compiler_params=pltpu.CompilerParams(vmem_limit_bytes=VMEM_LIMIT),
        cost_estimate=pl.CostEstimate(flops=1 << 20, bytes_accessed=1 << 16, transcendentals=0),
    )(ids, att, w_out)


def tables(seg_ids, seg_doc, doc_lens, prefix, cache):
    tokens = seg_ids.shape[0]
    tiles = tokens // TILE
    blocks = prefix // KEY_BLOCK
    docs = doc_lens.shape[0]
    order = jnp.arange(tokens, dtype=jnp.int32)
    start = jnp.sum((seg_ids[None, :] < seg_ids[:, None]).astype(jnp.int32), axis=1, dtype=jnp.int32)
    positions = prefix + order - start
    segments = jnp.arange(seg_doc.shape[0], dtype=jnp.int32)
    tok_doc = jnp.sum(
        jnp.where(seg_ids[:, None] == segments[None, :], seg_doc[None, :], 0), axis=1, dtype=jnp.int32
    )
    doc_list = jnp.arange(docs, dtype=jnp.int32)
    doc_ends = jnp.sum(jnp.where(doc_list[None, :] <= doc_list[:, None], doc_lens[None, :], 0), axis=1)
    doc_starts = doc_ends - doc_lens
    lanes = jnp.arange(HEAD, dtype=jnp.int32)
    half = HEAD // 2
    inverse = ROPE_THETA ** (-(jnp.arange(half, dtype=jnp.float32) * 2.0 / HEAD))
    inverse = jnp.concatenate([inverse, inverse])
    angles = positions.astype(jnp.float32)[:, None] * inverse[None, :]
    cosine = jnp.cos(angles)
    sine = jnp.sin(angles) * jnp.where(lanes < half, -1.0, 1.0)[None, :]
    doc_bias = jnp.where(lanes[None, :] == tok_doc[:, None], 0.0, MASKED).astype(jnp.bfloat16)
    spot = jnp.arange(prefix + KEY_BLOCK, dtype=jnp.int32).reshape(blocks + 1, 1, KEY_BLOCK)
    low = jnp.pad(doc_starts, (0, HEAD - docs), constant_values=prefix).reshape(1, HEAD, 1)
    high = jnp.pad(doc_ends, (0, HEAD - docs), constant_values=prefix + KEY_BLOCK).reshape(1, HEAD, 1)
    one_hot = ((spot >= low) & (spot < high)).astype(jnp.bfloat16)
    by_block = cache[:, :HEAD].reshape(blocks, KEY_BLOCK, HEAD).transpose(0, 2, 1)
    key_wide = jnp.concatenate([jnp.pad(by_block, ((0, 1), (0, 0), (0, 0))), one_hot], axis=1)
    first_key = jnp.maximum(jnp.arange(tiles, dtype=jnp.int32) - 1, 0) * TILE
    spots = first_key[:, None] + lanes[None, :]
    by_tile = seg_ids.reshape(tiles, TILE)
    earlier = jnp.concatenate([by_tile[:1], by_tile[:-1]], axis=0)
    later = jnp.concatenate([by_tile[1:2], by_tile[1:]], axis=0)
    window_seg = jnp.concatenate([earlier, later], axis=1)
    ok = (window_seg[:, None, :] == by_tile[:, :, None]) & (
        spots[:, None, :] <= order.reshape(tiles, TILE)[:, :, None]
    )
    own_bias = jnp.where(ok, 0.0, MASKED).astype(jnp.float32).reshape(tokens, HEAD)
    present = jnp.any(tok_doc.reshape(tiles, TILE)[:, :, None] == doc_list[None, None, :], axis=1)
    edge = jnp.arange(blocks, dtype=jnp.int32) * KEY_BLOCK
    overlap = (doc_starts[:, None] < edge[None, :] + KEY_BLOCK) & (doc_ends[:, None] > edge[None, :])
    flags = jnp.any(present[:, :, None] & overlap[None, :, :], axis=1).astype(jnp.int32)
    block_ids = jnp.arange(blocks, dtype=jnp.int32)
    rank = jnp.sum(jnp.where(block_ids[None, :, None] > block_ids[None, None, :], flags[:, None, :], 0), axis=2)
    listed = jnp.sum(
        jnp.where((rank[:, :, None] == block_ids[None, None, :]) & (flags[:, :, None] > 0), block_ids[None, :, None], 0),
        axis=1,
    )
    count = jnp.sum(flags, axis=1, keepdims=True)
    listed = jnp.where(block_ids[None, :] < count, listed, blocks)
    groups = (count + GROUP - 1) // GROUP
    lists = jnp.pad(jnp.concatenate([groups, listed], axis=1), ((0, 0), (0, GROUP - 1)))
    lists = lists.astype(jnp.int32).reshape(-1)
    return cosine, sine, key_wide, doc_bias, own_bias, lists


def local(
    hidden_in, norm_gain, w_query, keyvalue_weight, w_out, prefix_keyvalue_cache, seg_ids, seg_doc, doc_lens
):
    size = lax.axis_size("tensor")
    tokens = seg_ids.shape[0]
    prefix = prefix_keyvalue_cache.shape[0]
    chunk_rows, depth = hidden_in.shape
    heads = w_query.shape[1] // HEAD
    order = ring_order(size)
    half = size // 2
    rank = lax.axis_index("tensor")

    forward_pairs = [(order[i], order[(i + 1) % size]) for i in range(size)]
    backward_pairs = [(b, a) for a, b in forward_pairs]

    def forward(x):
        return lax.ppermute(x, "tensor", forward_pairs)

    def backward(x):
        return lax.ppermute(x, "tensor", backward_pairs)

    if keyvalue_weight.shape[1] == HEAD:
        swap = [(i, i ^ 1) for i in range(size)]
        even = rank % 2 == 0
        other_weight, other_cache = lax.ppermute((keyvalue_weight, prefix_keyvalue_cache), "tensor", swap)
        keyvalue_weight = jnp.concatenate(
            [jnp.where(even, keyvalue_weight, other_weight), jnp.where(even, other_weight, keyvalue_weight)], axis=1
        )
        prefix_keyvalue_cache = jnp.concatenate(
            [
                jnp.where(even, prefix_keyvalue_cache, other_cache),
                jnp.where(even, other_cache, prefix_keyvalue_cache),
            ],
            axis=1,
        )

    place = {r: i for i, r in enumerate(order)}
    flips = np.zeros((size,), np.int32)
    for r in range(size):
        flips[r] = int(order[(place[r] - 1) % size] == r - 1)
    sends = np.zeros((size, half + 1, 6), np.int32)
    for r in range(size):
        for d in range(half + 1):
            ahead, back = order[(place[r] + d) % size], order[(place[r] - d) % size]
            late = [2 * ahead + flips[ahead], 2 * back + 1 - flips[back]]
            sends[r, d] = late + [2 * ahead + 1 - flips[ahead], 2 * back + flips[back], 2 * r, 2 * r + 1]
    tiles = tile_plan(order, sends)
    most = max(len(call) for calls in tiles for call in calls)
    plan = np.zeros((size, size, HEADER + most), np.int32)
    for r in range(size):
        for call in range(size):
            d = min(call, half - 1) if call <= half else half
            back, ahead = 2 * order[(place[r] - d) % size], 2 * order[(place[r] + d) % size]
            if call == half - 1 or call == half + 1:
                parts = [back, ahead + 1, 0, 0]
            elif call == half:
                parts = [back + 1, ahead, 0, 0]
            else:
                parts = [back, ahead, 0, 0]
            terms = sends[r, half, :2] if call == half + 1 else sends[r, half - 1, 2:4]
            row = parts + [len(tiles[r][call])] + [int(i) for i in terms] + tiles[r][call]
            plan[r, call, :len(row)] = row
    my_plan = jnp.asarray(plan)[rank]
    my_sends = jnp.asarray(sends)[rank]
    late_ids = {d: my_sends[d, :2] for d in range(2, half)}
    late_ids[1] = jnp.concatenate([my_sends[1, :2], my_sends[1, 4:]])
    early_ids = {d: my_sends[d, 2:4] for d in range(1, half - 1)}
    flipped = jnp.asarray(flips)[rank] > 0

    cosine, sine, key_wide, doc_bias, own_bias, lists = tables(
        seg_ids, seg_doc, doc_lens, prefix, prefix_keyvalue_cache
    )
    gain = norm_gain.astype(jnp.float32).reshape(1, depth)
    fixed = (gain, w_query, keyvalue_weight, cosine, sine, key_wide, prefix_keyvalue_cache, doc_bias, own_bias)
    dims = (tokens, heads, prefix, depth)

    def pass_on(pair):
        return forward(pair[0]), backward(pair[1])

    def add(pair, arrived):
        return tuple((a.astype(jnp.float32) + b.astype(jnp.float32)).astype(jnp.bfloat16) for a, b in zip(pair, arrived))

    def step(call, parts, state):
        return tuple(run_step(my_plan[call], lists, parts, fixed, state, dims))

    def step_and_send(call, parts, state):
        made = tuple(run_step(my_plan[call], lists, parts, fixed, state, dims, w_out))
        return made[:3], made[3:]

    def halves_of(pair):
        return (pair[0][:TILE], pair[1][TILE:]), (pair[0][TILE:], pair[1][:TILE])

    held = pass_on((hidden_in, hidden_in))
    bare = fixed[:5] + (gain,) * 4
    state = tuple(run_step(my_plan[0], my_plan[0], [hidden_in], bare, None, dims))
    for distance in range(1, half - 2):
        held, state = lax.optimization_barrier((held, state))
        following = pass_on(held)
        state = step(distance, held, state)
        held = following
    state, late_ids, early_ids, flipped = lax.optimization_barrier((state, late_ids, early_ids, flipped))
    held, state = lax.optimization_barrier((held, state))
    first, rest = halves_of(held)
    first = pass_on(first)
    state = step(half - 2, held, state)
    rest, state = lax.optimization_barrier((rest, state))
    second = pass_on(rest)
    first, state = lax.optimization_barrier((first, state))
    last = pass_on(first)
    state = step(half - 1, first, state)
    second, state = lax.optimization_barrier((second, state))
    state, made = step_and_send(half, second, state)
    made, last, state = lax.optimization_barrier((made, last, state))
    early = pass_on(made)
    state, made = step_and_send(half + 1, last, state)
    far = pass_on(made)
    for distance in range(half - 1, 0, -1):
        near = distance - 1
        if near > 0:
            made, state = lax.optimization_barrier((made, state))
            ahead = tuple(product(early_ids[near], 2, state[2], w_out))
            early, ahead = lax.optimization_barrier((early, ahead))
            made = add(ahead, early)
            early = pass_on(made)
            made, state = lax.optimization_barrier((made, state))
            state = step(size - near, [], state)
        else:
            early, made, state = lax.optimization_barrier((early, made, state))
        late = product(late_ids[distance], 2 if near > 0 else 4, state[2], w_out)
        own, late = late[2:], tuple(late[:2])
        far, late = lax.optimization_barrier((far, late))
        made = add(late, far)
        far = pass_on(made)
    wide = [part.astype(jnp.float32) for part in early]
    own = [part.astype(jnp.float32) for part in own]
    base = (
        hidden_in[:TILE].astype(jnp.float32) + own[0] + jnp.where(flipped, wide[0], wide[1]),
        hidden_in[TILE:].astype(jnp.float32) + own[1] + jnp.where(flipped, wide[1], wide[0]),
    )
    base, far = lax.optimization_barrier((base, far))
    far = [part.astype(jnp.float32) for part in far]
    lower = base[0] + jnp.where(flipped, far[1], far[0])
    upper = base[1] + jnp.where(flipped, far[0], far[1])
    return jnp.concatenate([lower, upper], axis=0).astype(jnp.bfloat16)


def solution(mesh):
    return jax.shard_map(
        local,
        mesh=mesh,
        in_specs=(
            P(("dp", "tensor"), None),
            P(),
            P(None, "tensor"),
            P(None, "tensor"),
            P("tensor", None),
            P(None, "tensor"),
            P("dp"),
            P("dp"),
            P(),
        ),
        out_specs=P(("dp", "tensor"), None),
        check_vma=False,
    )
```
